128 devices in a mesh: ctx: 16 (over y_lo, z, core), mp: 8 (over y_hi, x).
Axes of the slice: x: 4, y: 4 (y_hi: 2, y_lo: 2; y = y_hi * 2 + y_lo), z: 4, core: 2. Of those that a mesh axis runs over, the one named last changes fastest.
Arguments:
- residual_in: bfloat16 [4, 32, 128, 1024], P(None, 'ctx', 'mp'), may hold values from -54 to 54
- attn_norm: float32 [1024], replicated, may hold values from 0.1 to 1.9
- query_key_value_weight: bfloat16 [1024, 8, 256], P(None, 'mp'), may hold values from -0.1875 to 0.1875
- query_gain: float32 [64], replicated, may hold values from 0.1 to 1.9
- key_gain: float32 [64], replicated, may hold values from 0.1 to 1.9
- out_weight: bfloat16 [1024, 1024], P('mp'), may hold values from -2 to 2
- ffn_norm: float32 [1024], replicated, may hold values from 0.1 to 1.9
- gate_up: bfloat16 [1024, 2, 4608], P(None, None, 'mp'), may hold values from -0.1875 to 0.1875
- down_weight: bfloat16 [4608, 1024], P('mp'), may hold values from -0.09375 to 0.09375
- cotangent: bfloat16 [4, 32, 128, 1024], P(None, 'ctx', 'mp'), may hold values from -6 to 6
- positions: int32 [4, 4096], replicated, may hold values from 256 to 8446, as said below
- block_map: int32 [32], replicated, may hold values from 0 to 31, as said below
Outputs:
- output: bfloat16 [4, 32, 128, 1024], P(None, 'ctx', 'mp')
- input_grad: bfloat16 [4, 32, 128, 1024], P(None, 'ctx', 'mp')
- attn_norm_grad: float32 [1024], replicated
- qkv_grad: float32 [1024, 8, 256], P(None, 'mp')
- query_gain_grad: float32 [64], replicated
- key_gain_grad: float32 [64], replicated
- out_grad: float32 [1024, 1024], P('mp')
- ffn_norm_grad: float32 [1024], replicated
- gate_up_grad: float32 [1024, 2, 4608], P(None, None, 'mp')
- down_grad: float32 [4608, 1024], P('mp')
The draws below stay inside these ranges and needn't reach their ends.
Inputs may be any that keep to these rules, and one draw needn't show every extreme that they name: `positions`: positions rise strictly along each sequence in steps of 1 or 2; every sequence ends at 8446. `block_map`: each block of a sequence stands in exactly one slot; slots 2c and 2c + 1 hold blocks b and 31 - b for some b, in either order.
All inputs are finite; a program needn't handle non-finite values.
Results may differ from the reference program's by a relative error of at most 0.028.
Values may be sent and summed in bfloat16 or wider, within the bound.
A program may use at most 128 MiB of HBM per device.

```python
import math
import jax
import jax.numpy as jnp
from jax import lax

MODEL_WIDTH = 1024
HQ = 16
KEY_VALUE_HEADS = 8
HEAD_SIZE = 64
FF = 4608
SEQS = 4
BLK = 128
QUERY_PER_KV = 2
SLOTS = 32
LENGTH = 4096


def draw_residual_in(key, part):
    row_key, col_key, value_key = jax.random.split(key, 3)
    row_scales = jnp.exp(jax.random.uniform(row_key, (SEQS, SLOTS, BLK, 1), jnp.float32, math.log(0.3), math.log(3.0)))
    col_scales = jnp.exp(jax.random.uniform(col_key, (MODEL_WIDTH,), jnp.float32, math.log(0.3), math.log(3.0)))
    base_values = jnp.clip(jax.random.normal(value_key, (SEQS, SLOTS, BLK, MODEL_WIDTH), jnp.float32), -5.5, 5.5)
    return (base_values * row_scales * col_scales).astype(jnp.bfloat16)


def draw_positions(key, part):
    step_sizes = jax.random.randint(key, (SEQS, LENGTH), 1, 3, dtype=jnp.int32)
    remaining = jnp.sum(step_sizes, axis=1, keepdims=True) - jnp.cumsum(step_sizes, axis=1)
    return (2 * LENGTH + 254 - remaining).astype(jnp.int32)


def draw_block_map(key, part):
    pair_key, flip_key = jax.random.split(jax.random.fold_in(key, 11), 2)
    pair_count = SLOTS // 2
    early = jax.random.permutation(pair_key, pair_count).astype(jnp.int32)
    late = (SLOTS - 1 - early).astype(jnp.int32)
    flips = jax.random.randint(flip_key, (pair_count,), 0, 2, dtype=jnp.int32)
    first = flips * late + (1 - flips) * early
    second = flips * early + (1 - flips) * late
    return jnp.stack([first, second], axis=1).reshape(SLOTS).astype(jnp.int32)


def steps_of(stream_key, extent, cuts, least, largest):
    loudness, own = 1.0, jax.random.fold_in(stream_key, 6)
    for axis_at, blocks in cuts:
        heights = jnp.exp(jax.random.uniform(jax.random.fold_in(own, axis_at), (blocks,), jnp.float32, least / len(cuts), largest / len(cuts)))
        loudness = loudness * jnp.repeat(heights, extent[axis_at] // blocks).reshape([-1 if axis == axis_at else 1 for axis in range(len(extent))])
    return loudness


def noise(key, shape, scale, limit, cuts=(), kind=jnp.bfloat16):
    entries = scale * jax.random.normal(key, shape, jnp.float32)
    if cuts:
        entries = entries * steps_of(key, shape, cuts, -0.22, 0.18)
    return jnp.clip(entries, -limit, limit).astype(kind)


def setup_inputs(seed: int = 0) -> dict:
    arg_keys = jax.random.split(jax.random.key(seed), 13)
    return {
        "residual_in": draw_residual_in(jax.random.fold_in(arg_keys[12], 71), 0),
        "attn_norm": jnp.clip(1.0 + 0.18 * jax.random.normal(arg_keys[1], (MODEL_WIDTH,), jnp.float32), 0.1, 1.9),
        "query_key_value_weight": noise(arg_keys[2], (MODEL_WIDTH, KEY_VALUE_HEADS, (QUERY_PER_KV + 2) * HEAD_SIZE), MODEL_WIDTH ** -0.5, 0.1875, ((1, 8),)),
        "query_gain": jnp.clip(1.0 + 0.18 * jax.random.normal(arg_keys[3], (HEAD_SIZE,), jnp.float32), 0.1, 1.9),
        "key_gain": jnp.clip(1.0 + 0.18 * jax.random.normal(arg_keys[4], (HEAD_SIZE,), jnp.float32), 0.1, 1.9),
        "out_weight": noise(arg_keys[5], (HQ * HEAD_SIZE, MODEL_WIDTH), 8 ** -0.5, 2.0, ((0, 8),)),
        "ffn_norm": jnp.clip(1.0 + 0.18 * jax.random.normal(arg_keys[6], (MODEL_WIDTH,), jnp.float32), 0.1, 1.9),
        "gate_up": noise(arg_keys[7], (MODEL_WIDTH, 2, FF), MODEL_WIDTH ** -0.5, 0.1875, ((2, 8),)),
        "down_weight": noise(arg_keys[8], (FF, MODEL_WIDTH), FF ** -0.5, 0.09375, ((0, 8),)),
        "cotangent": noise(arg_keys[9], (SEQS, SLOTS, BLK, MODEL_WIDTH), 1.0, 6.0, ((1, 16), (2, 8))),
        "positions": draw_positions(jax.random.fold_in(arg_keys[12], 71), 0),
        "block_map": draw_block_map(jax.random.fold_in(arg_keys[12], 71), 0),
    }


EPSILON = 1e-05
ROPE_BASE = 1000000.0
PRECISE = lax.Precision.HIGHEST

@jax.custom_vjp
def low(v):
    return lax.optimization_barrier(v.astype(jnp.bfloat16)).astype(jnp.float32)

@jax.custom_vjp
def low_back(v):
    return v

def low_keep(v):
    return (low(v), None)

def low_pass(kept, grad):
    return (grad,)

def back_keep(v):
    return (v, None)

def back_low(kept, grad):
    return (low(grad),)
low.defvjp(low_keep, low_pass)
low_back.defvjp(back_keep, back_low)

def rms_scale(values):
    return lax.rsqrt(lax.optimization_barrier(jnp.mean(values * values, axis=-1, keepdims=True)) + EPSILON)

def rotate(values, cosine_table, sine_table):
    half_dim = values.shape[-1] // 2
    first_half = values[..., :half_dim]
    second_half = values[..., half_dim:]
    return jnp.concatenate([first_half * cosine_table - second_half * sine_table, second_half * cosine_table + first_half * sine_table], axis=-1)

def attention(query_matrix, key_rows, values, token_index):
    combined_length = query_matrix.shape[0]
    rows_per_block = math.gcd(combined_length, 512)
    blocks_of_query = query_matrix.reshape(combined_length // rows_per_block, rows_per_block, KEY_VALUE_HEADS, QUERY_PER_KV, HEAD_SIZE)
    index_blocks = token_index.reshape(combined_length // rows_per_block, rows_per_block)
    scale_factor = 1.0 / math.sqrt(HEAD_SIZE)

    @jax.checkpoint
    def one_block(block_item):
        query_block, query_index = block_item
        scores = jnp.einsum('qhgd,khd->hgqk', query_block, key_rows, precision=PRECISE) * scale_factor
        scores = low_back(scores)
        allowed = token_index[None, :] <= query_index[:, None]
        scores = jnp.where(allowed, scores, -1e+30)
        prob_block = jax.nn.softmax(scores, axis=-1)
        return jnp.einsum('hgqk,khd->qhgd', low(prob_block), values, precision=PRECISE)
    output_list = lax.map(one_block, (blocks_of_query, index_blocks))
    return output_list.reshape(combined_length, KEY_VALUE_HEADS, QUERY_PER_KV, HEAD_SIZE)

def block_forward(tokens, params, cosine_table, sine_table, token_index):
    attn_norm, query_key_value_weight, query_gain, key_gain, out_weight, ffn_norm, gate_up, down_weight = params
    combined_length = tokens.shape[0]
    normed1 = low(tokens * rms_scale(tokens) * attn_norm)
    query_key_value_rows = low_back(jnp.dot(normed1, query_key_value_weight.reshape(MODEL_WIDTH, -1), precision=PRECISE))
    query_key_value_rows = query_key_value_rows.reshape(combined_length, KEY_VALUE_HEADS, QUERY_PER_KV + 2, HEAD_SIZE)
    query_matrix = query_key_value_rows[:, :, :QUERY_PER_KV]
    key_rows = query_key_value_rows[:, :, QUERY_PER_KV]
    values = query_key_value_rows[:, :, QUERY_PER_KV + 1]
    query_matrix = low(rotate(query_matrix * rms_scale(query_matrix) * query_gain, cosine_table[:, None, None, :], sine_table[:, None, None, :]))
    key_rows = low(rotate(key_rows * rms_scale(key_rows) * key_gain, cosine_table[:, None, :], sine_table[:, None, :]))
    values = low(values)
    attended = attention(query_matrix, key_rows, values, token_index)
    attended = low(low_back(attended)).reshape(combined_length, HQ * HEAD_SIZE)
    mixed_rows = tokens + low_back(jnp.dot(attended, out_weight, precision=PRECISE))
    normed2 = low(mixed_rows * rms_scale(mixed_rows) * ffn_norm)
    gate_values = low_back(jnp.dot(normed2, gate_up.reshape(MODEL_WIDTH, 2 * FF), precision=PRECISE))
    active = low(jax.nn.silu(gate_values[:, :FF]) * gate_values[:, FF:])
    return mixed_rows + jnp.dot(active, down_weight, precision=PRECISE)

def reference(residual_in, attn_norm, query_key_value_weight, query_gain, key_gain, out_weight, ffn_norm, gate_up, down_weight, cotangent, positions, block_map):
    token_index = (block_map[:, None] * BLK + jnp.arange(BLK, dtype=jnp.int32)[None, :]).reshape(-1).astype(jnp.int32)
    params = (attn_norm.astype(jnp.float32), query_key_value_weight.astype(jnp.float32), query_gain.astype(jnp.float32), key_gain.astype(jnp.float32), out_weight.astype(jnp.float32), ffn_norm.astype(jnp.float32), gate_up.astype(jnp.float32), down_weight.astype(jnp.float32))
    inverse_freq = 1.0 / ROPE_BASE ** (jnp.arange(0, HEAD_SIZE, 2, dtype=jnp.float32) / HEAD_SIZE)

    def one_sequence(totals, seq_item):
        seq_tokens, grad_output, seq_positions = seq_item
        seq_tokens = seq_tokens.reshape(SLOTS * BLK, MODEL_WIDTH).astype(jnp.float32)
        angles = jnp.take(seq_positions, token_index).astype(jnp.float32)[:, None] * inverse_freq[None, :]
        cosine_table = jnp.cos(angles)
        sine_table = jnp.sin(angles)

        def forward(token_values, weight_values):
            return block_forward(token_values, weight_values, cosine_table, sine_table, token_index)
        result, pullback = jax.vjp(forward, seq_tokens, params)
        token_grad, weight_grads = pullback(grad_output.reshape(SLOTS * BLK, MODEL_WIDTH).astype(jnp.float32))
        totals = jax.tree.map(lambda left_sum, right_sum: left_sum + right_sum, totals, weight_grads)
        return (totals, (result.astype(jnp.bfloat16), token_grad.astype(jnp.bfloat16)))
    start_totals = jax.tree.map(jnp.zeros_like, params)
    totals, (results, token_grads) = lax.scan(one_sequence, start_totals, (residual_in, cotangent, positions))
    return (results.reshape(residual_in.shape), token_grads.reshape(residual_in.shape), totals[0], totals[1], totals[2], totals[3], totals[4], totals[5], totals[6], totals[7])
```

```python
import functools
import math

import jax
import jax.numpy as jnp
from jax import lax
from jax.experimental import pallas as pl
from jax.experimental.pallas import tpu as pltpu
from jax.sharding import PartitionSpec as P

EPSILON = 1e-05
ROPE_BASE = 1000000.0
MESH = pl.DeviceIdType.MESH
F32 = jnp.float32
BF16 = jnp.bfloat16
RELS = ("L", "R", "X", "O", "OL", "OR", "OX")
VMEM_LIMIT = 56 << 20


def params(cid):
    return pltpu.CompilerParams(
        collective_id=cid, has_side_effects=True, vmem_limit_bytes=VMEM_LIMIT
    )


def rel_index(axis, rel):
    me = lax.axis_index(axis)
    core = 0
    if axis == "ctx":
        core = lax.rem(me, 2)
        me = me // 2
    pos = lax.rem(me, 4)
    row = me // 4
    step = {"L": 3, "R": 1, "X": 2, "M": 0}[rel[-1] if rel[-1] != "O" else "M"]
    if rel[0] == "O":
        row = 1 - row
    index = row * 4 + lax.rem(pos + step, 4)
    if axis == "ctx":
        index = index * 2 + core
    return index


def sibling():
    me = lax.axis_index("ctx")
    return me + 1 - 2 * lax.rem(me, 2)


def enter(axes, sib=False, extra=()):
    barrier = pltpu.get_barrier_semaphore()
    count = 0
    for axis in axes:
        for rel in ("L", "R", "O"):
            pl.semaphore_signal(
                barrier, inc=1, device_id={axis: rel_index(axis, rel)}, device_id_type=MESH
            )
            count += 1
    if sib:
        pl.semaphore_signal(barrier, inc=1, device_id={"ctx": sibling()}, device_id_type=MESH)
        count += 1
    pl.semaphore_wait(barrier, count)


def rcopy(src, dst, ssem, rsem, axis, index):
    return pltpu.make_async_remote_copy(
        src_ref=src,
        dst_ref=dst,
        send_sem=ssem,
        recv_sem=rsem,
        device_id={axis: index},
        device_id_type=MESH,
    )


class Gather:
    scratch = (pltpu.SemaphoreType.DMA((28,)), pltpu.SemaphoreType.DMA((7, 4)))

    def __init__(self, axis, dst, ssem, rsem):
        self.axis, self.dst, self.ssem, self.rsem = axis, dst, ssem, rsem
        self.index = {rel: rel_index(axis, rel) for rel in RELS + ("M",)}
        self.sent = []
        self.seen = set()

    def send(self, source, p, to, as_rel):
        view = self.dst(self.index[source], p)
        copy = rcopy(
            view,
            view,
            self.ssem.at[len(self.sent)],
            self.rsem.at[RELS.index(as_rel), p],
            self.axis,
            self.index[to],
        )
        copy.start()
        self.sent.append(copy)

    def arrive(self, rel, p):
        if (rel, p) in self.seen:
            return
        self.seen.add((rel, p))
        view = self.dst(self.index[rel], p)
        rcopy(
            view, view, self.ssem.at[0], self.rsem.at[RELS.index(rel), p], self.axis, self.index["L"]
        ).wait_recv()

    def start_piece(self, p):
        if p < 2:
            self.send("M", p, "R", "L")
            self.send("M", p, "O", "O")
            self.send("M", p, "L", "R")
        else:
            self.send("M", p, "L", "R")
            self.send("M", p, "O", "O")
            self.send("M", p, "R", "L")

    def start(self):
        for p in (0, 2, 1, 3):
            self.start_piece(p)

    def relay_row(self):
        for a, b in ((0, 2), (1, 3)):
            self.arrive("L", a)
            self.send("L", a, "R", "X")
            self.arrive("R", b)
            self.send("R", b, "L", "X")

    def relay_opposite(self):
        for p in (0, 2, 1, 3):
            self.arrive("O", p)
            if p < 2:
                self.send("O", p, "R", "OL")
                self.send("O", p, "L", "OR")
            else:
                self.send("O", p, "L", "OR")
                self.send("O", p, "R", "OL")

    def relay_last(self):
        for a, b in ((0, 2), (1, 3)):
            self.arrive("OL", a)
            self.send("OL", a, "R", "OX")
            self.arrive("OR", b)
            self.send("OR", b, "L", "OX")

    def finish_piece(self, p):
        for rel in RELS:
            self.arrive(rel, p)

    def finish(self):
        for p in range(4):
            self.finish_piece(p)

    def drain(self):
        for copy in self.sent:
            copy.wait_send()

    def run(self):
        self.start()
        self.relay_row()
        self.relay_opposite()
        self.relay_last()
        self.finish()
        self.drain()


class Scatter:
    @staticmethod
    def scratch(piece):
        return (
            pltpu.VMEM((2, 2, 2) + piece, BF16),
            pltpu.VMEM((2, 2, 2) + piece, BF16),
            pltpu.VMEM((2, 2, 4) + piece, BF16),
            pltpu.VMEM((2, 4) + piece, BF16),
            pltpu.SemaphoreType.DMA((28,)),
            pltpu.SemaphoreType.DMA((28,)),
        )

    def __init__(self, axis, part, relay, stage, arrived, across, ssem, rsem):
        self.axis, self.part = axis, part
        self.relay, self.stage, self.arrived, self.across = relay, stage, arrived, across
        self.ssem, self.rsem = ssem, rsem
        self.index = {rel: rel_index(axis, rel) for rel in RELS + ("M",)}
        self.sent = []

    def block(self, t, rel, p):
        name = rel if t == 0 else ("O" if rel == "M" else "O" + rel)
        return self.part(self.index[name], p)

    def send(self, src, dst, rslot, to):
        copy = rcopy(
            src, dst, self.ssem.at[len(self.sent)], self.rsem.at[rslot], self.axis, self.index[to]
        )
        copy.start()
        self.sent.append(copy)

    def arrive(self, dst, rslot):
        rcopy(dst, dst, self.ssem.at[0], self.rsem.at[rslot], self.axis, self.index["L"]).wait_recv()

    def start(self, t):
        for q in range(2):
            self.send(self.block(t, "X", q), self.relay.at[0, t, q], t * 2 + q, "R")
            self.send(self.block(t, "X", 2 + q), self.relay.at[1, t, q], 4 + t * 2 + q, "L")
        for q in range(2):
            self.send(
                self.block(t, "R", 2 + q), self.arrived.at[0, t, 2 + q], 8 + t * 4 + 2 + q, "R"
            )
            self.send(self.block(t, "L", q), self.arrived.at[1, t, q], 16 + t * 4 + q, "L")

    def middle(self, t):
        for q in range(2):
            for d, to, p in ((0, "R", q), (1, "L", 2 + q)):
                self.arrive(self.relay.at[d, t, q], d * 4 + t * 2 + q)
                total = self.block(t, to, p)[...].astype(F32) + self.relay[d, t, q].astype(F32)
                self.stage[d, t, q] = total.astype(BF16)
                self.send(
                    self.stage.at[d, t, q], self.arrived.at[d, t, p], 8 + d * 8 + t * 4 + p, to
                )

    def row_sum(self, t, p):
        for d in range(2):
            self.arrive(self.arrived.at[d, t, p], 8 + d * 8 + t * 4 + p)
        return (
            self.block(t, "M", p)[...].astype(F32)
            + self.arrived[0, t, p].astype(F32)
            + self.arrived[1, t, p].astype(F32)
        )

    def cross(self):
        for p in (2, 0, 3, 1):
            self.across[0, p] = self.row_sum(1, p).astype(BF16)
            self.send(self.across.at[0, p], self.across.at[1, p], 24 + p, "O")

    def result(self, p):
        total = self.row_sum(0, p)
        self.arrive(self.across.at[1, p], 24 + p)
        return total + self.across[1, p].astype(F32)

    def begin(self):
        self.start(1)
        self.start(0)
        self.middle(1)
        self.cross()
        self.middle(0)

    def drain(self):
        for copy in self.sent:
            copy.wait_send()


def take(refs, count):
    return refs[:count], refs[count:]


def lane_iota(shape):
    return lax.broadcasted_iota(jnp.int32, shape, len(shape) - 1)


def dot_nt(a, b):
    return lax.dot_general(a, b, (((1,), (1,)), ((), ())), preferred_element_type=F32)


def dot_tn(a, b):
    return lax.dot_general(a, b, (((0,), (0,)), ((), ())), preferred_element_type=F32)


def dot(a, b):
    return jnp.dot(a, b, preferred_element_type=F32)


def head_sums(values, low):
    zero = jnp.zeros_like(values)
    first = jnp.sum(jnp.where(low, values, zero), axis=-1, keepdims=True)
    second = jnp.sum(jnp.where(low, zero, values), axis=-1, keepdims=True)
    return first, second


def swap_halves(values, first_half):
    return jnp.where(first_half, pltpu.roll(values, 96, 1), pltpu.roll(values, 32, 1))


def rms_scale(values):
    return lax.rsqrt(jnp.mean(values * values, axis=-1, keepdims=True) + EPSILON)


def norm_back(gradient, normed, scale_rows, gain_vec):
    scaled = gradient * gain_vec
    return scale_rows * (scaled - normed * jnp.mean(scaled * normed, axis=-1, keepdims=True))


def rows_of(index):
    return pl.ds(pl.multiple_of(index * 16, 16), 16)


def qkv_kernel(
    x, cot, gain1, w, gains, cosine, sine, full, cot_full, raw, queries, kv_all, *sems
):
    mp = lax.axis_index("mp")
    ctx = lax.axis_index("ctx")
    enter(("mp", "ctx"), sib=True)
    (s1, r1, s2, r2, s3, r3), (s4, r4) = take(sems, 6)
    for s in range(4):
        t = x[s].astype(F32)
        full[s, :, rows_of(mp), :] = (t * rms_scale(t) * gain1[...]).astype(BF16)
    first = Gather("mp", lambda i, p: full.at[p, :, rows_of(i), :], s1, r1)
    first.run()
    for s in range(4):
        cot_full[s, :, rows_of(mp), :] = cot[s]
    kv_view = lambda i, p: kv_all.at[p, pl.ds(i * 2, 2)]
    keys = Gather("ctx", kv_view, s2, r2)
    second = Gather("mp", lambda i, p: cot_full.at[p, :, rows_of(i), :], s3, r3)
    lane = lane_iota((256, 128))
    low = lane < 64
    first_half = lax.rem(lane, 64) < 32
    for s in range(4):
        y = dot(full[s].reshape(256, 1024), w[...])
        raw[s] = y
        a, b = y[:, :128], y[:, 128:]
        cos, sin = cosine[s], sine[s]
        lo, hi = head_sums(a * a, low)
        scale = jnp.where(
            low, lax.rsqrt(lo * (1 / 64) + EPSILON), lax.rsqrt(hi * (1 / 64) + EPSILON)
        )
        g = a * scale * gains[0:1, :]
        turned = g * cos + swap_halves(g, first_half) * sin
        zero = jnp.zeros_like(turned)
        head0 = jnp.where(low, turned, zero).astype(BF16)
        head1 = jnp.where(low, pltpu.roll(turned, 64, 1), zero).astype(BF16)
        for t in range(2):
            queries[s, t, 0:128] = head0[t * 128 : t * 128 + 128]
            queries[s, t, 128:256] = head1[t * 128 : t * 128 + 128]
        lo, _ = head_sums(b * b, low)
        g = b * lax.rsqrt(lo * (1 / 64) + EPSILON) * gains[1:2, :]
        turned = g * cos + swap_halves(g, first_half) * sin
        packed = jnp.where(low, turned, b).astype(BF16)
        kv_all[s, pl.ds(ctx * 2, 2)] = packed.reshape(2, 128, 128)
        keys.start_piece(s)
    second.start()
    sib = sibling()
    forwards = []

    def forward(rel, slot):
        view = kv_all.at[:, pl.ds(keys.index[rel] * 2, 2)]
        copy = rcopy(view, view, s4.at[slot], r4.at[slot], "ctx", sib)
        copy.start()
        forwards.append(copy)

    forward("M", 0)
    keys.relay_row()
    second.relay_row()
    keys.relay_opposite()
    second.relay_opposite()
    keys.relay_last()
    second.relay_last()
    for slot, rel in enumerate(RELS):
        for p in range(4):
            keys.arrive(rel, p)
        forward(rel, slot + 1)
    second.finish()
    keys.drain()
    second.drain()
    for copy in forwards:
        copy.wait_send()
    delta = sib - ctx
    for slot, rel in enumerate(("M",) + RELS):
        view = kv_all.at[:, pl.ds((keys.index[rel] + delta) * 2, 2)]
        rcopy(view, view, s4.at[slot], r4.at[slot], "ctx", sib).wait_recv()


def attention_kernel(own, where, queries, kv_all, low_out, high_out, logs, acc):
    lane_k = lane_iota((256, 128)) < 64
    for j in range(2):
        mine = own[j]
        acc[...] = jnp.zeros_like(acc)

        def step(i, masked):
            slot0, slot1 = where[2 * i], where[2 * i + 1]
            if masked:
                row = lax.rem(lax.broadcasted_iota(jnp.int32, (256, 256), 0), 128)
                col = lax.broadcasted_iota(jnp.int32, (256, 256), 1)
                keep = col + 256 * i <= row + 128 * mine
            for s in range(4):
                kv = jnp.concatenate([kv_all[s, slot0], kv_all[s, slot1]], axis=0)
                weights = jnp.exp(dot_nt(queries[s, j], kv) * 0.125)
                if masked:
                    weights = jnp.where(keep, weights, 0.0)
                ones = jnp.where(lane_k, jnp.ones_like(kv), kv)
                acc[s] += dot(weights.astype(BF16), ones)

        last = mine // 2
        lax.fori_loop(0, last, lambda i, c: (step(i, False), c)[1], 0)
        step(last, True)
        low = lane_iota((128, 128)) < 64
        for s in range(4):
            a = acc[s]
            o = a * pltpu.roll(1.0 / a, 64, 1)
            both = jnp.where(low, pltpu.roll(o[0:128], 64, 1), o[128:256])
            low_out[s, j] = both.astype(BF16)
            high_out[s, j] = both
            logs[s, j] = jnp.log(a.T[0:8])


def attention_back_kernel(
    own, where, queries, kv_all, grad_out, out, logs, grad_q, grad_kv, acc, grad_pad, turned, delta
):
    acc[...] = jnp.zeros_like(acc)
    low = lane_iota((128, 128)) < 64
    for j in range(2):
        mine = own[j]
        turned[...] = jnp.zeros_like(turned)
        for s in range(4):
            g = grad_out[s, j]
            gf = g.astype(F32)
            zero = jnp.zeros_like(gf)
            grad_pad[s, 0:128] = jnp.where(low, zero, pltpu.roll(gf, 64, 1)).astype(BF16)
            grad_pad[s, 128:256] = jnp.where(low, zero, gf).astype(BF16)
            product = (gf * out[s, j]).T
            delta[s, :, 0:128] = jnp.broadcast_to(
                jnp.sum(product[0:64], axis=0, keepdims=True), (8, 128)
            )
            delta[s, :, 128:256] = jnp.broadcast_to(
                jnp.sum(product[64:128], axis=0, keepdims=True), (8, 128)
            )

        def step(i, masked):
            slot0, slot1 = where[2 * i], where[2 * i + 1]
            if masked:
                col = lax.rem(lax.broadcasted_iota(jnp.int32, (256, 256), 1), 128)
                row = lax.broadcasted_iota(jnp.int32, (256, 256), 0)
                keep = row + 256 * i <= col + 128 * mine
            for s in range(4):
                kv = jnp.concatenate([kv_all[s, slot0], kv_all[s, slot1]], axis=0)
                q, g = queries[s, j], grad_pad[s]
                probs = jnp.exp(dot_nt(kv, q) * 0.125 - logs[s, j, 0:1])
                if masked:
                    probs = jnp.where(keep, probs, 0.0)
                scores = (probs * (dot_nt(kv, g) - delta[s, 0:1])).astype(BF16)
                turned[s] += dot_tn(kv, scores)
                block = dot(
                    jnp.concatenate([scores, probs.astype(BF16)], axis=1),
                    jnp.concatenate([q, g], axis=0),
                )
                acc[s, slot0] += block[0:128]
                acc[s, slot1] += block[128:256]

        last = mine // 2
        lax.fori_loop(0, last, lambda i, c: (step(i, False), c)[1], 0)
        step(last, True)
        for s in range(4):
            t = turned[s].T * 0.125
            grad_q[s, j] = jnp.where(low, t[0:128], pltpu.roll(t[128:256], 64, 1))
    scale = jnp.where(low, 0.125, 1.0)

    def finish(n, c):
        for s in range(4):
            grad_kv[s, n] = (acc[s, n] * scale).astype(BF16)
        return c

    lax.fori_loop(0, 32, finish, 0)


def mix_kernel(x, attended, w, gain2, mixed, full, part, *scratch):
    mp = lax.axis_index("mp")
    enter(("mp",))
    sums, (s1, r1) = take(scratch, 6)
    for s in range(4):
        rows = dot(attended[s].reshape(256, 128), w[...])
        part[s] = rows.astype(BF16).reshape(2, 128, 1024)
    scatter = Scatter("mp", lambda i, p: part.at[p, :, rows_of(i), :], *sums)
    scatter.begin()
    gather = Gather("mp", lambda i, p: full.at[p, :, rows_of(i), :], s1, r1)
    for p in (2, 0, 3, 1):
        m = x[p].astype(F32) + scatter.result(p)
        mixed[p] = m
        full[p, :, rows_of(mp), :] = (m * rms_scale(m) * gain2[...]).astype(BF16)
        gather.start_piece(p)
    gather.relay_row()
    gather.relay_opposite()
    gather.relay_last()
    gather.finish()
    scatter.drain()
    gather.drain()


def branch_kernel(
    part_d, part_o, mixed, cot, gain2, w, out, d_mixed, full, d_att, gain_part, *scratch
):
    mp = lax.axis_index("mp")
    enter(("mp",))
    sums_d, rest = take(scratch, 6)
    sums_o, (s1, r1) = take(rest, 6)
    scatter = Scatter("mp", lambda i, p: part_d.at[p, :, rows_of(i), :], *sums_d)
    scatter.begin()
    other = Scatter("mp", lambda i, p: part_o.at[p, :, rows_of(i), :], *sums_o)
    gather = Gather("mp", lambda i, p: full.at[p, :, rows_of(i), :], s1, r1)
    gain_sum = jnp.zeros((1, 1024), F32)
    for p in (2, 0, 3, 1):
        g = scatter.result(p)
        m = mixed[p]
        scale = rms_scale(m)
        normed = m * scale
        gain_sum += jnp.sum((g * normed).reshape(32, 1024), axis=0, keepdims=True)
        dm = cot[p].astype(F32) + norm_back(g, normed, scale, gain2[...])
        d_mixed[p] = dm
        full[p, :, rows_of(mp), :] = dm.astype(BF16)
        gather.start_piece(p)
    gain_part[...] = gain_sum
    gather.relay_row()
    gather.relay_opposite()
    gather.relay_last()
    other.start(1)
    other.start(0)
    gather.finish()
    for s in range(4):
        d_att[s] = dot_nt(full[s].reshape(256, 1024), w[...]).astype(BF16).reshape(2, 128, 128)
    other.middle(1)
    other.cross()
    other.middle(0)
    for p in (2, 0, 3, 1):
        out[p] = (mixed[p] + other.result(p)).astype(BF16)
    scatter.drain()
    gather.drain()
    other.drain()


def last_kernel(
    grad_kv, grad_q, raw, cosine, sine, gains, w, x, gain1, d_mixed,
    d_qkv, in_grad, gain_part, head_part,
    pair, arrived, part, *scratch,
):
    ctx = lax.axis_index("ctx")
    enter(("mp", "ctx"), sib=True)
    sums_k, rest = take(scratch, 6)
    sums_n, (s1, r1) = take(rest, 6)
    core = lax.rem(ctx, 2)
    sib = sibling()
    copies = []
    for chip in range(8):
        src = grad_kv.at[:, pl.ds(chip * 4 + (1 - core) * 2, 2)]
        copy = rcopy(src, arrived.at[:, pl.ds(chip * 2, 2)], s1.at[chip], r1.at[chip], "ctx", sib)
        copy.start()
        copies.append(copy)
    for chip in range(8):
        copies[chip].wait_recv()
        for s in range(4):
            mine = grad_kv[s, pl.ds(chip * 4 + core * 2, 2)].astype(F32)
            pair[s, chip * 2 : chip * 2 + 2] = (
                mine + arrived[s, chip * 2 : chip * 2 + 2].astype(F32)
            ).astype(BF16)
    scatter = Scatter("ctx", lambda i, p: pair.at[p, pl.ds((i // 2) * 2, 2)], *sums_k)
    scatter.begin()
    lane = lane_iota((256, 128))
    low = lane < 64
    first_half = lax.rem(lane, 64) < 32
    inv = 1 / 64
    head_q = jnp.zeros((1, 128), F32)
    head_k = jnp.zeros((1, 128), F32)
    for s in (2, 0, 3, 1):
        y = raw[s]
        a, b = y[:, :128], y[:, 128:]
        cos, sin = cosine[s], sine[s]
        lo, hi = head_sums(a * a, low)
        scale = jnp.where(low, lax.rsqrt(lo * inv + EPSILON), lax.rsqrt(hi * inv + EPSILON))
        n = a * scale
        d = grad_q[s].reshape(256, 128)
        g = d * cos - swap_halves(d, first_half) * sin
        head_q += jnp.sum(g * n, axis=0, keepdims=True)
        e = g * gains[0:1, :]
        lo, hi = head_sums(e * n, low)
        dq = scale * (e - n * jnp.where(low, lo * inv, hi * inv))
        d_qkv[s, :, 0:128] = dq.astype(BF16)
        lo, _ = head_sums(b * b, low)
        scale = lax.rsqrt(lo * inv + EPSILON)
        n = b * scale
        d = scatter.result(s).reshape(256, 128)
        g = d * cos - swap_halves(d, first_half) * sin
        head_k += jnp.sum(g * n, axis=0, keepdims=True)
        e = g * gains[1:2, :]
        lo, _ = head_sums(e * n, low)
        dk = scale * (e - n * (lo * inv))
        d_qkv[s, :, 128:256] = jnp.where(low, dk, d).astype(BF16)
        part[s] = dot_nt(d_qkv[s], w[...]).astype(BF16).reshape(2, 128, 1024)
    head_part[0:1, :] = head_q
    head_part[1:2, :] = head_k
    total = Scatter("mp", lambda i, p: part.at[p, :, rows_of(i), :], *sums_n)
    total.begin()
    gain_sum = jnp.zeros((1, 1024), F32)
    for p in (2, 0, 3, 1):
        g = total.result(p)
        t = x[p].astype(F32)
        scale = rms_scale(t)
        normed = t * scale
        gain_sum += jnp.sum((g * normed).reshape(32, 1024), axis=0, keepdims=True)
        in_grad[p] = (d_mixed[p] + norm_back(g, normed, scale, gain1[...])).astype(BF16)
    gain_part[...] = gain_sum
    for copy in copies:
        copy.wait_send()
    scatter.drain()
    total.drain()


def reduce_kernel(ffn, attn, ffn_out, attn_out, pair_f, pair_a, got_f, got_a, *scratch):
    enter(("ctx",), sib=True)
    sums_f, rest = take(scratch, 6)
    sums_a, rest = take(rest, 6)
    (sf, rf, sa, ra), (s1, r1) = take(rest, 4)
    ctx = lax.axis_index("ctx")
    core = lax.rem(ctx, 2)
    sib = sibling()

    def rows64(i):
        return pl.ds(pl.multiple_of(i * 64, 64), 64)

    copies = []
    for chip in range(8):
        for n, (src, got) in enumerate(((ffn, got_f), (attn, got_a))):
            copy = rcopy(
                src.at[:, rows64(chip * 2 + 1 - core), :],
                got.at[:, rows64(chip), :],
                s1.at[n, chip],
                r1.at[n, chip],
                "ctx",
                sib,
            )
            copy.start()
            copies.append(copy)
    work = ((ffn, got_f, pair_f), (attn, got_a, pair_a))
    for chip in range(8):
        for n, (src, got, pair) in enumerate(work):
            copies[chip * 2 + n].wait_recv()
            rows = slice(chip * 64, chip * 64 + 64)
            mine = src[:, rows64(chip * 2 + core), :].astype(F32)
            pair[:, rows, :] = (mine + got[:, rows, :].astype(F32)).astype(BF16)

    def piece(ref, i, p):
        return ref.at[:, pl.ds(pl.multiple_of((i // 2) * 64 + p * 16, 16), 16), :]

    def place(ref, i, p):
        return ref.at[:, pl.ds(pl.multiple_of(i * 64 + p * 16, 16), 16), :]

    scat_f = Scatter("ctx", lambda i, p: piece(pair_f, i, p), *sums_f)
    scat_a = Scatter("ctx", lambda i, p: piece(pair_a, i, p), *sums_a)
    scat_f.begin()
    scat_a.begin()
    gath_f = Gather("ctx", lambda i, p: place(ffn_out, i, p), sf, rf)
    gath_a = Gather("ctx", lambda i, p: place(attn_out, i, p), sa, ra)
    for p in (2, 0, 3, 1):
        place(ffn_out, ctx, p)[...] = scat_f.result(p).astype(BF16)
        gath_f.start_piece(p)
    for p in (2, 0, 3, 1):
        place(attn_out, ctx, p)[...] = scat_a.result(p).astype(BF16)
        gath_a.start_piece(p)
    forwards = []

    def forward(ref, n, index, slot):
        view = ref.at[:, rows64(index), :]
        copy = rcopy(view, view, s1.at[2 + n, slot], r1.at[2 + n, slot], "ctx", sib)
        copy.start()
        forwards.append(copy)

    forward(ffn_out, 0, ctx, 0)
    forward(attn_out, 1, ctx, 0)
    for phase in ("relay_row", "relay_opposite", "relay_last"):
        getattr(gath_f, phase)()
        getattr(gath_a, phase)()
    for slot, rel in enumerate(RELS):
        for n, (gath, ref) in enumerate(((gath_f, ffn_out), (gath_a, attn_out))):
            for p in range(4):
                gath.arrive(rel, p)
            forward(ref, n, gath.index[rel], slot + 1)
    for copy in copies + forwards:
        copy.wait_send()
    for slot, rel in enumerate(("M",) + RELS):
        for n, ref in enumerate((ffn_out, attn_out)):
            view = ref.at[:, rows64(gath_f.index[rel] + sib - ctx), :]
            rcopy(view, view, s1.at[2 + n, slot], r1.at[2 + n, slot], "ctx", sib).wait_recv()
    for item in (scat_f, scat_a, gath_f, gath_a):
        item.drain()


def gains_kernel(parts, total, by_mp, by_ctx, s1, r1, s2, r2):
    mp, ctx = lax.axis_index("mp"), lax.axis_index("ctx")
    barrier = pltpu.get_barrier_semaphore()
    for k in range(1, 8):
        pl.semaphore_signal(
            barrier, inc=1, device_id={"mp": lax.rem(mp + k, 8)}, device_id_type=MESH
        )
    for k in range(1, 16):
        pl.semaphore_signal(
            barrier, inc=1, device_id={"ctx": lax.rem(ctx + k, 16)}, device_id_type=MESH
        )
    pl.semaphore_wait(barrier, 22)
    copies = []
    for k in range(1, 8):
        copy = rcopy(
            parts, by_mp.at[k], s1.at[k], r1.at[k], "mp", lax.rem(mp + k, 8)
        )
        copy.start()
        copies.append(copy)
    by_mp[0] = parts[...]
    for copy in copies:
        copy.wait()
    mine = jnp.sum(by_mp[...], axis=0)
    by_ctx[0] = mine
    copies = []
    for k in range(1, 16):
        copy = rcopy(
            by_ctx.at[0], by_ctx.at[k], s2.at[k], r2.at[k], "ctx", lax.rem(ctx + k, 16)
        )
        copy.start()
        copies.append(copy)
    for copy in copies:
        copy.wait()
    total[...] = jnp.zeros_like(total)

    def add(i, c):
        total[...] += by_ctx[lax.rem(ctx - i + 16, 16)]
        return c

    lax.fori_loop(0, 16, add, 0)


def vm(n):
    return [pl.BlockSpec(memory_space=pltpu.VMEM)] * n


def sds(shape, dtype):
    return jax.ShapeDtypeStruct(shape, dtype)


def local(
    residual_in,
    attn_norm,
    query_key_value_weight,
    query_gain,
    key_gain,
    out_weight,
    ffn_norm,
    gate_up,
    down_weight,
    cotangent,
    positions,
    block_map,
):
    ctx_index = lax.axis_index("ctx")
    rows_shape = (4, 2, 16, 1024)
    full_shape = (4, 2, 128, 1024)
    piece = (2, 16, 1024)
    kv_piece = (2, 128, 128)
    dma = pltpu.SemaphoreType.DMA

    own = lax.dynamic_slice_in_dim(block_map, ctx_index * 2, 2)
    where = jnp.sum(
        jnp.where(block_map[None, :] == jnp.arange(32)[:, None], jnp.arange(32)[None, :], 0),
        axis=1,
    ).astype(jnp.int32)
    position = jnp.concatenate(
        [lax.dynamic_slice_in_dim(positions, own[j] * 128, 128, 1) for j in range(2)], axis=1
    ).astype(F32)
    inverse_freq = 1.0 / ROPE_BASE ** (jnp.arange(0, 64, 2, dtype=F32) / 64)
    angles = position[:, :, None] * inverse_freq
    cos32, sin32 = jnp.cos(angles), jnp.sin(angles)
    cosine = jnp.concatenate([cos32] * 4, axis=-1)
    sine = jnp.concatenate([-sin32, sin32] * 2, axis=-1)
    gains = jnp.stack(
        [jnp.concatenate([query_gain] * 2), jnp.concatenate([key_gain, jnp.ones_like(key_gain)])]
    )
    gain1 = attn_norm.reshape(1, 1024)
    gain2 = ffn_norm.reshape(1, 1024)
    w_qkv = query_key_value_weight.reshape(1024, 256)

    full1, cot_full, raw, queries, kv_all = pl.pallas_call(
        qkv_kernel,
        out_shape=(
            sds(full_shape, BF16),
            sds(full_shape, BF16),
            sds((4, 256, 256), F32),
            sds((4, 2, 256, 128), BF16),
            sds((4, 32, 128, 128), BF16),
        ),
        in_specs=vm(7),
        out_specs=tuple(vm(5)),
        scratch_shapes=Gather.scratch * 3 + (dma((8,)), dma((8,))),
        compiler_params=params(1),
    )(residual_in, cotangent, gain1, w_qkv, gains, cosine, sine)

    smem = [pl.BlockSpec(memory_space=pltpu.SMEM)] * 2
    attended, attended_high, logs = pl.pallas_call(
        attention_kernel,
        out_shape=(
            sds((4, 2, 128, 128), BF16),
            sds((4, 2, 128, 128), F32),
            sds((4, 2, 8, 256), F32),
        ),
        in_specs=smem + vm(2),
        out_specs=tuple(vm(3)),
        scratch_shapes=[pltpu.VMEM((4, 256, 128), F32)],
        compiler_params=pltpu.CompilerParams(vmem_limit_bytes=VMEM_LIMIT),
    )(own, where, queries, kv_all)

    mixed, full2 = pl.pallas_call(
        mix_kernel,
        out_shape=(sds(rows_shape, F32), sds(full_shape, BF16)),
        in_specs=vm(4),
        out_specs=tuple(vm(2)),
        scratch_shapes=(pltpu.VMEM(full_shape, BF16),) + Scatter.scratch(piece) + Gather.scratch,
        compiler_params=params(2),
    )(residual_in, attended, out_weight, gain2)

    rows2 = full2.reshape(1024, 1024)
    cot_rows = cot_full.reshape(1024, 1024)
    gate = dot(rows2, gate_up[:, 0, :])
    up = dot(rows2, gate_up[:, 1, :])
    sig = jax.nn.sigmoid(gate)
    active = (gate * sig * up).astype(BF16)
    part_o = dot(active, down_weight).astype(BF16)
    d_active = dot_nt(cot_rows, down_weight)
    d_gate = (d_active * up * sig * (1.0 + gate * (1.0 - sig))).astype(BF16)
    d_up = (d_active * gate * sig).astype(BF16)
    part_d = (dot_nt(d_gate, gate_up[:, 0, :]) + dot_nt(d_up, gate_up[:, 1, :])).astype(BF16)
    ffn_grads = jnp.stack(
        [
            dot_tn(rows2, d_gate).astype(BF16),
            dot_tn(rows2, d_up).astype(BF16),
            dot_tn(cot_rows, active).astype(BF16),
        ]
    )

    output, d_mixed, branch, d_att, gain2_part = pl.pallas_call(
        branch_kernel,
        out_shape=(
            sds(rows_shape, BF16),
            sds(rows_shape, F32),
            sds(full_shape, BF16),
            sds((4, 2, 128, 128), BF16),
            sds((1, 1024), F32),
        ),
        in_specs=vm(6),
        out_specs=tuple(vm(5)),
        scratch_shapes=Scatter.scratch(piece) * 2 + Gather.scratch,
        compiler_params=params(3),
    )(part_d.reshape(full_shape), part_o.reshape(full_shape), mixed, cotangent, gain2, out_weight)

    grad_q, grad_kv = pl.pallas_call(
        attention_back_kernel,
        out_shape=(sds((4, 2, 128, 128), F32), sds((4, 32, 128, 128), BF16)),
        in_specs=smem + vm(5),
        out_specs=tuple(vm(2)),
        scratch_shapes=[
            pltpu.VMEM((4, 32, 128, 128), F32),
            pltpu.VMEM((4, 256, 128), BF16),
            pltpu.VMEM((4, 128, 256), F32),
            pltpu.VMEM((4, 8, 256), F32),
        ],
        compiler_params=pltpu.CompilerParams(vmem_limit_bytes=VMEM_LIMIT),
    )(own, where, queries, kv_all, d_att, attended_high, logs)

    d_qkv, input_grad, gain1_part, head_part = pl.pallas_call(
        last_kernel,
        out_shape=(
            sds((4, 256, 256), BF16),
            sds(rows_shape, BF16),
            sds((1, 1024), F32),
            sds((2, 128), F32),
        ),
        in_specs=vm(10),
        out_specs=tuple(vm(4)),
        scratch_shapes=(
            pltpu.VMEM((4, 16, 128, 128), BF16),
            pltpu.VMEM((4, 16, 128, 128), BF16),
            pltpu.VMEM(full_shape, BF16),
        )
        + Scatter.scratch(kv_piece)
        + Scatter.scratch(piece)
        + (dma((8,)), dma((8,))),
        compiler_params=params(4),
    )(
        grad_kv, grad_q, raw, cosine, sine, gains, w_qkv, residual_in, gain1, d_mixed
    )

    qkv_part = dot_tn(full1.reshape(1024, 1024), d_qkv.reshape(1024, 256))
    out_part = dot_tn(branch.reshape(1024, 1024), attended.reshape(1024, 128))
    attn_grads = jnp.concatenate([qkv_part.astype(BF16), out_part.astype(BF16)], axis=1)[None]
    ffn_sum, attn_sum = pl.pallas_call(
        reduce_kernel,
        out_shape=(sds((3, 1024, 576), BF16), sds((1, 1024, 384), BF16)),
        in_specs=vm(2),
        out_specs=tuple(vm(2)),
        scratch_shapes=(
            pltpu.VMEM((3, 512, 576), BF16),
            pltpu.VMEM((1, 512, 384), BF16),
            pltpu.VMEM((3, 512, 576), BF16),
            pltpu.VMEM((1, 512, 384), BF16),
        )
        + Scatter.scratch((3, 16, 576))
        + Scatter.scratch((1, 16, 384))
        + Gather.scratch * 2
        + (dma((4, 8)), dma((4, 8))),
        compiler_params=params(5),
    )(ffn_grads, attn_grads)

    head_sum = head_part[0, :64] + head_part[0, 64:]
    small = jnp.concatenate(
        [
            gain1_part,
            gain2_part,
            jnp.pad(jnp.concatenate([head_sum, head_part[1, :64]]), (0, 896))[None],
            jnp.zeros((5, 1024), F32),
        ]
    )
    sums = pl.pallas_call(
        gains_kernel,
        out_shape=sds((8, 1024), F32),
        in_specs=vm(1),
        out_specs=vm(1)[0],
        scratch_shapes=[
            pltpu.VMEM((8, 8, 1024), F32),
            pltpu.VMEM((16, 8, 1024), F32),
            dma((8,)),
            dma((8,)),
            dma((16,)),
            dma((16,)),
        ],
        compiler_params=params(6),
    )(small)

    return (
        output,
        input_grad,
        sums[0],
        attn_sum[0, :, :256].astype(F32).reshape(1024, 1, 256),
        sums[2, :64],
        sums[2, 64:128],
        attn_sum[0, :, 256:].astype(F32).T,
        sums[1],
        jnp.stack([ffn_sum[0], ffn_sum[1]], axis=1).astype(F32),
        ffn_sum[2].astype(F32).T,
    )


def solution(mesh):
    return jax.shard_map(
        local,
        mesh=mesh,
        in_specs=(
            P(None, "ctx", "mp", None),
            P(),
            P(None, "mp", None),
            P(),
            P(),
            P("mp", None),
            P(),
            P(None, None, "mp"),
            P("mp", None),
            P(None, "ctx", "mp", None),
            P(),
            P(),
        ),
        out_specs=(
            P(None, "ctx", "mp", None),
            P(None, "ctx", "mp", None),
            P(),
            P(None, "mp", None),
            P(),
            P(),
            P("mp", None),
            P(),
            P(None, None, "mp"),
            P("mp", None),
        ),
        check_vma=False,
    )
```

```python
import functools
import math

import jax
import jax.numpy as jnp
from jax import lax
from jax.experimental import pallas as pl
from jax.experimental.pallas import tpu as pltpu
from jax.sharding import PartitionSpec as P

EPSILON = 1e-05
ROPE_BASE = 1000000.0
MESH = pl.DeviceIdType.MESH
F32 = jnp.float32
BF16 = jnp.bfloat16
RELS = ("L", "R", "X", "O", "OL", "OR", "OX")
VMEM_LIMIT = 56 << 20


def params(cid):
    return pltpu.CompilerParams(
        collective_id=cid, has_side_effects=True, vmem_limit_bytes=VMEM_LIMIT
    )


def rel_index(axis, rel):
    me = lax.axis_index(axis)
    core = 0
    if axis == "ctx":
        core = lax.rem(me, 2)
        me = me // 2
    pos = lax.rem(me, 4)
    row = me // 4
    step = {"L": 3, "R": 1, "X": 2, "M": 0}[rel[-1] if rel[-1] != "O" else "M"]
    if rel[0] == "O":
        row = 1 - row
    index = row * 4 + lax.rem(pos + step, 4)
    if axis == "ctx":
        index = index * 2 + core
    return index


def sibling():
    me = lax.axis_index("ctx")
    return me + 1 - 2 * lax.rem(me, 2)


def enter(axes, sib=False, extra=()):
    barrier = pltpu.get_barrier_semaphore()
    count = 0
    for axis in axes:
        for rel in ("L", "R", "O"):
            pl.semaphore_signal(
                barrier, inc=1, device_id={axis: rel_index(axis, rel)}, device_id_type=MESH
            )
            count += 1
    if sib:
        pl.semaphore_signal(barrier, inc=1, device_id={"ctx": sibling()}, device_id_type=MESH)
        count += 1
    pl.semaphore_wait(barrier, count)


def rcopy(src, dst, ssem, rsem, axis, index):
    return pltpu.make_async_remote_copy(
        src_ref=src,
        dst_ref=dst,
        send_sem=ssem,
        recv_sem=rsem,
        device_id={axis: index},
        device_id_type=MESH,
    )


class Gather:
    @staticmethod
    def scratch(K):
        return (pltpu.SemaphoreType.DMA((14 * K,)), pltpu.SemaphoreType.DMA((7, 2 * K)))

    def __init__(self, axis, dst, ssem, rsem):
        self.axis, self.dst, self.ssem, self.rsem = axis, dst, ssem, rsem
        self.index = {rel: rel_index(axis, rel) for rel in RELS + ("M",)}
        self.sent = []
        self.seen = set()

    def send(self, source, k, route, to, as_rel):
        view = self.dst(self.index[source], k, route)
        copy = rcopy(
            view,
            view,
            self.ssem.at[len(self.sent)],
            self.rsem.at[RELS.index(as_rel), 2 * k + route],
            self.axis,
            self.index[to],
        )
        copy.start()
        self.sent.append(copy)

    def arrive(self, rel, k, route):
        if (rel, k, route) in self.seen:
            return
        self.seen.add((rel, k, route))
        view = self.dst(self.index[rel], k, route)
        rcopy(
            view,
            view,
            self.ssem.at[0],
            self.rsem.at[RELS.index(rel), 2 * k + route],
            self.axis,
            self.index["L"],
        ).wait_recv()

    def start(self, k):
        self.send("M", k, 0, "R", "L")
        self.send("M", k, 1, "L", "R")
        self.send("M", k, 0, "O", "O")
        self.send("M", k, 1, "O", "O")
        self.send("M", k, 0, "L", "R")
        self.send("M", k, 1, "R", "L")

    def relay_row(self, k):
        self.arrive("L", k, 0)
        self.send("L", k, 0, "R", "X")
        self.arrive("R", k, 1)
        self.send("R", k, 1, "L", "X")

    def relay_opposite(self, k):
        self.arrive("O", k, 0)
        self.send("O", k, 0, "R", "OL")
        self.arrive("O", k, 1)
        self.send("O", k, 1, "L", "OR")
        self.send("O", k, 0, "L", "OR")
        self.send("O", k, 1, "R", "OL")

    def relay_last(self, k):
        self.arrive("OL", k, 0)
        self.send("OL", k, 0, "R", "OX")
        self.arrive("OR", k, 1)
        self.send("OR", k, 1, "L", "OX")

    def finish(self, k):
        for rel in RELS:
            for route in range(2):
                self.arrive(rel, k, route)

    def drain(self):
        for copy in self.sent:
            copy.wait_send()


class Scatter:
    @staticmethod
    def scratch(K, piece):
        return (
            pltpu.VMEM((2, K, 2) + piece, BF16),
            pltpu.VMEM((2, K, 2) + piece, BF16),
            pltpu.VMEM((2, 2, K, 2) + piece, BF16),
            pltpu.VMEM((2, K, 2) + piece, BF16),
            pltpu.SemaphoreType.DMA((14 * K,)),
            pltpu.SemaphoreType.DMA((14 * K,)),
        )

    def __init__(self, axis, K, part, relay, stage, arrived, across, ssem, rsem):
        self.axis, self.K, self.part = axis, K, part
        self.relay, self.stage, self.arrived, self.across = relay, stage, arrived, across
        self.ssem, self.rsem = ssem, rsem
        self.index = {rel: rel_index(axis, rel) for rel in RELS + ("M",)}
        self.sent = []

    def block(self, t, rel, k, route):
        name = rel if t == 0 else ("O" if rel == "M" else "O" + rel)
        return self.part(self.index[name], k, route)

    def relay_slot(self, t, k, route):
        return (t * self.K + k) * 2 + route

    def arrived_slot(self, t, d, k, route):
        return 4 * self.K + ((t * 2 + d) * self.K + k) * 2 + route

    def across_slot(self, k, route):
        return 12 * self.K + 2 * k + route

    def send(self, src, dst, rslot, to):
        copy = rcopy(
            src, dst, self.ssem.at[len(self.sent)], self.rsem.at[rslot], self.axis, self.index[to]
        )
        copy.start()
        self.sent.append(copy)

    def arrive(self, dst, rslot):
        rcopy(dst, dst, self.ssem.at[0], self.rsem.at[rslot], self.axis, self.index["L"]).wait_recv()

    def start(self, t, k):
        for route, to in ((0, "R"), (1, "L")):
            self.send(
                self.block(t, "X", k, route),
                self.relay.at[t, k, route],
                self.relay_slot(t, k, route),
                to,
            )
        for d, route, to in ((0, 1, "R"), (1, 0, "L")):
            self.send(
                self.block(t, to, k, route),
                self.arrived.at[t, d, k, route],
                self.arrived_slot(t, d, k, route),
                to,
            )

    def middle(self, t, k):
        for route, to in ((0, "R"), (1, "L")):
            self.arrive(self.relay.at[t, k, route], self.relay_slot(t, k, route))
            total = self.block(t, to, k, route)[...].astype(F32)
            total += self.relay[t, k, route].astype(F32)
            self.stage[t, k, route] = total.astype(BF16)
            self.send(
                self.stage.at[t, k, route],
                self.arrived.at[t, route, k, route],
                self.arrived_slot(t, route, k, route),
                to,
            )

    def row_sum(self, t, k, route):
        for d in range(2):
            self.arrive(self.arrived.at[t, d, k, route], self.arrived_slot(t, d, k, route))
        return (
            self.block(t, "M", k, route)[...].astype(F32)
            + self.arrived[t, 0, k, route].astype(F32)
            + self.arrived[t, 1, k, route].astype(F32)
        )

    def cross(self, k):
        for route in range(2):
            self.across[0, k, route] = self.row_sum(1, k, route).astype(BF16)
            self.send(
                self.across.at[0, k, route],
                self.across.at[1, k, route],
                self.across_slot(k, route),
                "O",
            )

    def result(self, k, route):
        total = self.row_sum(0, k, route)
        self.arrive(self.across.at[1, k, route], self.across_slot(k, route))
        return total + self.across[1, k, route].astype(F32)

    def drain(self):
        for copy in self.sent:
            copy.wait_send()


def take(refs, count):
    return refs[:count], refs[count:]


def lane_iota(shape):
    return lax.broadcasted_iota(jnp.int32, shape, len(shape) - 1)


def dot_nt(a, b):
    return lax.dot_general(a, b, (((1,), (1,)), ((), ())), preferred_element_type=F32)


def dot_tn(a, b):
    return lax.dot_general(a, b, (((0,), (0,)), ((), ())), preferred_element_type=F32)


def dot(a, b):
    return jnp.dot(a, b, preferred_element_type=F32)


def head_sums(values, low):
    zero = jnp.zeros_like(values)
    first = jnp.sum(jnp.where(low, values, zero), axis=-1, keepdims=True)
    second = jnp.sum(jnp.where(low, zero, values), axis=-1, keepdims=True)
    return first, second


def swap_halves(values, first_half):
    return jnp.where(first_half, pltpu.roll(values, 96, 1), pltpu.roll(values, 32, 1))


def rms_scale(values):
    return lax.rsqrt(jnp.mean(values * values, axis=-1, keepdims=True) + EPSILON)


def norm_back(gradient, normed, scale_rows, gain_vec):
    scaled = gradient * gain_vec
    return scale_rows * (scaled - normed * jnp.mean(scaled * normed, axis=-1, keepdims=True))


def rows_of(index):
    return pl.ds(pl.multiple_of(index * 16, 16), 16)


def mp_rows(ref):
    return lambda i, k, route: ref.at[k, route, rows_of(i), :]


def kv_rows(ref):
    return lambda i, k, route: ref.at[k, i * 2 + route]


def forward_copy(view, ssem, rsem):
    copy = rcopy(view, view, ssem, rsem, "ctx", sibling())
    copy.start()
    return copy


def qkv_kernel(
    x, cot, gain1, w, gains, cosine, sine, full, cot_full, raw, queries, kv_all, *sems
):
    mp = lax.axis_index("mp")
    ctx = lax.axis_index("ctx")
    enter(("mp", "ctx"), sib=True)
    (s1, r1, s2, r2, s3, r3), (s4, r4) = take(sems, 6)
    first = Gather("mp", mp_rows(full), s1, r1)
    keys = Gather("ctx", kv_rows(kv_all), s2, r2)
    second = Gather("mp", mp_rows(cot_full), s3, r3)
    for s in range(4):
        t = x[s].astype(F32)
        full[s, :, rows_of(mp), :] = (t * rms_scale(t) * gain1[...]).astype(BF16)
        first.start(s)
    for s in range(4):
        cot_full[s, :, rows_of(mp), :] = cot[s]
    lane = lane_iota((256, 128))
    low = lane < 64
    first_half = lax.rem(lane, 64) < 32
    forwards = []

    def forward(rel, s):
        slot = (("M",) + RELS).index(rel)
        view = kv_all.at[s, pl.ds(keys.index[rel] * 2, 2)]
        forwards.append(forward_copy(view, s4.at[slot, s], r4.at[slot, s]))

    def project(s):
        y = dot(full[s].reshape(256, 1024), w[...])
        raw[s] = y
        a, b = y[:, :128], y[:, 128:]
        cos, sin = cosine[s], sine[s]
        lo, _ = head_sums(b * b, low)
        g = b * lax.rsqrt(lo * (1 / 64) + EPSILON) * gains[1:2, :]
        turned = g * cos + swap_halves(g, first_half) * sin
        packed = jnp.where(low, turned, b).astype(BF16)
        kv_all[s, pl.ds(ctx * 2, 2)] = packed.reshape(2, 128, 128)
        keys.start(s)
        forward("M", s)
        lo, hi = head_sums(a * a, low)
        scale = jnp.where(
            low, lax.rsqrt(lo * (1 / 64) + EPSILON), lax.rsqrt(hi * (1 / 64) + EPSILON)
        )
        g = a * scale * gains[0:1, :]
        turned = g * cos + swap_halves(g, first_half) * sin
        zero = jnp.zeros_like(turned)
        head0 = jnp.where(low, turned, zero).astype(BF16)
        head1 = jnp.where(low, pltpu.roll(turned, 64, 1), zero).astype(BF16)
        for t in range(2):
            queries[s, t, 0:128] = head0[t * 128 : t * 128 + 128]
            queries[s, t, 128:256] = head1[t * 128 : t * 128 + 128]

    def at(k, *steps):
        if 0 <= k < 4:
            for step in steps:
                step(k)

    def finish_keys(s):
        for rel in RELS:
            for route in range(2):
                keys.arrive(rel, s, route)
            forward(rel, s)

    for step in range(4 + 6):
        at(step, first.relay_row, first.relay_opposite)
        at(step - 1, first.relay_last)
        at(step - 2, first.finish, project)
        at(step - 3, keys.relay_row, keys.relay_opposite)
        at(step - 3, second.start)
        at(step - 4, keys.relay_last)
        at(step - 4, second.relay_row, second.relay_opposite)
        at(step - 5, finish_keys)
        at(step - 5, second.relay_last)
    for s in range(4):
        second.finish(s)
    first.drain()
    keys.drain()
    second.drain()
    for copy in forwards:
        copy.wait_send()
    for s in range(4):
        for slot, rel in enumerate(("M",) + RELS):
            view = kv_all.at[s, pl.ds((keys.index[rel] + sibling() - ctx) * 2, 2)]
            rcopy(view, view, s4.at[slot, s], r4.at[slot, s], "ctx", sibling()).wait_recv()


def attention_kernel(own, where, queries, kv_all, low_out, high_out, logs, acc):
    lane_k = lane_iota((256, 128)) < 64
    for j in range(2):
        mine = own[j]
        acc[...] = jnp.zeros_like(acc)

        def step(i, masked):
            slot0, slot1 = where[2 * i], where[2 * i + 1]
            if masked:
                row = lax.rem(lax.broadcasted_iota(jnp.int32, (256, 256), 0), 128)
                col = lax.broadcasted_iota(jnp.int32, (256, 256), 1)
                keep = col + 256 * i <= row + 128 * mine
            for s in range(4):
                kv = jnp.concatenate([kv_all[s, slot0], kv_all[s, slot1]], axis=0)
                weights = jnp.exp(dot_nt(queries[s, j], kv) * 0.125)
                if masked:
                    weights = jnp.where(keep, weights, 0.0)
                ones = jnp.where(lane_k, jnp.ones_like(kv), kv)
                acc[s] += dot(weights.astype(BF16), ones)

        last = mine // 2
        lax.fori_loop(0, last, lambda i, c: (step(i, False), c)[1], 0)
        step(last, True)
        low = lane_iota((128, 128)) < 64
        for s in range(4):
            a = acc[s]
            o = a * pltpu.roll(1.0 / a, 64, 1)
            both = jnp.where(low, pltpu.roll(o[0:128], 64, 1), o[128:256])
            low_out[s, j] = both.astype(BF16)
            high_out[s, j] = both
            logs[s, j] = jnp.log(a.T[0:8])


def attention_back_kernel(
    own, where, queries, kv_all, grad_out, out, logs, grad_q, grad_kv, acc, grad_pad, turned, delta
):
    acc[...] = jnp.zeros_like(acc)
    low = lane_iota((128, 128)) < 64
    for j in range(2):
        mine = own[j]
        turned[...] = jnp.zeros_like(turned)
        for s in range(4):
            g = grad_out[s, j]
            gf = g.astype(F32)
            zero = jnp.zeros_like(gf)
            grad_pad[s, 0:128] = jnp.where(low, zero, pltpu.roll(gf, 64, 1)).astype(BF16)
            grad_pad[s, 128:256] = jnp.where(low, zero, gf).astype(BF16)
            product = (gf * out[s, j]).T
            delta[s, :, 0:128] = jnp.broadcast_to(
                jnp.sum(product[0:64], axis=0, keepdims=True), (8, 128)
            )
            delta[s, :, 128:256] = jnp.broadcast_to(
                jnp.sum(product[64:128], axis=0, keepdims=True), (8, 128)
            )

        def step(i, masked):
            slot0, slot1 = where[2 * i], where[2 * i + 1]
            if masked:
                col = lax.rem(lax.broadcasted_iota(jnp.int32, (256, 256), 1), 128)
                row = lax.broadcasted_iota(jnp.int32, (256, 256), 0)
                keep = row + 256 * i <= col + 128 * mine
            for s in range(4):
                kv = jnp.concatenate([kv_all[s, slot0], kv_all[s, slot1]], axis=0)
                q, g = queries[s, j], grad_pad[s]
                probs = jnp.exp(dot_nt(kv, q) * 0.125 - logs[s, j, 0:1])
                if masked:
                    probs = jnp.where(keep, probs, 0.0)
                scores = (probs * (dot_nt(kv, g) - delta[s, 0:1])).astype(BF16)
                turned[s] += dot_tn(kv, scores)
                block = dot(
                    jnp.concatenate([scores, probs.astype(BF16)], axis=1),
                    jnp.concatenate([q, g], axis=0),
                )
                acc[s, slot0] += block[0:128]
                acc[s, slot1] += block[128:256]

        last = mine // 2
        lax.fori_loop(0, last, lambda i, c: (step(i, False), c)[1], 0)
        step(last, True)
        for s in range(4):
            t = turned[s].T * 0.125
            grad_q[s, j] = jnp.where(low, t[0:128], pltpu.roll(t[128:256], 64, 1))
    scale = jnp.where(low, 0.125, 1.0)

    def finish(n, c):
        for s in range(4):
            grad_kv[s, n] = (acc[s, n] * scale).astype(BF16)
        return c

    lax.fori_loop(0, 32, finish, 0)


class Reduce:
    @staticmethod
    def scratch(A, R):
        return (
            pltpu.VMEM((A, R, 512), BF16),
            pltpu.VMEM((A, R, 512), BF16),
            pltpu.SemaphoreType.DMA((2,)),
            pltpu.SemaphoreType.DMA((2,)),
        ) + Scatter.scratch(1, (A, R // 4, 128))

    def __init__(self, source, got, pair, ssem, rsem, *rest):
        self.source, self.got, self.pair = source, got, pair
        self.ssem, self.rsem = ssem, rsem
        self.rows = source.shape[1] // 4
        self.sum = Scatter("ctx", 1, self.piece, *rest)

    def piece(self, i, k, route):
        row = pl.multiple_of(lax.rem(i // 2, 4) * self.rows, 16)
        column = pl.multiple_of((i // 8) * 256 + route * 128, 128)
        return self.pair.at[:, pl.ds(row, self.rows), pl.ds(column, 128)]

    def columns(self, y, core):
        return pl.ds(pl.multiple_of((2 * y + core) * 256, 256), 256)

    def exchange(self):
        core = lax.rem(lax.axis_index("ctx"), 2)
        self.copies = []
        for y in range(2):
            copy = rcopy(
                self.source.at[:, :, self.columns(y, 1 - core)],
                self.got.at[:, :, y * 256 : y * 256 + 256],
                self.ssem.at[y],
                self.rsem.at[y],
                "ctx",
                sibling(),
            )
            copy.start()
            self.copies.append(copy)

    def start(self):
        core = lax.rem(lax.axis_index("ctx"), 2)
        for y in range(2):
            self.copies[y].wait_recv()
            columns = slice(y * 256, y * 256 + 256)
            mine = self.source[:, :, self.columns(y, core)].astype(F32)
            self.pair[:, :, columns] = (mine + self.got[:, :, columns].astype(F32)).astype(BF16)
        self.sum.start(1, 0)
        self.sum.start(0, 0)

    def result(self, store):
        for route in range(2):
            store(route, self.sum.result(0, route).astype(BF16))

    def drain(self):
        for copy in self.copies:
            copy.wait_send()
        self.sum.drain()


class Spread:
    @staticmethod
    def scratch():
        return Gather.scratch(1) + (pltpu.SemaphoreType.DMA((8,)), pltpu.SemaphoreType.DMA((8,)))

    def __init__(self, target, ssem, rsem, fs, fr):
        self.target, self.fs, self.fr = target, fs, fr
        self.rows = target.shape[1] // 4
        self.gather = Gather("ctx", self.piece, ssem, rsem)
        self.forwards = []

    def view(self, i, shift, width):
        row = pl.multiple_of(lax.rem(i // 2, 4) * self.rows, 16)
        column = pl.multiple_of((2 * (i // 8) + lax.rem(i, 2)) * 256 + shift, 128)
        return self.target.at[:, pl.ds(row, self.rows), pl.ds(column, width)]

    def piece(self, i, k, route):
        return self.view(i, route * 128, 128)

    def own(self):
        return self.view(lax.axis_index("ctx"), 0, 256)

    def forward(self, rel):
        slot = len(self.forwards)
        view = self.view(self.gather.index[rel], 0, 256)
        self.forwards.append(forward_copy(view, self.fs.at[slot], self.fr.at[slot]))

    def start(self):
        self.gather.start(0)
        self.forward("M")

    def finish(self):
        for rel in RELS:
            for route in range(2):
                self.gather.arrive(rel, 0, route)
            self.forward(rel)

    def drain(self):
        self.gather.drain()
        ctx = lax.axis_index("ctx")
        for slot, rel in enumerate(("M",) + RELS):
            self.forwards[slot].wait_send()
            view = self.view(self.gather.index[rel] + sibling() - ctx, 0, 256)
            rcopy(view, view, self.fs.at[slot], self.fr.at[slot], "ctx", sibling()).wait_recv()


def middle_kernel(
    x, attended, w, gain2, cot, cot_full, gate_up, down,
    mixed, d_mixed, part_o, d_att, gain_part, out_part, ffn_own,
    part, full, part_d, branch, turned, grads, *scratch,
):
    mp = lax.axis_index("mp")
    enter(("mp", "ctx"), sib=True)
    sums1, rest = take(scratch, 6)
    sums2, rest = take(rest, 6)
    (s1, r1, s2, r2), sums3 = take(rest, 4)
    rs1 = Scatter("mp", 4, mp_rows(part), *sums1)
    rs2 = Scatter("mp", 4, mp_rows(part_d), *sums2)
    ag2 = Gather("mp", mp_rows(full), s1, r1)
    ag3 = Gather("mp", mp_rows(branch), s2, r2)
    reduce = Reduce(grads, *sums3)

    def mix(k):
        for t in range(2):
            m = x[k, t].astype(F32) + rs1.result(k, t)
            mixed[k, t] = m
            full[k, t, rows_of(mp), :] = (m * rms_scale(m) * gain2[...]).astype(BF16)
        ag2.start(k)

    def feed(k):
        rows = full[k].reshape(256, 1024)
        columns = slice(k * 256, k * 256 + 256)
        gate = dot_nt(rows, gate_up[0])
        up = dot_nt(rows, gate_up[1])
        sig = 1.0 / (1.0 + jnp.exp(-gate))
        d_active = dot_nt(cot_full[k].reshape(256, 1024), down[...])
        d_gate = (d_active * up * sig * (1.0 + gate * (1.0 - sig))).astype(BF16)
        d_up = (d_active * gate * sig).astype(BF16)
        both = dot(d_gate, gate_up[0]) + dot(d_up, gate_up[1])
        part_d[k] = both.astype(BF16).reshape(2, 128, 1024)
        rs2.start(1, k)
        rs2.start(0, k)
        active = (gate * sig * up).astype(BF16)
        part_o[k] = dot(active, down[...]).astype(BF16).reshape(2, 128, 1024)
        turned[0, :, columns] = d_gate.T
        turned[1, :, columns] = d_up.T
        turned[2, :, columns] = active.T

    def weigh():
        def tile(n, c):
            columns = pl.ds(pl.multiple_of(n * 256, 256), 256)
            rows = full[:, :, :, columns].reshape(1024, 256)
            for i in range(2):
                grads[i, :, columns] = dot(turned[i], rows).astype(BF16)
            rows = cot_full[:, :, :, columns].reshape(1024, 256)
            grads[2, :, columns] = dot(turned[2], rows).astype(BF16)
            return c

        lax.fori_loop(0, 4, tile, 0)

    gain_part[...] = jnp.zeros_like(gain_part)

    def back(k):
        for t in range(2):
            g = rs2.result(k, t)
            m = mixed[k, t]
            scale = rms_scale(m)
            normed = m * scale
            gain_part[...] += jnp.sum(g * normed, axis=0, keepdims=True)
            dm = cot[k, t].astype(F32) + norm_back(g, normed, scale, gain2[...])
            d_mixed[k, t] = dm
            branch[k, t, rows_of(mp), :] = dm.astype(BF16)
        ag3.start(k)

    def attend(k):
        rows = branch[k].reshape(256, 1024)
        d_att[k] = dot_nt(rows, w[...]).astype(BF16).reshape(2, 128, 128)

    def at(k, *steps):
        if 0 <= k < 4:
            for step in steps:
                step(k)

    for k in range(4):
        part[k] = dot(attended[k].reshape(256, 128), w[...]).astype(BF16).reshape(2, 128, 1024)
        rs1.start(1, k)
        rs1.start(0, k)
    for step in range(4 + 11):
        at(step, lambda k: rs1.middle(1, k))
        at(step - 1, rs1.cross, lambda k: rs1.middle(0, k))
        at(step - 2, mix)
        at(step - 3, ag2.relay_row, ag2.relay_opposite)
        at(step - 4, ag2.relay_last)
        at(step - 5, ag2.finish, feed)
        if step == 8:
            weigh()
            reduce.exchange()
        at(step - 6, lambda k: rs2.middle(1, k))
        at(step - 7, rs2.cross, lambda k: rs2.middle(0, k))
        if step == 9:
            reduce.start()
        at(step - 8, back)
        if step == 10:
            reduce.sum.middle(1, 0)
        if step == 11:
            reduce.sum.cross(0)
            reduce.sum.middle(0, 0)
        at(step - 9, ag3.relay_row, ag3.relay_opposite)
        at(step - 10, ag3.relay_last)
        at(step - 11, ag3.finish, attend)
    rows = attended[...].reshape(1024, 128).T
    for n in range(4):
        columns = slice(n * 256, n * 256 + 256)
        out_part[:, columns] = dot(rows, branch[:, :, :, columns].reshape(1024, 256)).astype(BF16)

    def store(route, value):
        ffn_own[:, :, route * 128 : route * 128 + 128] = value

    reduce.result(store)
    for item in (rs1, ag2, rs2, ag3, reduce):
        item.drain()


def last_kernel(
    grad_kv, grad_q, raw, cosine, sine, gains, w, x, gain1, d_mixed,
    mixed, part_o, full, out_part, ffn_own, gain2_part,
    out, in_grad, ffn_sum, attn_sum, total,
    pair, got, d_qkv, part, grads, small, by_mp, by_ctx, *scratch,
):
    ctx = lax.axis_index("ctx")
    mp = lax.axis_index("mp")
    barrier = pltpu.get_barrier_semaphore()
    for axis, size in (("mp", 8), ("ctx", 16)):
        me = lax.axis_index(axis)
        for n in range(1, size):
            pl.semaphore_signal(
                barrier, inc=1, device_id={axis: lax.rem(me + n, size)}, device_id_type=MESH
            )
    pl.semaphore_wait(barrier, 22)
    sums_k, rest = take(scratch, 6)
    sums_o, rest = take(rest, 6)
    sums_n, rest = take(rest, 6)
    sums_a, rest = take(rest, 10)
    spread_f, rest = take(rest, 4)
    spread_a, rest = take(rest, 4)
    s1, r1, s2, r2, s3, r3 = rest
    core = lax.rem(ctx, 2)
    sib = sibling()
    copies = []
    for s in range(4):
        for chip in range(8):
            src = grad_kv.at[s, pl.ds(chip * 4 + (1 - core) * 2, 2)]
            copy = rcopy(
                src, got.at[s, pl.ds(chip * 2, 2)], s1.at[s, chip], r1.at[s, chip], "ctx", sib
            )
            copy.start()
            copies.append(copy)
    rs_k = Scatter("ctx", 4, lambda i, k, route: pair.at[k, (i // 2) * 2 + route], *sums_k)
    rs_o = Scatter("mp", 4, mp_rows(part_o), *sums_o)
    rs_n = Scatter("mp", 4, mp_rows(part), *sums_n)
    ffn = Spread(ffn_sum, *spread_f)
    reduce = Reduce(grads, *sums_a)
    attn = Spread(attn_sum, *spread_a)
    ffn.own()[...] = ffn_own[...]
    for s in range(4):
        rs_o.start(1, s)
        rs_o.start(0, s)
        for chip in range(8):
            copies[s * 8 + chip].wait_recv()
            mine = grad_kv[s, pl.ds(chip * 4 + core * 2, 2)].astype(F32)
            both = mine + got[s, chip * 2 : chip * 2 + 2].astype(F32)
            pair[s, chip * 2 : chip * 2 + 2] = both.astype(BF16)
        rs_k.start(1, s)
        rs_k.start(0, s)
    grads[0, 256:384, :] = out_part[...]
    lane = lane_iota((256, 128))
    low = lane < 64
    first_half = lax.rem(lane, 64) < 32
    inv = 1 / 64
    small[...] = jnp.zeros_like(small)
    small[1:2, :] = gain2_part[...]

    def project(s):
        y = raw[s]
        a, b = y[:, :128], y[:, 128:]
        cos, sin = cosine[s], sine[s]
        lo, hi = head_sums(a * a, low)
        scale = jnp.where(low, lax.rsqrt(lo * inv + EPSILON), lax.rsqrt(hi * inv + EPSILON))
        n = a * scale
        d = grad_q[s].reshape(256, 128)
        g = d * cos - swap_halves(d, first_half) * sin
        small[2:3, 0:128] += jnp.sum(g * n, axis=0, keepdims=True)
        e = g * gains[0:1, :]
        lo, hi = head_sums(e * n, low)
        dq = scale * (e - n * jnp.where(low, lo * inv, hi * inv))
        d_qkv[s, :, 0:128] = dq.astype(BF16)
        lo, _ = head_sums(b * b, low)
        scale = lax.rsqrt(lo * inv + EPSILON)
        n = b * scale
        d = jnp.concatenate([rs_k.result(s, 0), rs_k.result(s, 1)], axis=0)
        g = d * cos - swap_halves(d, first_half) * sin
        small[3:4, 0:128] += jnp.sum(g * n, axis=0, keepdims=True)
        e = g * gains[1:2, :]
        lo, _ = head_sums(e * n, low)
        dk = scale * (e - n * (lo * inv))
        d_qkv[s, :, 128:256] = jnp.where(low, dk, d).astype(BF16)
        part[s] = dot_nt(d_qkv[s], w[...]).astype(BF16).reshape(2, 128, 1024)
        rs_n.start(1, s)
        rs_n.start(0, s)

    def write_out(s):
        for t in range(2):
            out[s, t] = (mixed[s, t] + rs_o.result(s, t)).astype(BF16)

    def weigh():
        rows = d_qkv[...].reshape(1024, 256).T
        for n in range(4):
            columns = slice(n * 256, n * 256 + 256)
            value = dot(rows, full[:, :, :, columns].reshape(1024, 256))
            grads[0, 0:256, columns] = value.astype(BF16)

    def write_grad(s):
        for t in range(2):
            g = rs_n.result(s, t)
            v = x[s, t].astype(F32)
            scale = rms_scale(v)
            normed = v * scale
            small[0:1, :] += jnp.sum(g * normed, axis=0, keepdims=True)
            in_grad[s, t] = (d_mixed[s, t] + norm_back(g, normed, scale, gain1[...])).astype(BF16)

    def at(k, *steps):
        if 0 <= k < 4:
            for step in steps:
                step(k)

    for step in range(4 + 5):
        at(step, lambda k: rs_k.middle(1, k), lambda k: rs_o.middle(1, k))
        at(step - 1, rs_k.cross, lambda k: rs_k.middle(0, k))
        at(step - 1, rs_o.cross, lambda k: rs_o.middle(0, k))
        if step == 4:
            ffn.start()
        at(step - 2, project)
        if step == 5:
            weigh()
            reduce.exchange()
        at(step - 3, lambda k: rs_n.middle(1, k))
        at(step - 4, rs_n.cross, lambda k: rs_n.middle(0, k))
        if step == 6:
            reduce.start()
            ffn.gather.relay_row(0)
            ffn.gather.relay_opposite(0)
        if step == 7:
            reduce.sum.middle(1, 0)
        at(step - 3, write_out)
        at(step - 5, write_grad)
    copies2 = []
    for n in range(1, 8):
        copy = rcopy(small, by_mp.at[n], s2.at[n], r2.at[n], "mp", lax.rem(mp + n, 8))
        copy.start()
        copies2.append(copy)
    reduce.sum.cross(0)
    reduce.sum.middle(0, 0)
    ffn.gather.relay_last(0)

    def store(route, value):
        attn.piece(ctx, 0, route)[...] = value

    reduce.result(store)
    attn.start()
    by_mp[0] = small[...]
    for copy in copies2:
        copy.wait()
    by_ctx[0] = jnp.sum(by_mp[...], axis=0)
    copies3 = []
    for n in range(1, 16):
        copy = rcopy(
            by_ctx.at[0], by_ctx.at[n], s3.at[n], r3.at[n], "ctx", lax.rem(ctx + n, 16)
        )
        copy.start()
        copies3.append(copy)
    attn.gather.relay_row(0)
    attn.gather.relay_opposite(0)
    ffn.finish()
    attn.gather.relay_last(0)
    for copy in copies3:
        copy.wait()
    total[...] = jnp.zeros_like(total)

    def add(i, c):
        total[...] += by_ctx[lax.rem(ctx - i + 16, 16)]
        return c

    lax.fori_loop(0, 16, add, 0)
    attn.finish()
    for copy in copies:
        copy.wait_send()
    for item in (rs_k, rs_o, rs_n, reduce, ffn, attn):
        item.drain()


def vm(n):
    return [pl.BlockSpec(memory_space=pltpu.VMEM)] * n


def sds(shape, dtype):
    return jax.ShapeDtypeStruct(shape, dtype)


def local(
    residual_in,
    attn_norm,
    query_key_value_weight,
    query_gain,
    key_gain,
    out_weight,
    ffn_norm,
    gate_up,
    down_weight,
    cotangent,
    positions,
    block_map,
):
    ctx_index = lax.axis_index("ctx")
    rows_shape = (4, 2, 16, 1024)
    full_shape = (4, 2, 128, 1024)
    piece = (16, 1024)
    dma = pltpu.SemaphoreType.DMA

    own = lax.dynamic_slice_in_dim(block_map, ctx_index * 2, 2)
    where = jnp.sum(
        jnp.where(block_map[None, :] == jnp.arange(32)[:, None], jnp.arange(32)[None, :], 0),
        axis=1,
    ).astype(jnp.int32)
    position = jnp.concatenate(
        [lax.dynamic_slice_in_dim(positions, own[j] * 128, 128, 1) for j in range(2)], axis=1
    ).astype(F32)
    inverse_freq = 1.0 / ROPE_BASE ** (jnp.arange(0, 64, 2, dtype=F32) / 64)
    angles = position[:, :, None] * inverse_freq
    cos32, sin32 = jnp.cos(angles), jnp.sin(angles)
    cosine = jnp.concatenate([cos32] * 4, axis=-1)
    sine = jnp.concatenate([-sin32, sin32] * 2, axis=-1)
    gains = jnp.stack(
        [jnp.concatenate([query_gain] * 2), jnp.concatenate([key_gain, jnp.ones_like(key_gain)])]
    )
    gain1 = attn_norm.reshape(1, 1024)
    gain2 = ffn_norm.reshape(1, 1024)
    w_qkv = query_key_value_weight.reshape(1024, 256)

    full1, cot_full, raw, queries, kv_all = pl.pallas_call(
        qkv_kernel,
        out_shape=(
            sds(full_shape, BF16),
            sds(full_shape, BF16),
            sds((4, 256, 256), F32),
            sds((4, 2, 256, 128), BF16),
            sds((4, 32, 128, 128), BF16),
        ),
        in_specs=vm(7),
        out_specs=tuple(vm(5)),
        scratch_shapes=Gather.scratch(4) * 3 + (dma((8, 4)), dma((8, 4))),
        compiler_params=params(1),
    )(residual_in, cotangent, gain1, w_qkv, gains, cosine, sine)

    smem = [pl.BlockSpec(memory_space=pltpu.SMEM)] * 2
    attended, attended_high, logs = pl.pallas_call(
        attention_kernel,
        out_shape=(
            sds((4, 2, 128, 128), BF16),
            sds((4, 2, 128, 128), F32),
            sds((4, 2, 8, 256), F32),
        ),
        in_specs=smem + vm(2),
        out_specs=tuple(vm(3)),
        scratch_shapes=[pltpu.VMEM((4, 256, 128), F32)],
        compiler_params=pltpu.CompilerParams(vmem_limit_bytes=VMEM_LIMIT),
    )(own, where, queries, kv_all)

    gate_up_t = jnp.transpose(gate_up, (1, 2, 0))
    mixed, d_mixed, part_o, d_att, gain2_part, out_part, ffn_own = pl.pallas_call(
        middle_kernel,
        out_shape=(
            sds(rows_shape, F32),
            sds(rows_shape, F32),
            sds(full_shape, BF16),
            sds((4, 2, 128, 128), BF16),
            sds((1, 1024), F32),
            sds((128, 1024), BF16),
            sds((3, 144, 256), BF16),
        ),
        in_specs=vm(8),
        out_specs=tuple(vm(7)),
        scratch_shapes=(pltpu.VMEM(full_shape, BF16),) * 4
        + (pltpu.VMEM((3, 576, 1024), BF16),) * 2
        + Scatter.scratch(4, piece) * 2
        + Gather.scratch(4) * 2
        + Reduce.scratch(3, 576),
        compiler_params=params(2),
    )(
        residual_in, attended, out_weight, gain2, cotangent, cot_full, gate_up_t, down_weight
    )

    grad_q, grad_kv = pl.pallas_call(
        attention_back_kernel,
        out_shape=(sds((4, 2, 128, 128), F32), sds((4, 32, 128, 128), BF16)),
        in_specs=smem + vm(5),
        out_specs=tuple(vm(2)),
        scratch_shapes=[
            pltpu.VMEM((4, 32, 128, 128), F32),
            pltpu.VMEM((4, 256, 128), BF16),
            pltpu.VMEM((4, 128, 256), F32),
            pltpu.VMEM((4, 8, 256), F32),
        ],
        compiler_params=pltpu.CompilerParams(vmem_limit_bytes=VMEM_LIMIT),
    )(own, where, queries, kv_all, d_att, attended_high, logs)

    output, input_grad, ffn_sum, attn_sum, sums = pl.pallas_call(
        last_kernel,
        out_shape=(
            sds(rows_shape, BF16),
            sds(rows_shape, BF16),
            sds((3, 576, 1024), BF16),
            sds((1, 384, 1024), BF16),
            sds((8, 1024), F32),
        ),
        in_specs=vm(16),
        out_specs=tuple(vm(5)),
        scratch_shapes=(
            pltpu.VMEM((4, 16, 128, 128), BF16),
            pltpu.VMEM((4, 16, 128, 128), BF16),
            pltpu.VMEM((4, 256, 256), BF16),
            pltpu.VMEM(full_shape, BF16),
            pltpu.VMEM((1, 384, 1024), BF16),
            pltpu.VMEM((8, 1024), F32),
            pltpu.VMEM((8, 8, 1024), F32),
            pltpu.VMEM((16, 8, 1024), F32),
        )
        + Scatter.scratch(4, (128, 128))
        + Scatter.scratch(4, piece) * 2
        + Reduce.scratch(1, 384)
        + Spread.scratch() * 2
        + (dma((4, 8)), dma((4, 8)), dma((8,)), dma((8,)), dma((16,)), dma((16,))),
        compiler_params=params(3),
    )(
        grad_kv, grad_q, raw, cosine, sine, gains, w_qkv, residual_in, gain1, d_mixed,
        mixed, part_o, full1, out_part, ffn_own, gain2_part,
    )

    return (
        output,
        input_grad,
        sums[0],
        attn_sum[0, :256].astype(F32).T.reshape(1024, 1, 256),
        sums[2, :64] + sums[2, 64:128],
        sums[3, :64],
        attn_sum[0, 256:].astype(F32),
        sums[1],
        jnp.transpose(ffn_sum[:2].astype(F32), (2, 0, 1)),
        ffn_sum[2].astype(F32),
    )


def solution(mesh):
    return jax.shard_map(
        local,
        mesh=mesh,
        in_specs=(
            P(None, "ctx", "mp", None),
            P(),
            P(None, "mp", None),
            P(),
            P(),
            P("mp", None),
            P(),
            P(None, None, "mp"),
            P("mp", None),
            P(None, "ctx", "mp", None),
            P(),
            P(),
        ),
        out_specs=(
            P(None, "ctx", "mp", None),
            P(None, "ctx", "mp", None),
            P(),
            P(None, "mp", None),
            P(),
            P(),
            P("mp", None),
            P(),
            P(None, None, "mp"),
            P("mp", None),
        ),
        check_vma=False,
    )
```

```python
import functools
import math

import jax
import jax.numpy as jnp
import numpy as np
from jax import lax
from jax.experimental import pallas as pl
from jax.experimental.pallas import tpu as pltpu
from jax.sharding import PartitionSpec as P

EPSILON = 1e-05
ROPE_BASE = 1000000.0
MESH = pl.DeviceIdType.MESH
F32 = jnp.float32
BF16 = jnp.bfloat16
RELS = ("L", "R", "X", "O", "OL", "OR", "OX")
VMEM_LIMIT = 56 << 20


def params(cid):
    return pltpu.CompilerParams(
        collective_id=cid, has_side_effects=True, vmem_limit_bytes=VMEM_LIMIT
    )


def rel_index(axis, rel):
    me = lax.axis_index(axis)
    core = 0
    if axis == "ctx":
        core = lax.rem(me, 2)
        me = me // 2
    pos = lax.rem(me, 4)
    row = me // 4
    step = {"L": 3, "R": 1, "X": 2, "M": 0}[rel[-1] if rel[-1] != "O" else "M"]
    if rel[0] == "O":
        row = 1 - row
    index = row * 4 + lax.rem(pos + step, 4)
    if axis == "ctx":
        index = index * 2 + core
    return index


def sibling():
    me = lax.axis_index("ctx")
    return me + 1 - 2 * lax.rem(me, 2)


def enter(axes, sib=False, extra=()):
    barrier = pltpu.get_barrier_semaphore()
    count = 0
    for axis in axes:
        for rel in ("L", "R", "O"):
            pl.semaphore_signal(
                barrier, inc=1, device_id={axis: rel_index(axis, rel)}, device_id_type=MESH
            )
            count += 1
    if sib:
        pl.semaphore_signal(barrier, inc=1, device_id={"ctx": sibling()}, device_id_type=MESH)
        count += 1
    pl.semaphore_wait(barrier, count)


def rcopy(src, dst, ssem, rsem, axis, index):
    return pltpu.make_async_remote_copy(
        src_ref=src,
        dst_ref=dst,
        send_sem=ssem,
        recv_sem=rsem,
        device_id={axis: index},
        device_id_type=MESH,
    )


class Gather:
    @staticmethod
    def scratch(K):
        return (pltpu.SemaphoreType.DMA((14 * K,)), pltpu.SemaphoreType.DMA((7, 2 * K)))

    def __init__(self, axis, dst, ssem, rsem, alt=()):
        self.axis, self.dst, self.ssem, self.rsem = axis, dst, ssem, rsem
        self.alt = alt
        self.index = {rel: rel_index(axis, rel) for rel in RELS + ("M",)}
        self.sent = []
        self.seen = set()

    def send(self, source, k, route, to, as_rel):
        view = self.dst(self.index[source], k, route)
        copy = rcopy(
            view,
            view,
            self.ssem.at[len(self.sent)],
            self.rsem.at[RELS.index(as_rel), 2 * k + route],
            self.axis,
            self.index[to],
        )
        copy.start()
        self.sent.append(copy)

    def arrive(self, rel, k, route):
        if (rel, k, route) in self.seen:
            return
        self.seen.add((rel, k, route))
        view = self.dst(self.index[rel], k, route)
        rcopy(
            view,
            view,
            self.ssem.at[0],
            self.rsem.at[RELS.index(rel), 2 * k + route],
            self.axis,
            self.index["L"],
        ).wait_recv()

    def start(self, k):
        self.send("M", k, 0, "R", "L")
        self.send("M", k, 1, "L", "R")
        self.send("M", k, 0, "O", "O")
        self.send("M", k, 1, "O", "O")
        self.send("M", k, 0, "L", "R")
        self.send("M", k, 1, "R", "L")

    def relay_row(self, k):
        self.arrive("L", k, 0)
        self.send("L", k, 0, "R", "X")
        self.arrive("R", k, 1)
        self.send("R", k, 1, "L", "X")

    def relay_opposite(self, k):
        if k in self.alt:
            for first, second in ((0, 1), (1, 0)):
                for rel, route in (("L", first), ("R", second)):
                    self.arrive(rel, k, route)
                    self.send(rel, k, route, "O", "O" + rel)
            return
        self.arrive("O", k, 0)
        self.send("O", k, 0, "R", "OL")
        self.arrive("O", k, 1)
        self.send("O", k, 1, "L", "OR")
        self.send("O", k, 0, "L", "OR")
        self.send("O", k, 1, "R", "OL")

    def relay_last(self, k):
        if k in self.alt:
            for route in range(2):
                self.arrive("X", k, route)
                self.send("X", k, route, "O", "OX")
            return
        self.arrive("OL", k, 0)
        self.send("OL", k, 0, "R", "OX")
        self.arrive("OR", k, 1)
        self.send("OR", k, 1, "L", "OX")

    def finish(self, k):
        for rel in RELS:
            for route in range(2):
                self.arrive(rel, k, route)

    def drain(self):
        for copy in self.sent:
            copy.wait_send()


class Scatter:
    @staticmethod
    def scratch(K, piece):
        return (
            pltpu.VMEM((2, K, 2) + piece, BF16),
            pltpu.VMEM((2, K, 2) + piece, BF16),
            pltpu.VMEM((2, 2, K, 2) + piece, BF16),
            pltpu.VMEM((2, K, 2) + piece, BF16),
            pltpu.SemaphoreType.DMA((14 * K,)),
            pltpu.SemaphoreType.DMA((14 * K,)),
        )

    def __init__(self, axis, K, part, relay, stage, arrived, across, ssem, rsem, alt=()):
        self.axis, self.K, self.part, self.alt = axis, K, part, alt
        self.relay, self.stage, self.arrived, self.across = relay, stage, arrived, across
        self.ssem, self.rsem = ssem, rsem
        self.index = {rel: rel_index(axis, rel) for rel in RELS + ("M",)}
        self.sent = []

    def far(self, rel, k, route):
        if rel == "M":
            return self.across.at[1, k, route], self.across_slot(k, route)
        if rel == "L":
            return self.relay.at[1, k, route], self.relay_slot(1, k, route)
        d = ("R", "X").index(rel)
        return self.arrived.at[1, d, k, route], self.arrived_slot(1, d, k, route)

    def block(self, t, rel, k, route):
        if k in self.alt and t == 0 and rel != "M":
            return self.far(rel, k, route)[0]
        name = rel if t == 0 else ("O" if rel == "M" else "O" + rel)
        return self.part(self.index[name], k, route)

    def relay_slot(self, t, k, route):
        return (t * self.K + k) * 2 + route

    def arrived_slot(self, t, d, k, route):
        return 4 * self.K + ((t * 2 + d) * self.K + k) * 2 + route

    def across_slot(self, k, route):
        return 12 * self.K + 2 * k + route

    def send(self, src, dst, rslot, to):
        copy = rcopy(
            src, dst, self.ssem.at[len(self.sent)], self.rsem.at[rslot], self.axis, self.index[to]
        )
        copy.start()
        self.sent.append(copy)

    def arrive(self, dst, rslot):
        rcopy(dst, dst, self.ssem.at[0], self.rsem.at[rslot], self.axis, self.index["L"]).wait_recv()

    def start(self, t, k):
        if k in self.alt:
            if t == 1:
                for rel in ("X", "R", "L", "M"):
                    for route in range(2):
                        self.send(self.block(1, rel, k, route), *self.far(rel, k, route), "O")
            return
        self.ring(t, k)

    def ring(self, t, k):
        for route, to in ((0, "R"), (1, "L")):
            self.send(
                self.block(t, "X", k, route),
                self.relay.at[t, k, route],
                self.relay_slot(t, k, route),
                to,
            )
        for d, route, to in ((0, 1, "R"), (1, 0, "L")):
            self.send(
                self.block(t, to, k, route),
                self.arrived.at[t, d, k, route],
                self.arrived_slot(t, d, k, route),
                to,
            )

    def middle(self, t, k):
        if k in self.alt and t == 1:
            for rel in ("X", "R", "L"):
                for route in range(2):
                    share, slot = self.far(rel, k, route)
                    self.arrive(share, slot)
                    mine = self.part(self.index[rel], k, route)[...].astype(F32)
                    share[...] = (mine + share[...].astype(F32)).astype(BF16)
            self.ring(0, k)
            return
        for route, to in ((0, "R"), (1, "L")):
            self.arrive(self.relay.at[t, k, route], self.relay_slot(t, k, route))
            total = self.block(t, to, k, route)[...].astype(F32)
            total += self.relay[t, k, route].astype(F32)
            self.stage[t, k, route] = total.astype(BF16)
            self.send(
                self.stage.at[t, k, route],
                self.arrived.at[t, route, k, route],
                self.arrived_slot(t, route, k, route),
                to,
            )

    def row_sum(self, t, k, route):
        for d in range(2):
            self.arrive(self.arrived.at[t, d, k, route], self.arrived_slot(t, d, k, route))
        return (
            self.block(t, "M", k, route)[...].astype(F32)
            + self.arrived[t, 0, k, route].astype(F32)
            + self.arrived[t, 1, k, route].astype(F32)
        )

    def cross(self, k):
        if k in self.alt:
            return
        for route in range(2):
            self.across[0, k, route] = self.row_sum(1, k, route).astype(BF16)
            self.send(
                self.across.at[0, k, route],
                self.across.at[1, k, route],
                self.across_slot(k, route),
                "O",
            )

    def result(self, k, route):
        total = self.row_sum(0, k, route)
        self.arrive(self.across.at[1, k, route], self.across_slot(k, route))
        return total + self.across[1, k, route].astype(F32)

    def drain(self):
        for copy in self.sent:
            copy.wait_send()


def take(refs, count):
    return refs[:count], refs[count:]


def lane_iota(shape):
    return lax.broadcasted_iota(jnp.int32, shape, len(shape) - 1)


def dot_nt(a, b):
    return lax.dot_general(a, b, (((1,), (1,)), ((), ())), preferred_element_type=F32)


def dot_tn(a, b):
    return lax.dot_general(a, b, (((0,), (0,)), ((), ())), preferred_element_type=F32)


def dot(a, b):
    return jnp.dot(a, b, preferred_element_type=F32)


def head_sums(values, low):
    zero = jnp.zeros_like(values)
    first = jnp.sum(jnp.where(low, values, zero), axis=-1, keepdims=True)
    second = jnp.sum(jnp.where(low, zero, values), axis=-1, keepdims=True)
    return first, second


def swap_halves(values, first_half):
    return jnp.where(first_half, pltpu.roll(values, 96, 1), pltpu.roll(values, 32, 1))


def rms_scale(values):
    return lax.rsqrt(jnp.mean(values * values, axis=-1, keepdims=True) + EPSILON)


def norm_back(gradient, normed, scale_rows, gain_vec):
    scaled = gradient * gain_vec
    return scale_rows * (scaled - normed * jnp.mean(scaled * normed, axis=-1, keepdims=True))


def rows_of(index):
    return pl.ds(pl.multiple_of(index * 16, 16), 16)


def mp_rows(ref):
    return lambda i, k, route: ref.at[k, route, rows_of(i), :]


def kv_rows(ref):
    return lambda i, k, route: ref.at[k, i * 2 + route]


def forward_copy(view, ssem, rsem):
    copy = rcopy(view, view, ssem, rsem, "ctx", sibling())
    copy.start()
    return copy


def head_gains(query_gain, key_gain):
    q, k = query_gain[...], key_gain[...]
    return jnp.concatenate([q, q], axis=1), jnp.concatenate([k, jnp.ones_like(k)], axis=1)


def qkv_kernel(
    block_map, x, gain1, w, query_gain, key_gain, positions, frequency,
    full, cosine, sine, raw, queries, kv_all, *sems,
):
    mp = lax.axis_index("mp")
    ctx = lax.axis_index("ctx")
    enter(("mp", "ctx"), sib=True)
    (s1, r1, s2, r2), (s4, r4) = take(sems, 4)
    gain_q, gain_k = head_gains(query_gain, key_gain)
    first = Gather("mp", mp_rows(full), s1, r1, alt=(0, 2))
    keys = Gather("ctx", kv_rows(kv_all), s2, r2)
    for s in range(4):
        t = x[s].astype(F32)
        full[s, :, rows_of(mp), :] = (t * rms_scale(t) * gain1[...]).astype(BF16)
        first.start(s)
    lane = lane_iota((256, 128))
    low = lane < 64
    first_half = lax.rem(lane, 64) < 32
    sign = jnp.where(first_half[0:128], -1.0, 1.0)
    for t in range(2):
        chosen = lax.broadcasted_iota(jnp.int32, (32, 128), 0) == block_map[ctx * 2 + t]
        for s in range(4):
            row = jnp.where(chosen, positions[s].astype(F32), 0.0)
            row = jnp.sum(row, axis=0, keepdims=True)
            angle = jnp.broadcast_to(row, (128, 128)).T * frequency[...]
            cosine[s, t * 128 : t * 128 + 128] = jnp.cos(angle)
            sine[s, t * 128 : t * 128 + 128] = jnp.sin(angle) * sign
    forwards = []

    def forward(rel, s):
        slot = (("M",) + RELS).index(rel)
        view = kv_all.at[s, pl.ds(keys.index[rel] * 2, 2)]
        forwards.append(forward_copy(view, s4.at[slot, s], r4.at[slot, s]))

    def project(s):
        y = dot(full[s].reshape(256, 1024), w[...])
        raw[s] = y
        a, b = y[:, :128], y[:, 128:]
        cos, sin = cosine[s], sine[s]
        lo, _ = head_sums(b * b, low)
        g = b * lax.rsqrt(lo * (1 / 64) + EPSILON) * gain_k
        turned = g * cos + swap_halves(g, first_half) * sin
        packed = jnp.where(low, turned, b).astype(BF16)
        kv_all[s, pl.ds(ctx * 2, 2)] = packed.reshape(2, 128, 128)
        keys.start(s)
        forward("M", s)
        lo, hi = head_sums(a * a, low)
        scale = jnp.where(
            low, lax.rsqrt(lo * (1 / 64) + EPSILON), lax.rsqrt(hi * (1 / 64) + EPSILON)
        )
        g = a * scale * gain_q
        turned = g * cos + swap_halves(g, first_half) * sin
        zero = jnp.zeros_like(turned)
        head0 = jnp.where(low, turned, zero).astype(BF16)
        head1 = jnp.where(low, pltpu.roll(turned, 64, 1), zero).astype(BF16)
        for t in range(2):
            queries[s, t, 0:128] = head0[t * 128 : t * 128 + 128]
            queries[s, t, 128:256] = head1[t * 128 : t * 128 + 128]

    def at(k, *steps):
        if 0 <= k < 4:
            for step in steps:
                step(k)

    def finish_keys(s):
        for rel in RELS:
            for route in range(2):
                keys.arrive(rel, s, route)
            forward(rel, s)

    for step in range(4 + 6):
        at(step, first.relay_row, first.relay_opposite)
        at(step - 1, first.relay_last)
        at(step - 2, first.finish, project)
        at(step - 3, keys.relay_row, keys.relay_opposite)
        at(step - 4, keys.relay_last)
        at(step - 5, finish_keys)
    first.drain()
    keys.drain()
    for copy in forwards:
        copy.wait_send()
    for s in range(4):
        for slot, rel in enumerate(("M",) + RELS):
            view = kv_all.at[s, pl.ds((keys.index[rel] + sibling() - ctx) * 2, 2)]
            rcopy(view, view, s4.at[slot, s], r4.at[slot, s], "ctx", sibling()).wait_recv()


def attention_kernel(block_map, queries, kv_all, low_out, high_out, logs, where, acc):
    me = lax.axis_index("ctx")
    for slot in range(32):
        where[block_map[slot]] = slot
    lane_k = lane_iota((256, 128)) < 64
    for j in range(2):
        mine = block_map[2 * me + j]
        acc[...] = jnp.zeros_like(acc)

        def step(i, masked):
            slot0, slot1 = where[2 * i], where[2 * i + 1]
            if masked:
                row = lax.rem(lax.broadcasted_iota(jnp.int32, (256, 256), 0), 128)
                col = lax.broadcasted_iota(jnp.int32, (256, 256), 1)
                keep = col + 256 * i <= row + 128 * mine
            for s in range(4):
                kv = jnp.concatenate([kv_all[s, slot0], kv_all[s, slot1]], axis=0)
                weights = jnp.exp(dot_nt(queries[s, j], kv) * 0.125)
                if masked:
                    weights = jnp.where(keep, weights, 0.0)
                ones = jnp.where(lane_k, jnp.ones_like(kv), kv)
                acc[s] += dot(weights.astype(BF16), ones)

        last = mine // 2
        lax.fori_loop(0, last, lambda i, c: (step(i, False), c)[1], 0)
        step(last, True)
        low = lane_iota((128, 128)) < 64
        for s in range(4):
            a = acc[s]
            o = a * pltpu.roll(1.0 / a, 64, 1)
            both = jnp.where(low, pltpu.roll(o[0:128], 64, 1), o[128:256])
            low_out[s, j] = both.astype(BF16)
            high_out[s, j] = both
            logs[s, j] = jnp.log(a.T[0:8])


def attention_back_kernel(
    block_map, queries, kv_all, grad_out, out, logs,
    grad_q, grad_kv, where, acc, grad_pad, turned, delta,
):
    me = lax.axis_index("ctx")
    for slot in range(32):
        where[block_map[slot]] = slot
    acc[...] = jnp.zeros_like(acc)
    low = lane_iota((128, 128)) < 64
    for j in range(2):
        mine = block_map[2 * me + j]
        turned[...] = jnp.zeros_like(turned)
        for s in range(4):
            g = grad_out[s, j]
            gf = g.astype(F32)
            zero = jnp.zeros_like(gf)
            grad_pad[s, 0:128] = jnp.where(low, zero, pltpu.roll(gf, 64, 1)).astype(BF16)
            grad_pad[s, 128:256] = jnp.where(low, zero, gf).astype(BF16)
            product = (gf * out[s, j]).T
            delta[s, :, 0:128] = jnp.broadcast_to(
                jnp.sum(product[0:64], axis=0, keepdims=True), (8, 128)
            )
            delta[s, :, 128:256] = jnp.broadcast_to(
                jnp.sum(product[64:128], axis=0, keepdims=True), (8, 128)
            )

        def step(i, masked):
            slot0, slot1 = where[2 * i], where[2 * i + 1]
            if masked:
                col = lax.rem(lax.broadcasted_iota(jnp.int32, (256, 256), 1), 128)
                row = lax.broadcasted_iota(jnp.int32, (256, 256), 0)
                keep = row + 256 * i <= col + 128 * mine
            for s in range(4):
                kv = jnp.concatenate([kv_all[s, slot0], kv_all[s, slot1]], axis=0)
                q, g = queries[s, j], grad_pad[s]
                probs = jnp.exp(dot_nt(kv, q) * 0.125 - logs[s, j, 0:1])
                if masked:
                    probs = jnp.where(keep, probs, 0.0)
                scores = (probs * (dot_nt(kv, g) - delta[s, 0:1])).astype(BF16)
                turned[s] += dot_tn(kv, scores)
                block = dot(
                    jnp.concatenate([scores, probs.astype(BF16)], axis=1),
                    jnp.concatenate([q, g], axis=0),
                )
                acc[s, slot0] += block[0:128]
                acc[s, slot1] += block[128:256]

        last = mine // 2
        lax.fori_loop(0, last, lambda i, c: (step(i, False), c)[1], 0)
        step(last, True)
        for s in range(4):
            t = turned[s].T * 0.125
            grad_q[s, j] = jnp.where(low, t[0:128], pltpu.roll(t[128:256], 64, 1))
    scale = jnp.where(low, 0.125, 1.0)

    def finish(n, c):
        for s in range(4):
            grad_kv[s, n] = (acc[s, n] * scale).astype(BF16)
        return c

    lax.fori_loop(0, 32, finish, 0)


class Reduce:
    @staticmethod
    def scratch(A, R):
        return (
            pltpu.VMEM((A, R, 512), BF16),
            pltpu.VMEM((A, R, 512), BF16),
            pltpu.SemaphoreType.DMA((2,)),
            pltpu.SemaphoreType.DMA((2,)),
        ) + Scatter.scratch(1, (A, R // 4, 128))

    def __init__(self, source, got, pair, ssem, rsem, *rest):
        self.source, self.got, self.pair = source, got, pair
        self.ssem, self.rsem = ssem, rsem
        self.rows = source.shape[1] // 4
        self.sum = Scatter("ctx", 1, self.piece, *rest)

    def piece(self, i, k, route):
        row = pl.multiple_of(lax.rem(i // 2, 4) * self.rows, 16)
        column = pl.multiple_of((i // 8) * 256 + route * 128, 128)
        return self.pair.at[:, pl.ds(row, self.rows), pl.ds(column, 128)]

    def columns(self, y, core):
        return pl.ds(pl.multiple_of((2 * y + core) * 256, 256), 256)

    def exchange(self):
        core = lax.rem(lax.axis_index("ctx"), 2)
        self.copies = []
        for y in range(2):
            copy = rcopy(
                self.source.at[:, :, self.columns(y, 1 - core)],
                self.got.at[:, :, y * 256 : y * 256 + 256],
                self.ssem.at[y],
                self.rsem.at[y],
                "ctx",
                sibling(),
            )
            copy.start()
            self.copies.append(copy)

    def start(self):
        core = lax.rem(lax.axis_index("ctx"), 2)
        for y in range(2):
            self.copies[y].wait_recv()
            columns = slice(y * 256, y * 256 + 256)
            mine = self.source[:, :, self.columns(y, core)].astype(F32)
            self.pair[:, :, columns] = (mine + self.got[:, :, columns].astype(F32)).astype(BF16)
        self.sum.start(1, 0)
        self.sum.start(0, 0)

    def result(self, store):
        for route in range(2):
            store(route, self.sum.result(0, route).astype(BF16))

    def drain(self):
        for copy in self.copies:
            copy.wait_send()
        self.sum.drain()


class Spread:
    @staticmethod
    def scratch():
        return Gather.scratch(1) + (pltpu.SemaphoreType.DMA((8,)), pltpu.SemaphoreType.DMA((8,)))

    def __init__(self, target, ssem, rsem, fs, fr):
        self.target, self.fs, self.fr = target, fs, fr
        self.rows = target.shape[1] // 4
        self.gather = Gather("ctx", self.piece, ssem, rsem)
        self.forwards = []

    def view(self, i, shift, width):
        row = pl.multiple_of(lax.rem(i // 2, 4) * self.rows, 16)
        column = pl.multiple_of((2 * (i // 8) + lax.rem(i, 2)) * 256 + shift, 128)
        return self.target.at[:, pl.ds(row, self.rows), pl.ds(column, width)]

    def piece(self, i, k, route):
        return self.view(i, route * 128, 128)

    def own(self):
        return self.view(lax.axis_index("ctx"), 0, 256)

    def forward(self, rel):
        slot = len(self.forwards)
        view = self.view(self.gather.index[rel], 0, 256)
        self.forwards.append(forward_copy(view, self.fs.at[slot], self.fr.at[slot]))

    def start(self):
        self.gather.start(0)
        self.forward("M")

    def finish(self):
        for rel in RELS:
            for route in range(2):
                self.gather.arrive(rel, 0, route)
            self.forward(rel)

    def drain(self):
        self.gather.drain()
        ctx = lax.axis_index("ctx")
        for slot, rel in enumerate(("M",) + RELS):
            self.forwards[slot].wait_send()
            view = self.view(self.gather.index[rel] + sibling() - ctx, 0, 256)
            rcopy(view, view, self.fs.at[slot], self.fr.at[slot], "ctx", sibling()).wait_recv()


def middle_kernel(
    x, attended, w, gain2, cot, cot_full, gate_up, down,
    mixed, d_mixed, part_o, d_att, gain_part, out_part, ffn_own,
    part, full, part_d, branch, turned, grads, *scratch,
):
    mp = lax.axis_index("mp")
    enter(("mp", "ctx"), sib=True)
    sums1, rest = take(scratch, 6)
    sums2, rest = take(rest, 6)
    (s1, r1, s2, r2), sums3 = take(rest, 4)
    rs1 = Scatter("mp", 4, mp_rows(part), *sums1, alt=(3,))
    rs2 = Scatter("mp", 4, mp_rows(part_d), *sums2, alt=(3,))
    ag2 = Gather("mp", mp_rows(full), s1, r1, alt=(0, 2))
    ag3 = Gather("mp", mp_rows(branch), s2, r2, alt=(0,))
    reduce = Reduce(grads, *sums3)

    def mix(k):
        for t in range(2):
            m = x[k, t].astype(F32) + rs1.result(k, t)
            mixed[k, t] = m
            full[k, t, rows_of(mp), :] = (m * rms_scale(m) * gain2[...]).astype(BF16)
        ag2.start(k)

    def feed(k):
        rows = full[k].reshape(256, 1024)
        columns = slice(k * 256, k * 256 + 256)
        gate = dot_nt(rows, gate_up[0])
        up = dot_nt(rows, gate_up[1])
        sig = 1.0 / (1.0 + jnp.exp(-gate))
        d_active = dot_nt(cot_full[k].reshape(256, 1024), down[...])
        d_gate = (d_active * up * sig * (1.0 + gate * (1.0 - sig))).astype(BF16)
        d_up = (d_active * gate * sig).astype(BF16)
        both = dot(d_gate, gate_up[0]) + dot(d_up, gate_up[1])
        part_d[k] = both.astype(BF16).reshape(2, 128, 1024)
        rs2.start(1, k)
        rs2.start(0, k)
        active = (gate * sig * up).astype(BF16)
        part_o[k] = dot(active, down[...]).astype(BF16).reshape(2, 128, 1024)
        turned[0, :, columns] = d_gate.T
        turned[1, :, columns] = d_up.T
        turned[2, :, columns] = active.T

    def weigh():
        def tile(n, c):
            columns = pl.ds(pl.multiple_of(n * 256, 256), 256)
            rows = full[:, :, :, columns].reshape(1024, 256)
            for i in range(2):
                grads[i, :, columns] = dot(turned[i], rows).astype(BF16)
            rows = cot_full[:, :, :, columns].reshape(1024, 256)
            grads[2, :, columns] = dot(turned[2], rows).astype(BF16)
            return c

        lax.fori_loop(0, 4, tile, 0)

    gain_part[...] = jnp.zeros_like(gain_part)

    def back(k):
        for t in range(2):
            g = rs2.result(k, t)
            m = mixed[k, t]
            scale = rms_scale(m)
            normed = m * scale
            gain_part[...] += jnp.sum(g * normed, axis=0, keepdims=True)
            dm = cot[k, t].astype(F32) + norm_back(g, normed, scale, gain2[...])
            d_mixed[k, t] = dm
            branch[k, t, rows_of(mp), :] = dm.astype(BF16)
        ag3.start(k)

    def attend(k):
        rows = branch[k].reshape(256, 1024)
        d_att[k] = dot_nt(rows, w[...]).astype(BF16).reshape(2, 128, 128)

    def at(k, *steps):
        if 0 <= k < 4:
            for step in steps:
                step(k)

    for k in range(4):
        part[k] = dot(attended[k].reshape(256, 128), w[...]).astype(BF16).reshape(2, 128, 1024)
        rs1.start(1, k)
        rs1.start(0, k)
    for step in range(4 + 11):
        at(step, lambda k: rs1.middle(1, k))
        at(step - 1, rs1.cross, lambda k: rs1.middle(0, k))
        at(step - 2, mix)
        at(step - 3, ag2.relay_row, ag2.relay_opposite)
        at(step - 4, ag2.relay_last)
        at(step - 5, ag2.finish, feed)
        if step == 8:
            weigh()
            reduce.exchange()
        at(step - 6, lambda k: rs2.middle(1, k))
        at(step - 7, rs2.cross, lambda k: rs2.middle(0, k))
        if step == 9:
            reduce.start()
        at(step - 8, back)
        if step == 10:
            reduce.sum.middle(1, 0)
        if step == 11:
            reduce.sum.cross(0)
            reduce.sum.middle(0, 0)
        at(step - 9, ag3.relay_row, ag3.relay_opposite)
        at(step - 10, ag3.relay_last)
        at(step - 11, ag3.finish, attend)
    rows = attended[...].reshape(1024, 128).T
    for n in range(4):
        columns = slice(n * 256, n * 256 + 256)
        out_part[:, columns] = dot(rows, branch[:, :, :, columns].reshape(1024, 256)).astype(BF16)

    def store(route, value):
        ffn_own[:, :, route * 128 : route * 128 + 128] = value

    reduce.result(store)
    for item in (rs1, ag2, rs2, ag3, reduce):
        item.drain()


def last_kernel(
    grad_kv, grad_q, raw, cosine, sine, query_gain, key_gain, w, x, gain1, d_mixed,
    mixed, part_o, full, out_part, gain2_part,
    out, in_grad, attn_sum, total,
    pair, got, d_qkv, part, grads, gain_row, small, by_mp, by_ctx, *scratch,
):
    ctx = lax.axis_index("ctx")
    mp = lax.axis_index("mp")
    barrier = pltpu.get_barrier_semaphore()
    for axis, size in (("mp", 8), ("ctx", 16)):
        me = lax.axis_index(axis)
        for n in range(1, size):
            pl.semaphore_signal(
                barrier, inc=1, device_id={axis: lax.rem(me + n, size)}, device_id_type=MESH
            )
    pl.semaphore_wait(barrier, 22)
    sums_k, rest = take(scratch, 6)
    sums_o, rest = take(rest, 6)
    sums_n, rest = take(rest, 6)
    sums_a, rest = take(rest, 10)
    spread_a, rest = take(rest, 4)
    s1, r1, s2, r2, s3, r3 = rest
    core = lax.rem(ctx, 2)
    sib = sibling()
    copies = []
    for s in range(4):
        for chip in range(8):
            src = grad_kv.at[s, pl.ds(chip * 4 + (1 - core) * 2, 2)]
            copy = rcopy(
                src, got.at[s, pl.ds(chip * 2, 2)], s1.at[s, chip], r1.at[s, chip], "ctx", sib
            )
            copy.start()
            copies.append(copy)
    rs_k = Scatter("ctx", 4, lambda i, k, route: pair.at[k, (i // 2) * 2 + route], *sums_k)
    rs_o = Scatter("mp", 4, mp_rows(part_o), *sums_o)
    rs_n = Scatter("mp", 4, mp_rows(part), *sums_n, alt=(3,))
    reduce = Reduce(grads, *sums_a)
    attn = Spread(attn_sum, *spread_a)
    for s in range(4):
        rs_o.start(1, s)
        rs_o.start(0, s)
        for chip in range(8):
            copies[s * 8 + chip].wait_recv()
            mine = grad_kv[s, pl.ds(chip * 4 + core * 2, 2)].astype(F32)
            both = mine + got[s, chip * 2 : chip * 2 + 2].astype(F32)
            pair[s, chip * 2 : chip * 2 + 2] = both.astype(BF16)
        rs_k.start(1, s)
        rs_k.start(0, s)
    grads[0, 256:384, :] = out_part[...]
    lane = lane_iota((256, 128))
    low = lane < 64
    first_half = lax.rem(lane, 64) < 32
    inv = 1 / 64
    small[...] = jnp.zeros_like(small)
    gain_row[...] = jnp.zeros_like(gain_row)
    for n in range(8):
        small[8 + n : 9 + n, :] = gain2_part[:, n * 128 : n * 128 + 128]
    gain_q, gain_k = head_gains(query_gain, key_gain)

    def project(s):
        y = raw[s]
        a, b = y[:, :128], y[:, 128:]
        cos, sin = cosine[s], sine[s]
        lo, hi = head_sums(a * a, low)
        scale = jnp.where(low, lax.rsqrt(lo * inv + EPSILON), lax.rsqrt(hi * inv + EPSILON))
        n = a * scale
        d = grad_q[s].reshape(256, 128)
        g = d * cos - swap_halves(d, first_half) * sin
        small[16:17, :] += jnp.sum(g * n, axis=0, keepdims=True)
        e = g * gain_q
        lo, hi = head_sums(e * n, low)
        dq = scale * (e - n * jnp.where(low, lo * inv, hi * inv))
        d_qkv[s, :, 0:128] = dq.astype(BF16)
        lo, _ = head_sums(b * b, low)
        scale = lax.rsqrt(lo * inv + EPSILON)
        n = b * scale
        d = jnp.concatenate([rs_k.result(s, 0), rs_k.result(s, 1)], axis=0)
        g = d * cos - swap_halves(d, first_half) * sin
        small[17:18, :] += jnp.sum(g * n, axis=0, keepdims=True)
        e = g * gain_k
        lo, _ = head_sums(e * n, low)
        dk = scale * (e - n * (lo * inv))
        d_qkv[s, :, 128:256] = jnp.where(low, dk, d).astype(BF16)
        part[s] = dot_nt(d_qkv[s], w[...]).astype(BF16).reshape(2, 128, 1024)
        rs_n.start(1, s)
        rs_n.start(0, s)

    def write_out(s):
        for t in range(2):
            out[s, t] = (mixed[s, t] + rs_o.result(s, t)).astype(BF16)

    def weigh():
        rows = d_qkv[...].reshape(1024, 256).T
        for n in range(4):
            columns = slice(n * 256, n * 256 + 256)
            value = dot(rows, full[:, :, :, columns].reshape(1024, 256))
            grads[0, 0:256, columns] = value.astype(BF16)

    def write_grad(s):
        for t in range(2):
            g = rs_n.result(s, t)
            v = x[s, t].astype(F32)
            scale = rms_scale(v)
            normed = v * scale
            gain_row[...] += jnp.sum(g * normed, axis=0, keepdims=True)
            in_grad[s, t] = (d_mixed[s, t] + norm_back(g, normed, scale, gain1[...])).astype(BF16)

    def at(k, *steps):
        if 0 <= k < 4:
            for step in steps:
                step(k)

    def store(route, value):
        attn.piece(ctx, 0, route)[...] = value

    for step in range(4 + 3):
        at(step, lambda k: rs_k.middle(1, k), lambda k: rs_o.middle(1, k))
        at(step - 1, rs_k.cross, lambda k: rs_k.middle(0, k))
        at(step - 1, rs_o.cross, lambda k: rs_o.middle(0, k))
        at(step - 2, project)
        if step == 5:
            weigh()
            reduce.exchange()
        at(step - 3, lambda k: rs_n.middle(1, k))
    reduce.start()
    for k in range(4):
        rs_n.cross(k)
        rs_n.middle(0, k)
    for k in range(4):
        write_out(k)
    reduce.sum.middle(1, 0)
    reduce.sum.cross(0)
    reduce.sum.middle(0, 0)
    write_grad(0)
    write_grad(1)
    reduce.result(store)
    attn.start()
    write_grad(2)
    write_grad(3)
    for n in range(8):
        small[n : n + 1, :] = gain_row[:, n * 128 : n * 128 + 128]
    copies2 = []
    for n in range(1, 8):
        copy = rcopy(small, by_mp.at[n], s2.at[n], r2.at[n], "mp", lax.rem(mp + n, 8))
        copy.start()
        copies2.append(copy)
    attn.gather.relay_row(0)
    attn.gather.relay_opposite(0)
    by_mp[0] = small[...]
    for copy in copies2:
        copy.wait()
    by_ctx[0] = jnp.sum(by_mp[...], axis=0)
    copies3 = []
    for n in range(1, 16):
        copy = rcopy(
            by_ctx.at[0], by_ctx.at[n], s3.at[n], r3.at[n], "ctx", lax.rem(ctx + n, 16)
        )
        copy.start()
        copies3.append(copy)
    attn.gather.relay_last(0)
    attn.finish()
    for copy in copies3:
        copy.wait()
    total[...] = jnp.zeros_like(total)

    def add(i, c):
        total[...] += by_ctx[lax.rem(ctx - i + 16, 16)]
        return c

    lax.fori_loop(0, 16, add, 0)
    for copy in copies:
        copy.wait_send()
    for item in (rs_k, rs_o, rs_n, reduce, attn):
        item.drain()


def widen_kernel(ffn_all, attn_sum, gate_up_grad, down_grad, qkv_grad, out_grad):
    step = pl.program_id(0)

    def widen(target):
        for y in range(2):
            for core in range(2):
                start = (2 * y + core) * 256
                target[:, start : start + 256] = ffn_all[y, 0, core, 0].astype(F32)

    @pl.when(step == 0)
    def _():
        qkv_grad[...] = attn_sum[0, 0:256].astype(F32).T.reshape(1024, 1, 256)
        out_grad[...] = attn_sum[0, 256:384].astype(F32)

    @pl.when(step < 8)
    def _():
        widen(gate_up_grad.at[0])

    @pl.when(step >= 8)
    def _():
        widen(down_grad)


def vm(n):
    return [pl.BlockSpec(memory_space=pltpu.VMEM)] * n


def sds(shape, dtype):
    return jax.ShapeDtypeStruct(shape, dtype)


def local(
    residual_in,
    attn_norm,
    query_key_value_weight,
    query_gain,
    key_gain,
    out_weight,
    ffn_norm,
    gate_up,
    down_weight,
    cotangent,
    positions,
    block_map,
):
    rows_shape = (4, 2, 16, 1024)
    full_shape = (4, 2, 128, 1024)
    piece = (16, 1024)
    dma = pltpu.SemaphoreType.DMA

    inverse_freq = 1.0 / ROPE_BASE ** (np.arange(0, 64, 2) / 64)
    frequency = np.tile(inverse_freq, 4).reshape(1, 128).astype(np.float32)
    gain_q, gain_k = query_gain.reshape(1, 64), key_gain.reshape(1, 64)
    smem = [pl.BlockSpec(memory_space=pltpu.SMEM)]
    cot_full = lax.all_gather(cotangent, "mp", axis=2, tiled=True)
    gain1 = attn_norm.reshape(1, 1024)
    gain2 = ffn_norm.reshape(1, 1024)
    w_qkv = query_key_value_weight.reshape(1024, 256)

    full1, cosine, sine, raw, queries, kv_all = pl.pallas_call(
        qkv_kernel,
        out_shape=(
            sds(full_shape, BF16),
            sds((4, 256, 128), F32),
            sds((4, 256, 128), F32),
            sds((4, 256, 256), F32),
            sds((4, 2, 256, 128), BF16),
            sds((4, 32, 128, 128), BF16),
        ),
        in_specs=smem + vm(7),
        out_specs=tuple(vm(6)),
        scratch_shapes=Gather.scratch(4) * 2 + (dma((8, 4)), dma((8, 4))),
        compiler_params=params(1),
    )(block_map, residual_in, gain1, w_qkv, gain_q, gain_k, positions.reshape(4, 32, 128), frequency)

    attended, attended_high, logs = pl.pallas_call(
        attention_kernel,
        out_shape=(
            sds((4, 2, 128, 128), BF16),
            sds((4, 2, 128, 128), F32),
            sds((4, 2, 8, 256), F32),
        ),
        in_specs=smem + vm(2),
        out_specs=tuple(vm(3)),
        scratch_shapes=[pltpu.SMEM((32,), jnp.int32), pltpu.VMEM((4, 256, 128), F32)],
        compiler_params=pltpu.CompilerParams(vmem_limit_bytes=VMEM_LIMIT),
    )(block_map, queries, kv_all)

    gate_up_t = jnp.transpose(gate_up, (1, 2, 0))
    mixed, d_mixed, part_o, d_att, gain2_part, out_part, ffn_own = pl.pallas_call(
        middle_kernel,
        out_shape=(
            sds(rows_shape, F32),
            sds(rows_shape, F32),
            sds(full_shape, BF16),
            sds((4, 2, 128, 128), BF16),
            sds((1, 1024), F32),
            sds((128, 1024), BF16),
            sds((3, 144, 256), BF16),
        ),
        in_specs=vm(8),
        out_specs=tuple(vm(7)),
        scratch_shapes=(pltpu.VMEM(full_shape, BF16),) * 4
        + (pltpu.VMEM((3, 576, 1024), BF16),) * 2
        + Scatter.scratch(4, piece) * 2
        + Gather.scratch(4) * 2
        + Reduce.scratch(3, 576),
        compiler_params=params(2),
    )(
        residual_in, attended, out_weight, gain2, cotangent, cot_full, gate_up_t, down_weight
    )

    ffn_all = lax.all_gather(ffn_own, "ctx", axis=0).reshape(2, 4, 2, 3, 144, 256)

    grad_q, grad_kv = pl.pallas_call(
        attention_back_kernel,
        out_shape=(sds((4, 2, 128, 128), F32), sds((4, 32, 128, 128), BF16)),
        in_specs=smem + vm(5),
        out_specs=tuple(vm(2)),
        scratch_shapes=[
            pltpu.SMEM((32,), jnp.int32),
            pltpu.VMEM((4, 32, 128, 128), F32),
            pltpu.VMEM((4, 256, 128), BF16),
            pltpu.VMEM((4, 128, 256), F32),
            pltpu.VMEM((4, 8, 256), F32),
        ],
        compiler_params=pltpu.CompilerParams(vmem_limit_bytes=VMEM_LIMIT),
    )(block_map, queries, kv_all, d_att, attended_high, logs)

    output, input_grad, attn_sum, sums = pl.pallas_call(
        last_kernel,
        out_shape=(
            sds(rows_shape, BF16),
            sds(rows_shape, BF16),
            sds((1, 384, 1024), BF16),
            sds((24, 128), F32),
        ),
        in_specs=vm(16),
        out_specs=tuple(vm(4)),
        scratch_shapes=(
            pltpu.VMEM((4, 16, 128, 128), BF16),
            pltpu.VMEM((4, 16, 128, 128), BF16),
            pltpu.VMEM((4, 256, 256), BF16),
            pltpu.VMEM(full_shape, BF16),
            pltpu.VMEM((1, 384, 1024), BF16),
            pltpu.VMEM((1, 1024), F32),
            pltpu.VMEM((24, 128), F32),
            pltpu.VMEM((8, 24, 128), F32),
            pltpu.VMEM((16, 24, 128), F32),
        )
        + Scatter.scratch(4, (128, 128))
        + Scatter.scratch(4, piece) * 2
        + Reduce.scratch(1, 384)
        + Spread.scratch()
        + (dma((4, 8)), dma((4, 8)), dma((8,)), dma((8,)), dma((16,)), dma((16,))),
        compiler_params=params(3),
    )(
        grad_kv, grad_q, raw, cosine, sine, gain_q, gain_k, w_qkv, residual_in, gain1,
        d_mixed, mixed, part_o, full1, out_part, gain2_part,
    )

    gate_up_grad, down_grad, qkv_grad, out_grad = pl.pallas_call(
        widen_kernel,
        grid=(12,),
        out_shape=(
            sds((2, 576, 1024), F32),
            sds((576, 1024), F32),
            sds((1024, 1, 256), F32),
            sds((128, 1024), F32),
        ),
        in_specs=[
            pl.BlockSpec((2, 1, 2, 1, 144, 256), lambda i: (0, i % 4, 0, i // 4, 0, 0)),
            pl.BlockSpec((1, 384, 1024), lambda i: (0, 0, 0)),
        ],
        out_specs=(
            pl.BlockSpec((1, 144, 1024), lambda i: (jnp.minimum(i, 7) // 4, jnp.minimum(i, 7) % 4, 0)),
            pl.BlockSpec((144, 1024), lambda i: (jnp.maximum(i - 8, 0), 0)),
            pl.BlockSpec((1024, 1, 256), lambda i: (0, 0, 0)),
            pl.BlockSpec((128, 1024), lambda i: (0, 0)),
        ),
        compiler_params=pltpu.CompilerParams(vmem_limit_bytes=VMEM_LIMIT),
    )(ffn_all, attn_sum)

    return (
        output,
        input_grad,
        sums[0:8].reshape(1024),
        qkv_grad,
        sums[16, :64] + sums[16, 64:128],
        sums[17, :64],
        out_grad,
        sums[8:16].reshape(1024),
        jnp.transpose(gate_up_grad, (2, 0, 1)),
        down_grad,
    )


def solution(mesh):
    return jax.shard_map(
        local,
        mesh=mesh,
        in_specs=(
            P(None, "ctx", "mp", None),
            P(),
            P(None, "mp", None),
            P(),
            P(),
            P("mp", None),
            P(),
            P(None, None, "mp"),
            P("mp", None),
            P(None, "ctx", "mp", None),
            P(),
            P(),
        ),
        out_specs=(
            P(None, "ctx", "mp", None),
            P(None, "ctx", "mp", None),
            P(),
            P(None, "mp", None),
            P(),
            P(),
            P("mp", None),
            P(),
            P(None, None, "mp"),
            P("mp", None),
        ),
        check_vma=False,
    )
```

```python
import functools
import math

import jax
import jax.numpy as jnp
import numpy as np
from jax import lax
from jax.experimental import pallas as pl
from jax.experimental.pallas import tpu as pltpu
from jax.sharding import PartitionSpec as P

EPSILON = 1e-05
ROPE_BASE = 1000000.0
EXPONENT_SCALE = 0.125 * math.log2(math.e)
MESH = pl.DeviceIdType.MESH
F32 = jnp.float32
BF16 = jnp.bfloat16
RELS = ("L", "R", "X", "O", "OL", "OR", "OX")
VMEM_LIMIT = 56 << 20


def params(cid):
    return pltpu.CompilerParams(
        collective_id=cid, has_side_effects=True, vmem_limit_bytes=VMEM_LIMIT
    )


def rel_index(axis, rel):
    me = lax.axis_index(axis)
    core = 0
    if axis == "ctx":
        core = lax.rem(me, 2)
        me = me // 2
    pos = lax.rem(me, 4)
    row = me // 4
    step = {"L": 3, "R": 1, "X": 2, "M": 0}[rel[-1] if rel[-1] != "O" else "M"]
    if rel[0] == "O":
        row = 1 - row
    index = row * 4 + lax.rem(pos + step, 4)
    if axis == "ctx":
        index = index * 2 + core
    return index


def sibling():
    me = lax.axis_index("ctx")
    return me + 1 - 2 * lax.rem(me, 2)


def enter(axes, sib=False, extra=()):
    barrier = pltpu.get_barrier_semaphore()
    count = 0
    for axis in axes:
        for rel in ("L", "R", "O"):
            pl.semaphore_signal(
                barrier, inc=1, device_id={axis: rel_index(axis, rel)}, device_id_type=MESH
            )
            count += 1
    if sib:
        pl.semaphore_signal(barrier, inc=1, device_id={"ctx": sibling()}, device_id_type=MESH)
        count += 1
    pl.semaphore_wait(barrier, count)


def rcopy(src, dst, ssem, rsem, axis, index):
    return pltpu.make_async_remote_copy(
        src_ref=src,
        dst_ref=dst,
        send_sem=ssem,
        recv_sem=rsem,
        device_id={axis: index},
        device_id_type=MESH,
    )


class Gather:
    @staticmethod
    def scratch(K):
        return (pltpu.SemaphoreType.DMA((14 * K,)), pltpu.SemaphoreType.DMA((7, 2 * K)))

    def __init__(self, axis, dst, ssem, rsem, alt=()):
        self.axis, self.dst, self.ssem, self.rsem = axis, dst, ssem, rsem
        self.alt = alt
        self.index = {rel: rel_index(axis, rel) for rel in RELS + ("M",)}
        self.sent = []
        self.seen = set()

    def send(self, source, k, route, to, as_rel):
        view = self.dst(self.index[source], k, route)
        copy = rcopy(
            view,
            view,
            self.ssem.at[len(self.sent)],
            self.rsem.at[RELS.index(as_rel), 2 * k + route],
            self.axis,
            self.index[to],
        )
        copy.start()
        self.sent.append(copy)

    def arrive(self, rel, k, route):
        if (rel, k, route) in self.seen:
            return
        self.seen.add((rel, k, route))
        view = self.dst(self.index[rel], k, route)
        rcopy(
            view,
            view,
            self.ssem.at[0],
            self.rsem.at[RELS.index(rel), 2 * k + route],
            self.axis,
            self.index["L"],
        ).wait_recv()

    def start(self, k):
        self.send("M", k, 0, "R", "L")
        self.send("M", k, 1, "L", "R")
        self.send("M", k, 0, "O", "O")
        self.send("M", k, 1, "O", "O")
        self.send("M", k, 0, "L", "R")
        self.send("M", k, 1, "R", "L")

    def relay_row(self, k):
        self.arrive("L", k, 0)
        self.send("L", k, 0, "R", "X")
        self.arrive("R", k, 1)
        self.send("R", k, 1, "L", "X")

    def relay_opposite(self, k):
        if k in self.alt:
            for first, second in ((0, 1), (1, 0)):
                for rel, route in (("L", first), ("R", second)):
                    self.arrive(rel, k, route)
                    self.send(rel, k, route, "O", "O" + rel)
            return
        self.arrive("O", k, 0)
        self.send("O", k, 0, "R", "OL")
        self.arrive("O", k, 1)
        self.send("O", k, 1, "L", "OR")
        self.send("O", k, 0, "L", "OR")
        self.send("O", k, 1, "R", "OL")

    def relay_last(self, k):
        if k in self.alt:
            for route in range(2):
                self.arrive("X", k, route)
                self.send("X", k, route, "O", "OX")
            return
        self.arrive("OL", k, 0)
        self.send("OL", k, 0, "R", "OX")
        self.arrive("OR", k, 1)
        self.send("OR", k, 1, "L", "OX")

    def finish(self, k):
        for rel in RELS:
            for route in range(2):
                self.arrive(rel, k, route)

    def drain(self):
        for copy in self.sent:
            copy.wait_send()


class Scatter:
    @staticmethod
    def scratch(K, piece):
        return (
            pltpu.VMEM((2, K, 2) + piece, BF16),
            pltpu.VMEM((2, K, 2) + piece, BF16),
            pltpu.VMEM((2, 2, K, 2) + piece, BF16),
            pltpu.VMEM((2, K, 2) + piece, BF16),
            pltpu.SemaphoreType.DMA((14 * K,)),
            pltpu.SemaphoreType.DMA((14 * K,)),
        )

    def __init__(self, axis, K, part, relay, stage, arrived, across, ssem, rsem, alt=()):
        self.axis, self.K, self.part, self.alt = axis, K, part, alt
        self.relay, self.stage, self.arrived, self.across = relay, stage, arrived, across
        self.ssem, self.rsem = ssem, rsem
        self.index = {rel: rel_index(axis, rel) for rel in RELS + ("M",)}
        self.sent = []

    def far(self, rel, k, route):
        if rel == "M":
            return self.across.at[1, k, route], self.across_slot(k, route)
        if rel == "L":
            return self.relay.at[1, k, route], self.relay_slot(1, k, route)
        d = ("R", "X").index(rel)
        return self.arrived.at[1, d, k, route], self.arrived_slot(1, d, k, route)

    def block(self, t, rel, k, route):
        if k in self.alt and t == 0 and rel != "M":
            return self.far(rel, k, route)[0]
        name = rel if t == 0 else ("O" if rel == "M" else "O" + rel)
        return self.part(self.index[name], k, route)

    def relay_slot(self, t, k, route):
        return (t * self.K + k) * 2 + route

    def arrived_slot(self, t, d, k, route):
        return 4 * self.K + ((t * 2 + d) * self.K + k) * 2 + route

    def across_slot(self, k, route):
        return 12 * self.K + 2 * k + route

    def send(self, src, dst, rslot, to):
        copy = rcopy(
            src, dst, self.ssem.at[len(self.sent)], self.rsem.at[rslot], self.axis, self.index[to]
        )
        copy.start()
        self.sent.append(copy)

    def arrive(self, dst, rslot):
        rcopy(dst, dst, self.ssem.at[0], self.rsem.at[rslot], self.axis, self.index["L"]).wait_recv()

    def start(self, t, k):
        if k in self.alt:
            if t == 1:
                for rel in ("X", "R", "L", "M"):
                    for route in range(2):
                        self.send(self.block(1, rel, k, route), *self.far(rel, k, route), "O")
            return
        self.ring(t, k)

    def ring(self, t, k):
        for route, to in ((0, "R"), (1, "L")):
            self.send(
                self.block(t, "X", k, route),
                self.relay.at[t, k, route],
                self.relay_slot(t, k, route),
                to,
            )
        for d, route, to in ((0, 1, "R"), (1, 0, "L")):
            self.send(
                self.block(t, to, k, route),
                self.arrived.at[t, d, k, route],
                self.arrived_slot(t, d, k, route),
                to,
            )

    def middle(self, t, k):
        if k in self.alt and t == 1:
            for rel in ("X", "R", "L"):
                for route in range(2):
                    share, slot = self.far(rel, k, route)
                    self.arrive(share, slot)
                    mine = self.part(self.index[rel], k, route)[...].astype(F32)
                    share[...] = (mine + share[...].astype(F32)).astype(BF16)
            self.ring(0, k)
            return
        for route, to in ((0, "R"), (1, "L")):
            self.arrive(self.relay.at[t, k, route], self.relay_slot(t, k, route))
            total = self.block(t, to, k, route)[...].astype(F32)
            total += self.relay[t, k, route].astype(F32)
            self.stage[t, k, route] = total.astype(BF16)
            self.send(
                self.stage.at[t, k, route],
                self.arrived.at[t, route, k, route],
                self.arrived_slot(t, route, k, route),
                to,
            )

    def row_sum(self, t, k, route):
        for d in range(2):
            self.arrive(self.arrived.at[t, d, k, route], self.arrived_slot(t, d, k, route))
        return (
            self.block(t, "M", k, route)[...].astype(F32)
            + self.arrived[t, 0, k, route].astype(F32)
            + self.arrived[t, 1, k, route].astype(F32)
        )

    def cross(self, k):
        if k in self.alt:
            return
        for route in range(2):
            self.across[0, k, route] = self.row_sum(1, k, route).astype(BF16)
            self.send(
                self.across.at[0, k, route],
                self.across.at[1, k, route],
                self.across_slot(k, route),
                "O",
            )

    def result(self, k, route):
        total = self.row_sum(0, k, route)
        self.arrive(self.across.at[1, k, route], self.across_slot(k, route))
        return total + self.across[1, k, route].astype(F32)

    def drain(self):
        for copy in self.sent:
            copy.wait_send()


def take(refs, count):
    return refs[:count], refs[count:]


def lane_iota(shape):
    return lax.broadcasted_iota(jnp.int32, shape, len(shape) - 1)


def dot_nt(a, b):
    return lax.dot_general(a, b, (((1,), (1,)), ((), ())), preferred_element_type=F32)


def dot_tn(a, b):
    return lax.dot_general(a, b, (((0,), (0,)), ((), ())), preferred_element_type=F32)


def dot(a, b):
    return jnp.dot(a, b, preferred_element_type=F32)


def head_sums(values, low):
    zero = jnp.zeros_like(values)
    first = jnp.sum(jnp.where(low, values, zero), axis=-1, keepdims=True)
    second = jnp.sum(jnp.where(low, zero, values), axis=-1, keepdims=True)
    return first, second


def swap_halves(values, first_half):
    return jnp.where(first_half, pltpu.roll(values, 96, 1), pltpu.roll(values, 32, 1))


def rms_scale(values):
    return lax.rsqrt(jnp.mean(values * values, axis=-1, keepdims=True) + EPSILON)


def norm_back(gradient, normed, scale_rows, gain_vec):
    scaled = gradient * gain_vec
    return scale_rows * (scaled - normed * jnp.mean(scaled * normed, axis=-1, keepdims=True))


def rows_of(index):
    return pl.ds(pl.multiple_of(index * 16, 16), 16)


def mp_rows(ref):
    return lambda i, k, route: ref.at[k, route, rows_of(i), :]


def kv_rows(ref):
    return lambda i, k, route: ref.at[k, i * 2 + route]


def forward_copy(view, ssem, rsem):
    copy = rcopy(view, view, ssem, rsem, "ctx", sibling())
    copy.start()
    return copy


def head_gains(query_gain, key_gain):
    q, k = query_gain[...], key_gain[...]
    return jnp.concatenate([q, q], axis=1), jnp.concatenate([k, jnp.ones_like(k)], axis=1)


def qkv_kernel(
    block_map, x, gain1, w, query_gain, key_gain, positions, frequency,
    full, cosine, sine, raw, queries, kv_all, *sems,
):
    mp = lax.axis_index("mp")
    ctx = lax.axis_index("ctx")
    enter(("mp", "ctx"), sib=True)
    (s1, r1, s2, r2), (s4, r4) = take(sems, 4)
    gain_q, gain_k = head_gains(query_gain, key_gain)
    first = Gather("mp", mp_rows(full), s1, r1, alt=(0, 2))
    keys = Gather("ctx", kv_rows(kv_all), s2, r2)
    for s in range(4):
        t = x[s].astype(F32)
        full[s, :, rows_of(mp), :] = (t * rms_scale(t) * gain1[...]).astype(BF16)
        first.start(s)
    lane = lane_iota((256, 128))
    low = lane < 64
    first_half = lax.rem(lane, 64) < 32
    sign = jnp.where(first_half[0:128], -1.0, 1.0)
    for t in range(2):
        chosen = lax.broadcasted_iota(jnp.int32, (32, 128), 0) == block_map[ctx * 2 + t]
        for s in range(4):
            row = jnp.where(chosen, positions[s].astype(F32), 0.0)
            row = jnp.sum(row, axis=0, keepdims=True)
            angle = jnp.broadcast_to(row, (128, 128)).T * frequency[...]
            cosine[s, t * 128 : t * 128 + 128] = jnp.cos(angle)
            sine[s, t * 128 : t * 128 + 128] = jnp.sin(angle) * sign
    forwards = []

    def forward(rel, s):
        slot = (("M",) + RELS).index(rel)
        view = kv_all.at[s, pl.ds(keys.index[rel] * 2, 2)]
        forwards.append(forward_copy(view, s4.at[slot, s], r4.at[slot, s]))

    def project(s):
        y = dot(full[s].reshape(256, 1024), w[...])
        raw[s] = y
        a, b = y[:, :128], y[:, 128:]
        cos, sin = cosine[s], sine[s]
        lo, _ = head_sums(b * b, low)
        g = b * lax.rsqrt(lo * (1 / 64) + EPSILON) * gain_k
        turned = g * cos + swap_halves(g, first_half) * sin
        packed = jnp.where(low, turned, b).astype(BF16)
        kv_all[s, pl.ds(ctx * 2, 2)] = packed.reshape(2, 128, 128)
        keys.start(s)
        forward("M", s)
        lo, hi = head_sums(a * a, low)
        scale = jnp.where(
            low, lax.rsqrt(lo * (1 / 64) + EPSILON), lax.rsqrt(hi * (1 / 64) + EPSILON)
        )
        g = a * scale * gain_q
        turned = g * cos + swap_halves(g, first_half) * sin
        zero = jnp.zeros_like(turned)
        head0 = jnp.where(low, turned, zero).astype(BF16)
        head1 = jnp.where(low, pltpu.roll(turned, 64, 1), zero).astype(BF16)
        for t in range(2):
            queries[s, t, 0:128] = head0[t * 128 : t * 128 + 128]
            queries[s, t, 128:256] = head1[t * 128 : t * 128 + 128]

    def at(k, *steps):
        if 0 <= k < 4:
            for step in steps:
                step(k)

    def finish_keys(s):
        for rel in RELS:
            for route in range(2):
                keys.arrive(rel, s, route)
            forward(rel, s)

    for step in range(4 + 6):
        at(step, first.relay_row, first.relay_opposite)
        at(step - 1, first.relay_last)
        at(step - 2, first.finish, project)
        at(step - 3, keys.relay_row, keys.relay_opposite)
        at(step - 4, keys.relay_last)
        at(step - 5, finish_keys)
    first.drain()
    keys.drain()
    for copy in forwards:
        copy.wait_send()
    for s in range(4):
        for slot, rel in enumerate(("M",) + RELS):
            view = kv_all.at[s, pl.ds((keys.index[rel] + sibling() - ctx) * 2, 2)]
            rcopy(view, view, s4.at[slot, s], r4.at[slot, s], "ctx", sibling()).wait_recv()


def attention_kernel(block_map, queries, kv_all, low_out, high_out, logs, where, acc):
    me = lax.axis_index("ctx")
    for slot in range(32):
        where[block_map[slot]] = slot
    lane_k = lane_iota((256, 128)) < 64
    for j in range(2):
        mine = block_map[2 * me + j]
        acc[...] = jnp.zeros_like(acc)

        def step(i, masked):
            slot0, slot1 = where[2 * i], where[2 * i + 1]
            if masked:
                row = lax.rem(lax.broadcasted_iota(jnp.int32, (256, 256), 0), 128)
                col = lax.broadcasted_iota(jnp.int32, (256, 256), 1)
                keep = col + 256 * i <= row + 128 * mine
            kvs = [
                jnp.concatenate([kv_all[s, slot0], kv_all[s, slot1]], axis=0) for s in range(4)
            ]
            scores = [dot_nt(queries[s, j], kvs[s]) for s in range(4)]
            for s in range(4):
                weights = jnp.exp2(scores[s] * EXPONENT_SCALE)
                if masked:
                    weights = jnp.where(keep, weights, 0.0)
                ones = jnp.where(lane_k, jnp.ones_like(kvs[s]), kvs[s])
                acc[s] += dot(weights.astype(BF16), ones)

        last = mine // 2
        lax.fori_loop(0, last, lambda i, c: (step(i, False), c)[1], 0)
        step(last, True)
        low = lane_iota((128, 128)) < 64
        for s in range(4):
            a = acc[s]
            o = a * pltpu.roll(1.0 / a, 64, 1)
            both = jnp.where(low, pltpu.roll(o[0:128], 64, 1), o[128:256])
            low_out[s, j] = both.astype(BF16)
            high_out[s, j] = both
            logs[s, j] = jnp.log2(a.T[0:8])


def attention_back_kernel(
    block_map, queries, kv_all, grad_out, out, logs,
    grad_q, grad_kv, where, acc, grad_pad, turned, delta,
):
    me = lax.axis_index("ctx")
    for slot in range(32):
        where[block_map[slot]] = slot
    acc[...] = jnp.zeros_like(acc)
    low = lane_iota((128, 128)) < 64
    for j in range(2):
        mine = block_map[2 * me + j]
        turned[...] = jnp.zeros_like(turned)
        for s in range(4):
            g = grad_out[s, j]
            gf = g.astype(F32)
            zero = jnp.zeros_like(gf)
            grad_pad[s, 0:128] = jnp.where(low, zero, pltpu.roll(gf, 64, 1)).astype(BF16)
            grad_pad[s, 128:256] = jnp.where(low, zero, gf).astype(BF16)
            product = (gf * out[s, j]).T
            delta[s, :, 0:128] = jnp.broadcast_to(
                jnp.sum(product[0:64], axis=0, keepdims=True), (8, 128)
            )
            delta[s, :, 128:256] = jnp.broadcast_to(
                jnp.sum(product[64:128], axis=0, keepdims=True), (8, 128)
            )

        def step(i, masked):
            slot0, slot1 = where[2 * i], where[2 * i + 1]
            if masked:
                col = lax.rem(lax.broadcasted_iota(jnp.int32, (256, 256), 1), 128)
                row = lax.broadcasted_iota(jnp.int32, (256, 256), 0)
                keep = row + 256 * i <= col + 128 * mine
            kvs = [
                jnp.concatenate([kv_all[s, slot0], kv_all[s, slot1]], axis=0) for s in range(4)
            ]
            scores = [dot_nt(kvs[s], queries[s, j]) for s in range(4)]
            grads = [dot_nt(kvs[s], grad_pad[s]) for s in range(4)]
            both = []
            for s in range(4):
                probs = jnp.exp2(
                    scores[s] * EXPONENT_SCALE - logs[s, j, 0:1]
                )
                if masked:
                    probs = jnp.where(keep, probs, 0.0)
                wide = (probs * (grads[s] - delta[s, 0:1])).astype(BF16)
                both.append((wide, probs.astype(BF16)))
            for s in range(4):
                turned[s] += dot_tn(kvs[s], both[s][0])
                block = dot(
                    jnp.concatenate(both[s], axis=1),
                    jnp.concatenate([queries[s, j], grad_pad[s]], axis=0),
                )
                acc[s, slot0] += block[0:128]
                acc[s, slot1] += block[128:256]

        last = mine // 2
        lax.fori_loop(0, last, lambda i, c: (step(i, False), c)[1], 0)
        step(last, True)
        for s in range(4):
            t = turned[s].T * 0.125
            grad_q[s, j] = jnp.where(low, t[0:128], pltpu.roll(t[128:256], 64, 1))
    scale = jnp.where(low, 0.125, 1.0)

    def finish(n, c):
        for s in range(4):
            grad_kv[s, n] = (acc[s, n] * scale).astype(BF16)
        return c

    lax.fori_loop(0, 32, finish, 0)


class Reduce:
    @staticmethod
    def scratch(A, R):
        return (
            pltpu.VMEM((A, R, 512), BF16),
            pltpu.VMEM((A, R, 512), BF16),
            pltpu.SemaphoreType.DMA((2,)),
            pltpu.SemaphoreType.DMA((2,)),
        ) + Scatter.scratch(1, (A, R // 4, 128))

    def __init__(self, source, got, pair, ssem, rsem, *rest):
        self.source, self.got, self.pair = source, got, pair
        self.ssem, self.rsem = ssem, rsem
        self.rows = source.shape[1] // 4
        self.sum = Scatter("ctx", 1, self.piece, *rest)

    def piece(self, i, k, route):
        row = pl.multiple_of(lax.rem(i // 2, 4) * self.rows, 16)
        column = pl.multiple_of((i // 8) * 256 + route * 128, 128)
        return self.pair.at[:, pl.ds(row, self.rows), pl.ds(column, 128)]

    def columns(self, y, core):
        return pl.ds(pl.multiple_of((2 * y + core) * 256, 256), 256)

    def exchange(self):
        core = lax.rem(lax.axis_index("ctx"), 2)
        self.copies = []
        for y in range(2):
            copy = rcopy(
                self.source.at[:, :, self.columns(y, 1 - core)],
                self.got.at[:, :, y * 256 : y * 256 + 256],
                self.ssem.at[y],
                self.rsem.at[y],
                "ctx",
                sibling(),
            )
            copy.start()
            self.copies.append(copy)

    def start(self):
        core = lax.rem(lax.axis_index("ctx"), 2)
        for y in range(2):
            self.copies[y].wait_recv()
            columns = slice(y * 256, y * 256 + 256)
            mine = self.source[:, :, self.columns(y, core)].astype(F32)
            self.pair[:, :, columns] = (mine + self.got[:, :, columns].astype(F32)).astype(BF16)
        self.sum.start(1, 0)
        self.sum.start(0, 0)

    def result(self, store):
        for route in range(2):
            store(route, self.sum.result(0, route).astype(BF16))

    def drain(self):
        for copy in self.copies:
            copy.wait_send()
        self.sum.drain()


class Spread:
    @staticmethod
    def scratch():
        return Gather.scratch(1) + (pltpu.SemaphoreType.DMA((8,)), pltpu.SemaphoreType.DMA((8,)))

    def __init__(self, target, ssem, rsem, fs, fr):
        self.target, self.fs, self.fr = target, fs, fr
        self.rows = target.shape[1] // 4
        self.gather = Gather("ctx", self.piece, ssem, rsem)
        self.forwards = []

    def view(self, i, shift, width):
        row = pl.multiple_of(lax.rem(i // 2, 4) * self.rows, 16)
        column = pl.multiple_of((2 * (i // 8) + lax.rem(i, 2)) * 256 + shift, 128)
        return self.target.at[:, pl.ds(row, self.rows), pl.ds(column, width)]

    def piece(self, i, k, route):
        return self.view(i, route * 128, 128)

    def own(self):
        return self.view(lax.axis_index("ctx"), 0, 256)

    def forward(self, rel):
        slot = len(self.forwards)
        view = self.view(self.gather.index[rel], 0, 256)
        self.forwards.append(forward_copy(view, self.fs.at[slot], self.fr.at[slot]))

    def start(self):
        self.gather.start(0)
        self.forward("M")

    def finish(self):
        for rel in RELS:
            for route in range(2):
                self.gather.arrive(rel, 0, route)
            self.forward(rel)

    def drain(self):
        self.gather.drain()
        ctx = lax.axis_index("ctx")
        for slot, rel in enumerate(("M",) + RELS):
            self.forwards[slot].wait_send()
            view = self.view(self.gather.index[rel] + sibling() - ctx, 0, 256)
            rcopy(view, view, self.fs.at[slot], self.fr.at[slot], "ctx", sibling()).wait_recv()


def middle_kernel(
    x, attended, w, gain2, cot, cot_full, gate_up, down,
    mixed, d_mixed, part_o, d_att, gain_part, out_part, ffn_own,
    part, full, part_d, branch, turned, grads, *scratch,
):
    mp = lax.axis_index("mp")
    enter(("mp", "ctx"), sib=True)
    sums1, rest = take(scratch, 6)
    sums2, rest = take(rest, 6)
    (s1, r1, s2, r2), sums3 = take(rest, 4)
    rs1 = Scatter("mp", 4, mp_rows(part), *sums1, alt=(3,))
    rs2 = Scatter("mp", 4, mp_rows(part_d), *sums2, alt=(3,))
    ag2 = Gather("mp", mp_rows(full), s1, r1, alt=(0, 2))
    ag3 = Gather("mp", mp_rows(branch), s2, r2, alt=(0,))
    reduce = Reduce(grads, *sums3)

    def mix(k):
        for t in range(2):
            m = x[k, t].astype(F32) + rs1.result(k, t)
            mixed[k, t] = m
            full[k, t, rows_of(mp), :] = (m * rms_scale(m) * gain2[...]).astype(BF16)
        ag2.start(k)

    def feed(k):
        rows = full[k].reshape(256, 1024)
        columns = slice(k * 256, k * 256 + 256)
        gate = dot_nt(rows, gate_up[0])
        up = dot_nt(rows, gate_up[1])
        sig = 1.0 / (1.0 + jnp.exp(-gate))
        d_active = dot_nt(cot_full[k].reshape(256, 1024), down[...])
        d_gate = (d_active * up * sig * (1.0 + gate * (1.0 - sig))).astype(BF16)
        d_up = (d_active * gate * sig).astype(BF16)
        both = dot(d_gate, gate_up[0]) + dot(d_up, gate_up[1])
        part_d[k] = both.astype(BF16).reshape(2, 128, 1024)
        rs2.start(1, k)
        rs2.start(0, k)
        active = (gate * sig * up).astype(BF16)
        part_o[k] = dot(active, down[...]).astype(BF16).reshape(2, 128, 1024)
        turned[0, :, columns] = d_gate.T
        turned[1, :, columns] = d_up.T
        turned[2, :, columns] = active.T

    def weigh():
        def tile(n, c):
            columns = pl.ds(pl.multiple_of(n * 256, 256), 256)
            rows = full[:, :, :, columns].reshape(1024, 256)
            for i in range(2):
                grads[i, :, columns] = dot(turned[i], rows).astype(BF16)
            rows = cot_full[:, :, :, columns].reshape(1024, 256)
            grads[2, :, columns] = dot(turned[2], rows).astype(BF16)
            return c

        lax.fori_loop(0, 4, tile, 0)

    gain_part[...] = jnp.zeros_like(gain_part)

    def back(k):
        for t in range(2):
            g = rs2.result(k, t)
            m = mixed[k, t]
            scale = rms_scale(m)
            normed = m * scale
            gain_part[...] += jnp.sum(g * normed, axis=0, keepdims=True)
            dm = cot[k, t].astype(F32) + norm_back(g, normed, scale, gain2[...])
            d_mixed[k, t] = dm
            branch[k, t, rows_of(mp), :] = dm.astype(BF16)
        ag3.start(k)

    def attend(k):
        rows = branch[k].reshape(256, 1024)
        d_att[k] = dot_nt(rows, w[...]).astype(BF16).reshape(2, 128, 128)

    def at(k, *steps):
        if 0 <= k < 4:
            for step in steps:
                step(k)

    for k in range(4):
        part[k] = dot(attended[k].reshape(256, 128), w[...]).astype(BF16).reshape(2, 128, 1024)
        rs1.start(1, k)
        rs1.start(0, k)
    for step in range(4 + 11):
        at(step, lambda k: rs1.middle(1, k))
        at(step - 1, rs1.cross, lambda k: rs1.middle(0, k))
        at(step - 2, mix)
        at(step - 3, ag2.relay_row, ag2.relay_opposite)
        at(step - 4, ag2.relay_last)
        at(step - 5, ag2.finish, feed)
        if step == 8:
            weigh()
            reduce.exchange()
        at(step - 6, lambda k: rs2.middle(1, k))
        at(step - 7, rs2.cross, lambda k: rs2.middle(0, k))
        if step == 9:
            reduce.start()
        at(step - 8, back)
        if step == 10:
            reduce.sum.middle(1, 0)
        if step == 11:
            reduce.sum.cross(0)
            reduce.sum.middle(0, 0)
        at(step - 9, ag3.relay_row, ag3.relay_opposite)
        at(step - 10, ag3.relay_last)
        at(step - 11, ag3.finish, attend)
    rows = attended[...].reshape(1024, 128).T
    for n in range(4):
        columns = slice(n * 256, n * 256 + 256)
        out_part[:, columns] = dot(rows, branch[:, :, :, columns].reshape(1024, 256)).astype(BF16)

    def store(route, value):
        ffn_own[:, :, route * 128 : route * 128 + 128] = value

    reduce.result(store)
    for item in (rs1, ag2, rs2, ag3, reduce):
        item.drain()


def last_kernel(
    grad_kv, grad_q, raw, cosine, sine, query_gain, key_gain, w, x, gain1, d_mixed,
    mixed, part_o, full, out_part, gain2_part,
    out, in_grad, attn_sum, total,
    pair, got, d_qkv, part, grads, gain_row, small, by_mp, by_ctx, *scratch,
):
    ctx = lax.axis_index("ctx")
    mp = lax.axis_index("mp")
    barrier = pltpu.get_barrier_semaphore()
    for axis, size in (("mp", 8), ("ctx", 16)):
        me = lax.axis_index(axis)
        for n in range(1, size):
            pl.semaphore_signal(
                barrier, inc=1, device_id={axis: lax.rem(me + n, size)}, device_id_type=MESH
            )
    pl.semaphore_wait(barrier, 22)
    sums_k, rest = take(scratch, 6)
    sums_o, rest = take(rest, 6)
    sums_n, rest = take(rest, 6)
    sums_a, rest = take(rest, 10)
    spread_a, rest = take(rest, 4)
    s1, r1, s2, r2, s3, r3 = rest
    core = lax.rem(ctx, 2)
    sib = sibling()
    copies = []
    for s in range(4):
        for chip in range(8):
            src = grad_kv.at[s, pl.ds(chip * 4 + (1 - core) * 2, 2)]
            copy = rcopy(
                src, got.at[s, pl.ds(chip * 2, 2)], s1.at[s, chip], r1.at[s, chip], "ctx", sib
            )
            copy.start()
            copies.append(copy)
    rs_k = Scatter("ctx", 4, lambda i, k, route: pair.at[k, (i // 2) * 2 + route], *sums_k)
    rs_o = Scatter("mp", 4, mp_rows(part_o), *sums_o)
    rs_n = Scatter("mp", 4, mp_rows(part), *sums_n, alt=(3,))
    reduce = Reduce(grads, *sums_a)
    attn = Spread(attn_sum, *spread_a)
    for s in range(4):
        rs_o.start(1, s)
        rs_o.start(0, s)
        for chip in range(8):
            copies[s * 8 + chip].wait_recv()
            mine = grad_kv[s, pl.ds(chip * 4 + core * 2, 2)].astype(F32)
            both = mine + got[s, chip * 2 : chip * 2 + 2].astype(F32)
            pair[s, chip * 2 : chip * 2 + 2] = both.astype(BF16)
        rs_k.start(1, s)
        rs_k.start(0, s)
    grads[0, 256:384, :] = out_part[...]
    lane = lane_iota((256, 128))
    low = lane < 64
    first_half = lax.rem(lane, 64) < 32
    inv = 1 / 64
    small[...] = jnp.zeros_like(small)
    gain_row[...] = jnp.zeros_like(gain_row)
    for n in range(8):
        small[8 + n : 9 + n, :] = gain2_part[:, n * 128 : n * 128 + 128]
    gain_q, gain_k = head_gains(query_gain, key_gain)

    def project(s):
        y = raw[s]
        a, b = y[:, :128], y[:, 128:]
        cos, sin = cosine[s], sine[s]
        lo, hi = head_sums(a * a, low)
        scale = jnp.where(low, lax.rsqrt(lo * inv + EPSILON), lax.rsqrt(hi * inv + EPSILON))
        n = a * scale
        d = grad_q[s].reshape(256, 128)
        g = d * cos - swap_halves(d, first_half) * sin
        small[16:17, :] += jnp.sum(g * n, axis=0, keepdims=True)
        e = g * gain_q
        lo, hi = head_sums(e * n, low)
        dq = scale * (e - n * jnp.where(low, lo * inv, hi * inv))
        d_qkv[s, :, 0:128] = dq.astype(BF16)
        lo, _ = head_sums(b * b, low)
        scale = lax.rsqrt(lo * inv + EPSILON)
        n = b * scale
        d = jnp.concatenate([rs_k.result(s, 0), rs_k.result(s, 1)], axis=0)
        g = d * cos - swap_halves(d, first_half) * sin
        small[17:18, :] += jnp.sum(g * n, axis=0, keepdims=True)
        e = g * gain_k
        lo, _ = head_sums(e * n, low)
        dk = scale * (e - n * (lo * inv))
        d_qkv[s, :, 128:256] = jnp.where(low, dk, d).astype(BF16)
        part[s] = dot_nt(d_qkv[s], w[...]).astype(BF16).reshape(2, 128, 1024)
        rs_n.start(1, s)
        rs_n.start(0, s)

    def write_out(s):
        for t in range(2):
            out[s, t] = (mixed[s, t] + rs_o.result(s, t)).astype(BF16)

    def weigh():
        rows = d_qkv[...].reshape(1024, 256).T
        for n in range(4):
            columns = slice(n * 256, n * 256 + 256)
            value = dot(rows, full[:, :, :, columns].reshape(1024, 256))
            grads[0, 0:256, columns] = value.astype(BF16)

    def write_grad(s):
        for t in range(2):
            g = rs_n.result(s, t)
            v = x[s, t].astype(F32)
            scale = rms_scale(v)
            normed = v * scale
            gain_row[...] += jnp.sum(g * normed, axis=0, keepdims=True)
            in_grad[s, t] = (d_mixed[s, t] + norm_back(g, normed, scale, gain1[...])).astype(BF16)

    def at(k, *steps):
        if 0 <= k < 4:
            for step in steps:
                step(k)

    def store(route, value):
        attn.piece(ctx, 0, route)[...] = value

    for step in range(4 + 3):
        at(step, lambda k: rs_k.middle(1, k), lambda k: rs_o.middle(1, k))
        at(step - 1, rs_k.cross, lambda k: rs_k.middle(0, k))
        at(step - 1, rs_o.cross, lambda k: rs_o.middle(0, k))
        at(step - 2, project)
        if step == 5:
            weigh()
            reduce.exchange()
        at(step - 3, lambda k: rs_n.middle(1, k))
    reduce.start()
    for k in range(4):
        rs_n.cross(k)
        rs_n.middle(0, k)
    for k in range(4):
        write_out(k)
    reduce.sum.middle(1, 0)
    reduce.sum.cross(0)
    reduce.sum.middle(0, 0)
    write_grad(0)
    write_grad(1)
    reduce.result(store)
    attn.start()
    write_grad(2)
    write_grad(3)
    for n in range(8):
        small[n : n + 1, :] = gain_row[:, n * 128 : n * 128 + 128]
    copies2 = []
    for n in range(1, 8):
        copy = rcopy(small, by_mp.at[n], s2.at[n], r2.at[n], "mp", lax.rem(mp + n, 8))
        copy.start()
        copies2.append(copy)
    attn.gather.relay_row(0)
    attn.gather.relay_opposite(0)
    by_mp[0] = small[...]
    for copy in copies2:
        copy.wait()
    by_ctx[0] = jnp.sum(by_mp[...], axis=0)
    copies3 = []
    for n in range(1, 16):
        copy = rcopy(
            by_ctx.at[0], by_ctx.at[n], s3.at[n], r3.at[n], "ctx", lax.rem(ctx + n, 16)
        )
        copy.start()
        copies3.append(copy)
    attn.gather.relay_last(0)
    attn.finish()
    for copy in copies3:
        copy.wait()
    total[...] = jnp.zeros_like(total)

    def add(i, c):
        total[...] += by_ctx[lax.rem(ctx - i + 16, 16)]
        return c

    lax.fori_loop(0, 16, add, 0)
    for copy in copies:
        copy.wait_send()
    for item in (rs_k, rs_o, rs_n, reduce, attn):
        item.drain()


def widen_kernel(ffn_all, attn_sum, gate_up_grad, down_grad, qkv_grad, out_grad):
    step = pl.program_id(0)

    def widen(target):
        for y in range(2):
            for core in range(2):
                start = (2 * y + core) * 256
                target[:, start : start + 256] = ffn_all[y, 0, core, 0].astype(F32)

    @pl.when(step == 0)
    def _():
        qkv_grad[...] = attn_sum[0, 0:256].astype(F32).T.reshape(1024, 1, 256)
        out_grad[...] = attn_sum[0, 256:384].astype(F32)

    @pl.when(step < 8)
    def _():
        widen(gate_up_grad.at[0])

    @pl.when(step >= 8)
    def _():
        widen(down_grad)


def vm(n):
    return [pl.BlockSpec(memory_space=pltpu.VMEM)] * n


def sds(shape, dtype):
    return jax.ShapeDtypeStruct(shape, dtype)


def local(
    residual_in,
    attn_norm,
    query_key_value_weight,
    query_gain,
    key_gain,
    out_weight,
    ffn_norm,
    gate_up,
    down_weight,
    cotangent,
    positions,
    block_map,
):
    rows_shape = (4, 2, 16, 1024)
    full_shape = (4, 2, 128, 1024)
    piece = (16, 1024)
    dma = pltpu.SemaphoreType.DMA

    inverse_freq = 1.0 / ROPE_BASE ** (np.arange(0, 64, 2) / 64)
    frequency = np.tile(inverse_freq, 4).reshape(1, 128).astype(np.float32)
    gain_q, gain_k = query_gain.reshape(1, 64), key_gain.reshape(1, 64)
    smem = [pl.BlockSpec(memory_space=pltpu.SMEM)]
    cot_full = lax.all_gather(cotangent, "mp", axis=2, tiled=True)
    gain1 = attn_norm.reshape(1, 1024)
    gain2 = ffn_norm.reshape(1, 1024)
    w_qkv = query_key_value_weight.reshape(1024, 256)

    full1, cosine, sine, raw, queries, kv_all = pl.pallas_call(
        qkv_kernel,
        out_shape=(
            sds(full_shape, BF16),
            sds((4, 256, 128), F32),
            sds((4, 256, 128), F32),
            sds((4, 256, 256), F32),
            sds((4, 2, 256, 128), BF16),
            sds((4, 32, 128, 128), BF16),
        ),
        in_specs=smem + vm(7),
        out_specs=tuple(vm(6)),
        scratch_shapes=Gather.scratch(4) * 2 + (dma((8, 4)), dma((8, 4))),
        compiler_params=params(1),
    )(block_map, residual_in, gain1, w_qkv, gain_q, gain_k, positions.reshape(4, 32, 128), frequency)

    attended, attended_high, logs = pl.pallas_call(
        attention_kernel,
        out_shape=(
            sds((4, 2, 128, 128), BF16),
            sds((4, 2, 128, 128), F32),
            sds((4, 2, 8, 256), F32),
        ),
        in_specs=smem + vm(2),
        out_specs=tuple(vm(3)),
        scratch_shapes=[pltpu.SMEM((32,), jnp.int32), pltpu.VMEM((4, 256, 128), F32)],
        compiler_params=pltpu.CompilerParams(vmem_limit_bytes=VMEM_LIMIT),
    )(block_map, queries, kv_all)

    gate_up_t = jnp.transpose(gate_up, (1, 2, 0))
    mixed, d_mixed, part_o, d_att, gain2_part, out_part, ffn_own = pl.pallas_call(
        middle_kernel,
        out_shape=(
            sds(rows_shape, F32),
            sds(rows_shape, F32),
            sds(full_shape, BF16),
            sds((4, 2, 128, 128), BF16),
            sds((1, 1024), F32),
            sds((128, 1024), BF16),
            sds((3, 144, 256), BF16),
        ),
        in_specs=vm(8),
        out_specs=tuple(vm(7)),
        scratch_shapes=(pltpu.VMEM(full_shape, BF16),) * 4
        + (pltpu.VMEM((3, 576, 1024), BF16),) * 2
        + Scatter.scratch(4, piece) * 2
        + Gather.scratch(4) * 2
        + Reduce.scratch(3, 576),
        compiler_params=params(2),
    )(
        residual_in, attended, out_weight, gain2, cotangent, cot_full, gate_up_t, down_weight
    )

    ffn_all = lax.all_gather(ffn_own, "ctx", axis=0).reshape(2, 4, 2, 3, 144, 256)

    grad_q, grad_kv = pl.pallas_call(
        attention_back_kernel,
        out_shape=(sds((4, 2, 128, 128), F32), sds((4, 32, 128, 128), BF16)),
        in_specs=smem + vm(5),
        out_specs=tuple(vm(2)),
        scratch_shapes=[
            pltpu.SMEM((32,), jnp.int32),
            pltpu.VMEM((4, 32, 128, 128), F32),
            pltpu.VMEM((4, 256, 128), BF16),
            pltpu.VMEM((4, 128, 256), F32),
            pltpu.VMEM((4, 8, 256), F32),
        ],
        compiler_params=pltpu.CompilerParams(vmem_limit_bytes=VMEM_LIMIT),
    )(block_map, queries, kv_all, d_att, attended_high, logs)

    output, input_grad, attn_sum, sums = pl.pallas_call(
        last_kernel,
        out_shape=(
            sds(rows_shape, BF16),
            sds(rows_shape, BF16),
            sds((1, 384, 1024), BF16),
            sds((24, 128), F32),
        ),
        in_specs=vm(16),
        out_specs=tuple(vm(4)),
        scratch_shapes=(
            pltpu.VMEM((4, 16, 128, 128), BF16),
            pltpu.VMEM((4, 16, 128, 128), BF16),
            pltpu.VMEM((4, 256, 256), BF16),
            pltpu.VMEM(full_shape, BF16),
            pltpu.VMEM((1, 384, 1024), BF16),
            pltpu.VMEM((1, 1024), F32),
            pltpu.VMEM((24, 128), F32),
            pltpu.VMEM((8, 24, 128), F32),
            pltpu.VMEM((16, 24, 128), F32),
        )
        + Scatter.scratch(4, (128, 128))
        + Scatter.scratch(4, piece) * 2
        + Reduce.scratch(1, 384)
        + Spread.scratch()
        + (dma((4, 8)), dma((4, 8)), dma((8,)), dma((8,)), dma((16,)), dma((16,))),
        compiler_params=params(3),
    )(
        grad_kv, grad_q, raw, cosine, sine, gain_q, gain_k, w_qkv, residual_in, gain1,
        d_mixed, mixed, part_o, full1, out_part, gain2_part,
    )

    gate_up_grad, down_grad, qkv_grad, out_grad = pl.pallas_call(
        widen_kernel,
        grid=(12,),
        out_shape=(
            sds((2, 576, 1024), F32),
            sds((576, 1024), F32),
            sds((1024, 1, 256), F32),
            sds((128, 1024), F32),
        ),
        in_specs=[
            pl.BlockSpec((2, 1, 2, 1, 144, 256), lambda i: (0, i % 4, 0, i // 4, 0, 0)),
            pl.BlockSpec((1, 384, 1024), lambda i: (0, 0, 0)),
        ],
        out_specs=(
            pl.BlockSpec((1, 144, 1024), lambda i: (jnp.minimum(i, 7) // 4, jnp.minimum(i, 7) % 4, 0)),
            pl.BlockSpec((144, 1024), lambda i: (jnp.maximum(i - 8, 0), 0)),
            pl.BlockSpec((1024, 1, 256), lambda i: (0, 0, 0)),
            pl.BlockSpec((128, 1024), lambda i: (0, 0)),
        ),
        compiler_params=pltpu.CompilerParams(vmem_limit_bytes=VMEM_LIMIT),
    )(ffn_all, attn_sum)

    return (
        output,
        input_grad,
        sums[0:8].reshape(1024),
        qkv_grad,
        sums[16, :64] + sums[16, 64:128],
        sums[17, :64],
        out_grad,
        sums[8:16].reshape(1024),
        jnp.transpose(gate_up_grad, (2, 0, 1)),
        down_grad,
    )


def solution(mesh):
    return jax.shard_map(
        local,
        mesh=mesh,
        in_specs=(
            P(None, "ctx", "mp", None),
            P(),
            P(None, "mp", None),
            P(),
            P(),
            P("mp", None),
            P(),
            P(None, None, "mp"),
            P("mp", None),
            P(None, "ctx", "mp", None),
            P(),
            P(),
        ),
        out_specs=(
            P(None, "ctx", "mp", None),
            P(None, "ctx", "mp", None),
            P(),
            P(None, "mp", None),
            P(),
            P(),
            P("mp", None),
            P(),
            P(None, None, "mp"),
            P("mp", None),
        ),
        check_vma=False,
    )
```

```python
import functools
import math

import jax
import jax.numpy as jnp
import numpy as np
from jax import lax
from jax.experimental import pallas as pl
from jax.experimental.pallas import tpu as pltpu
from jax.sharding import PartitionSpec as P

EPSILON = 1e-05
ROPE_BASE = 1000000.0
EXPONENT_SCALE = 0.125 * math.log2(math.e)
MESH = pl.DeviceIdType.MESH
F32 = jnp.float32
BF16 = jnp.bfloat16
RELS = ("L", "R", "X", "O", "OL", "OR", "OX")
VMEM_LIMIT = 56 << 20


def params(cid):
    return pltpu.CompilerParams(
        collective_id=cid, has_side_effects=True, vmem_limit_bytes=VMEM_LIMIT
    )


def rel_index(axis, rel):
    me = lax.axis_index(axis)
    core = 0
    if axis == "ctx":
        core = lax.rem(me, 2)
        me = me // 2
    pos = lax.rem(me, 4)
    row = me // 4
    step = {"L": 3, "R": 1, "X": 2, "M": 0}[rel[-1] if rel[-1] != "O" else "M"]
    if rel[0] == "O":
        row = 1 - row
    index = row * 4 + lax.rem(pos + step, 4)
    if axis == "ctx":
        index = index * 2 + core
    return index


def sibling():
    me = lax.axis_index("ctx")
    return me + 1 - 2 * lax.rem(me, 2)


def enter(axes, sib=False, extra=()):
    barrier = pltpu.get_barrier_semaphore()
    count = 0
    for axis in axes:
        for rel in ("L", "R", "O"):
            pl.semaphore_signal(
                barrier, inc=1, device_id={axis: rel_index(axis, rel)}, device_id_type=MESH
            )
            count += 1
    if sib:
        pl.semaphore_signal(barrier, inc=1, device_id={"ctx": sibling()}, device_id_type=MESH)
        count += 1
    pl.semaphore_wait(barrier, count)


def rcopy(src, dst, ssem, rsem, axis, index):
    return pltpu.make_async_remote_copy(
        src_ref=src,
        dst_ref=dst,
        send_sem=ssem,
        recv_sem=rsem,
        device_id={axis: index},
        device_id_type=MESH,
    )


class Gather:
    @staticmethod
    def scratch(K):
        return (pltpu.SemaphoreType.DMA((14 * K,)), pltpu.SemaphoreType.DMA((7, 2 * K)))

    def __init__(self, axis, dst, ssem, rsem, alt=()):
        self.axis, self.dst, self.ssem, self.rsem = axis, dst, ssem, rsem
        self.alt = alt
        self.index = {rel: rel_index(axis, rel) for rel in RELS + ("M",)}
        self.sent = []
        self.seen = set()

    def send(self, source, k, route, to, as_rel):
        view = self.dst(self.index[source], k, route)
        copy = rcopy(
            view,
            view,
            self.ssem.at[len(self.sent)],
            self.rsem.at[RELS.index(as_rel), 2 * k + route],
            self.axis,
            self.index[to],
        )
        copy.start()
        self.sent.append(copy)

    def arrive(self, rel, k, route):
        if (rel, k, route) in self.seen:
            return
        self.seen.add((rel, k, route))
        view = self.dst(self.index[rel], k, route)
        rcopy(
            view,
            view,
            self.ssem.at[0],
            self.rsem.at[RELS.index(rel), 2 * k + route],
            self.axis,
            self.index["L"],
        ).wait_recv()

    def start(self, k):
        self.send("M", k, 0, "R", "L")
        self.send("M", k, 1, "L", "R")
        self.send("M", k, 0, "O", "O")
        self.send("M", k, 1, "O", "O")
        self.send("M", k, 0, "L", "R")
        self.send("M", k, 1, "R", "L")

    def relay_row(self, k):
        self.arrive("L", k, 0)
        self.send("L", k, 0, "R", "X")
        self.arrive("R", k, 1)
        self.send("R", k, 1, "L", "X")

    def relay_opposite(self, k):
        if k in self.alt:
            for first, second in ((0, 1), (1, 0)):
                for rel, route in (("L", first), ("R", second)):
                    self.arrive(rel, k, route)
                    self.send(rel, k, route, "O", "O" + rel)
            return
        self.arrive("O", k, 0)
        self.send("O", k, 0, "R", "OL")
        self.arrive("O", k, 1)
        self.send("O", k, 1, "L", "OR")
        self.send("O", k, 0, "L", "OR")
        self.send("O", k, 1, "R", "OL")

    def relay_last(self, k):
        if k in self.alt:
            for route in range(2):
                self.arrive("X", k, route)
                self.send("X", k, route, "O", "OX")
            return
        self.arrive("OL", k, 0)
        self.send("OL", k, 0, "R", "OX")
        self.arrive("OR", k, 1)
        self.send("OR", k, 1, "L", "OX")

    def finish(self, k):
        for rel in RELS:
            for route in range(2):
                self.arrive(rel, k, route)

    def drain(self):
        for copy in self.sent:
            copy.wait_send()


class Scatter:
    @staticmethod
    def scratch(K, piece):
        return (
            pltpu.VMEM((2, K, 2) + piece, BF16),
            pltpu.VMEM((2, K, 2) + piece, BF16),
            pltpu.VMEM((2, 2, K, 2) + piece, BF16),
            pltpu.VMEM((2, K, 2) + piece, BF16),
            pltpu.SemaphoreType.DMA((14 * K,)),
            pltpu.SemaphoreType.DMA((14 * K,)),
        )

    def __init__(self, axis, K, part, relay, stage, arrived, across, ssem, rsem, alt=()):
        self.axis, self.K, self.part, self.alt = axis, K, part, alt
        self.relay, self.stage, self.arrived, self.across = relay, stage, arrived, across
        self.ssem, self.rsem = ssem, rsem
        self.index = {rel: rel_index(axis, rel) for rel in RELS + ("M",)}
        self.sent = []

    def far(self, rel, k, route):
        if rel == "M":
            return self.across.at[1, k, route], self.across_slot(k, route)
        if rel == "L":
            return self.relay.at[1, k, route], self.relay_slot(1, k, route)
        d = ("R", "X").index(rel)
        return self.arrived.at[1, d, k, route], self.arrived_slot(1, d, k, route)

    def block(self, t, rel, k, route):
        if k in self.alt and t == 0 and rel != "M":
            return self.far(rel, k, route)[0]
        name = rel if t == 0 else ("O" if rel == "M" else "O" + rel)
        return self.part(self.index[name], k, route)

    def relay_slot(self, t, k, route):
        return (t * self.K + k) * 2 + route

    def arrived_slot(self, t, d, k, route):
        return 4 * self.K + ((t * 2 + d) * self.K + k) * 2 + route

    def across_slot(self, k, route):
        return 12 * self.K + 2 * k + route

    def send(self, src, dst, rslot, to):
        copy = rcopy(
            src, dst, self.ssem.at[len(self.sent)], self.rsem.at[rslot], self.axis, self.index[to]
        )
        copy.start()
        self.sent.append(copy)

    def arrive(self, dst, rslot):
        rcopy(dst, dst, self.ssem.at[0], self.rsem.at[rslot], self.axis, self.index["L"]).wait_recv()

    def start(self, t, k):
        if k in self.alt:
            if t == 1:
                for rel in ("X", "R", "L", "M"):
                    for route in range(2):
                        self.send(self.block(1, rel, k, route), *self.far(rel, k, route), "O")
            return
        self.ring(t, k)

    def ring(self, t, k):
        for route, to in ((0, "R"), (1, "L")):
            self.send(
                self.block(t, "X", k, route),
                self.relay.at[t, k, route],
                self.relay_slot(t, k, route),
                to,
            )
        for d, route, to in ((0, 1, "R"), (1, 0, "L")):
            self.send(
                self.block(t, to, k, route),
                self.arrived.at[t, d, k, route],
                self.arrived_slot(t, d, k, route),
                to,
            )

    def middle(self, t, k):
        if k in self.alt and t == 1:
            for rel in ("X", "R", "L"):
                for route in range(2):
                    share, slot = self.far(rel, k, route)
                    self.arrive(share, slot)
                    mine = self.part(self.index[rel], k, route)[...].astype(F32)
                    share[...] = (mine + share[...].astype(F32)).astype(BF16)
            self.ring(0, k)
            return
        for route, to in ((0, "R"), (1, "L")):
            self.arrive(self.relay.at[t, k, route], self.relay_slot(t, k, route))
            total = self.block(t, to, k, route)[...].astype(F32)
            total += self.relay[t, k, route].astype(F32)
            self.stage[t, k, route] = total.astype(BF16)
            self.send(
                self.stage.at[t, k, route],
                self.arrived.at[t, route, k, route],
                self.arrived_slot(t, route, k, route),
                to,
            )

    def row_sum(self, t, k, route):
        for d in range(2):
            self.arrive(self.arrived.at[t, d, k, route], self.arrived_slot(t, d, k, route))
        return (
            self.block(t, "M", k, route)[...].astype(F32)
            + self.arrived[t, 0, k, route].astype(F32)
            + self.arrived[t, 1, k, route].astype(F32)
        )

    def cross(self, k):
        if k in self.alt:
            return
        for route in range(2):
            self.across[0, k, route] = self.row_sum(1, k, route).astype(BF16)
            self.send(
                self.across.at[0, k, route],
                self.across.at[1, k, route],
                self.across_slot(k, route),
                "O",
            )

    def result(self, k, route):
        total = self.row_sum(0, k, route)
        self.arrive(self.across.at[1, k, route], self.across_slot(k, route))
        return total + self.across[1, k, route].astype(F32)

    def drain(self):
        for copy in self.sent:
            copy.wait_send()


def take(refs, count):
    return refs[:count], refs[count:]


def lane_iota(shape):
    return lax.broadcasted_iota(jnp.int32, shape, len(shape) - 1)


def dot_nt(a, b):
    return lax.dot_general(a, b, (((1,), (1,)), ((), ())), preferred_element_type=F32)


def dot_tn(a, b):
    return lax.dot_general(a, b, (((0,), (0,)), ((), ())), preferred_element_type=F32)


def dot(a, b):
    return jnp.dot(a, b, preferred_element_type=F32)


def head_sums(values, low):
    zero = jnp.zeros_like(values)
    first = jnp.sum(jnp.where(low, values, zero), axis=-1, keepdims=True)
    second = jnp.sum(jnp.where(low, zero, values), axis=-1, keepdims=True)
    return first, second


def swap_halves(values, first_half):
    return jnp.where(first_half, pltpu.roll(values, 96, 1), pltpu.roll(values, 32, 1))


def rms_scale(values):
    return lax.rsqrt(jnp.mean(values * values, axis=-1, keepdims=True) + EPSILON)


def norm_back(gradient, normed, scale_rows, gain_vec):
    scaled = gradient * gain_vec
    return scale_rows * (scaled - normed * jnp.mean(scaled * normed, axis=-1, keepdims=True))


def rows_of(index):
    return pl.ds(pl.multiple_of(index * 16, 16), 16)


def mp_rows(ref):
    return lambda i, k, route: ref.at[k, route, rows_of(i), :]


def kv_rows(ref):
    return lambda i, k, route: ref.at[k, i * 2 + route]


def forward_copy(view, ssem, rsem):
    copy = rcopy(view, view, ssem, rsem, "ctx", sibling())
    copy.start()
    return copy


def head_gains(query_gain, key_gain):
    q, k = query_gain[...], key_gain[...]
    return jnp.concatenate([q, q], axis=1), jnp.concatenate([k, jnp.ones_like(k)], axis=1)


def qkv_kernel(
    block_map, x, gain1, w, query_gain, key_gain, positions, frequency,
    full, cosine, sine, raw, queries, kv_all, *sems,
):
    mp = lax.axis_index("mp")
    ctx = lax.axis_index("ctx")
    enter(("mp", "ctx"), sib=True)
    (s1, r1, s2, r2), (s4, r4) = take(sems, 4)
    gain_q, gain_k = head_gains(query_gain, key_gain)
    first = Gather("mp", mp_rows(full), s1, r1, alt=(0, 2))
    keys = Gather("ctx", kv_rows(kv_all), s2, r2)
    for s in range(4):
        t = x[s].astype(F32)
        full[s, :, rows_of(mp), :] = (t * rms_scale(t) * gain1[...]).astype(BF16)
        first.start(s)
    lane = lane_iota((256, 128))
    low = lane < 64
    first_half = lax.rem(lane, 64) < 32
    sign = jnp.where(first_half[0:128], -1.0, 1.0)
    for t in range(2):
        chosen = lax.broadcasted_iota(jnp.int32, (32, 128), 0) == block_map[ctx * 2 + t]
        for s in range(4):
            row = jnp.where(chosen, positions[s].astype(F32), 0.0)
            row = jnp.sum(row, axis=0, keepdims=True)
            angle = jnp.broadcast_to(row, (128, 128)).T * frequency[...]
            cosine[s, t * 128 : t * 128 + 128] = jnp.cos(angle)
            sine[s, t * 128 : t * 128 + 128] = jnp.sin(angle) * sign
    forwards = []

    def forward(rel, s):
        slot = (("M",) + RELS).index(rel)
        view = kv_all.at[s, pl.ds(keys.index[rel] * 2, 2)]
        forwards.append(forward_copy(view, s4.at[slot, s], r4.at[slot, s]))

    def project(s):
        y = dot(full[s].reshape(256, 1024), w[...])
        raw[s] = y
        a, b = y[:, :128], y[:, 128:]
        cos, sin = cosine[s], sine[s]
        lo, _ = head_sums(b * b, low)
        g = b * lax.rsqrt(lo * (1 / 64) + EPSILON) * gain_k
        turned = g * cos + swap_halves(g, first_half) * sin
        packed = jnp.where(low, turned, b).astype(BF16)
        kv_all[s, pl.ds(ctx * 2, 2)] = packed.reshape(2, 128, 128)
        keys.start(s)
        forward("M", s)
        lo, hi = head_sums(a * a, low)
        scale = jnp.where(
            low, lax.rsqrt(lo * (1 / 64) + EPSILON), lax.rsqrt(hi * (1 / 64) + EPSILON)
        )
        g = a * scale * gain_q
        turned = g * cos + swap_halves(g, first_half) * sin
        zero = jnp.zeros_like(turned)
        head0 = jnp.where(low, turned, zero).astype(BF16)
        head1 = jnp.where(low, pltpu.roll(turned, 64, 1), zero).astype(BF16)
        for t in range(2):
            queries[s, t, 0:128] = head0[t * 128 : t * 128 + 128]
            queries[s, t, 128:256] = head1[t * 128 : t * 128 + 128]

    def at(k, *steps):
        if 0 <= k < 4:
            for step in steps:
                step(k)

    def finish_keys(s):
        for rel in RELS:
            for route in range(2):
                keys.arrive(rel, s, route)
            forward(rel, s)

    for step in range(4 + 6):
        at(step, first.relay_row, first.relay_opposite)
        at(step - 1, first.relay_last)
        at(step - 2, first.finish, project)
        at(step - 3, keys.relay_row, keys.relay_opposite)
        at(step - 4, keys.relay_last)
        at(step - 5, finish_keys)
    first.drain()
    keys.drain()
    for copy in forwards:
        copy.wait_send()
    for s in range(4):
        for slot, rel in enumerate(("M",) + RELS):
            view = kv_all.at[s, pl.ds((keys.index[rel] + sibling() - ctx) * 2, 2)]
            rcopy(view, view, s4.at[slot, s], r4.at[slot, s], "ctx", sibling()).wait_recv()


def attention_kernel(block_map, queries, kv_all, low_out, high_out, logs, where, acc):
    me = lax.axis_index("ctx")
    for slot in range(32):
        where[block_map[slot]] = slot
    lane_k = lane_iota((256, 128)) < 64
    for j in range(2):
        mine = block_map[2 * me + j]
        acc[...] = jnp.zeros_like(acc)

        def step(i, masked):
            slot0, slot1 = where[2 * i], where[2 * i + 1]
            if masked:
                row = lax.rem(lax.broadcasted_iota(jnp.int32, (256, 256), 0), 128)
                col = lax.broadcasted_iota(jnp.int32, (256, 256), 1)
                keep = col + 256 * i <= row + 128 * mine
            kvs = [
                jnp.concatenate([kv_all[s, slot0], kv_all[s, slot1]], axis=0) for s in range(4)
            ]
            scores = [dot_nt(queries[s, j], kvs[s]) for s in range(4)]
            for s in range(4):
                weights = jnp.exp2(scores[s] * EXPONENT_SCALE)
                if masked:
                    weights = jnp.where(keep, weights, 0.0)
                ones = jnp.where(lane_k, jnp.ones_like(kvs[s]), kvs[s])
                acc[s] += dot(weights.astype(BF16), ones)

        last = mine // 2
        lax.fori_loop(0, last, lambda i, c: (step(i, False), c)[1], 0)
        step(last, True)
        low = lane_iota((128, 128)) < 64
        for s in range(4):
            a = acc[s]
            o = a * pltpu.roll(1.0 / a, 64, 1)
            both = jnp.where(low, pltpu.roll(o[0:128], 64, 1), o[128:256])
            low_out[s, j] = both.astype(BF16)
            high_out[s, j] = both
            logs[s, j] = jnp.log2(a.T[0:8])


def attention_back_kernel(
    block_map, queries, kv_all, grad_out, out, logs,
    grad_q, grad_kv, where, acc, grad_pad, turned, delta,
):
    me = lax.axis_index("ctx")
    for slot in range(32):
        where[block_map[slot]] = slot
    acc[...] = jnp.zeros_like(acc)
    low = lane_iota((128, 128)) < 64
    for j in range(2):
        mine = block_map[2 * me + j]
        turned[...] = jnp.zeros_like(turned)
        for s in range(4):
            g = grad_out[s, j]
            gf = g.astype(F32)
            zero = jnp.zeros_like(gf)
            grad_pad[s, 0:128] = jnp.where(low, zero, pltpu.roll(gf, 64, 1)).astype(BF16)
            grad_pad[s, 128:256] = jnp.where(low, zero, gf).astype(BF16)
            product = (gf * out[s, j]).T
            delta[s, :, 0:128] = jnp.broadcast_to(
                jnp.sum(product[0:64], axis=0, keepdims=True), (8, 128)
            )
            delta[s, :, 128:256] = jnp.broadcast_to(
                jnp.sum(product[64:128], axis=0, keepdims=True), (8, 128)
            )

        def step(i, masked):
            slot0, slot1 = where[2 * i], where[2 * i + 1]
            if masked:
                col = lax.rem(lax.broadcasted_iota(jnp.int32, (256, 256), 1), 128)
                row = lax.broadcasted_iota(jnp.int32, (256, 256), 0)
                keep = row + 256 * i <= col + 128 * mine
            kvs = [
                jnp.concatenate([kv_all[s, slot0], kv_all[s, slot1]], axis=0) for s in range(4)
            ]
            scores = [dot_nt(kvs[s], queries[s, j]) for s in range(4)]
            grads = [dot_nt(kvs[s], grad_pad[s]) for s in range(4)]
            both = []
            for s in range(4):
                probs = jnp.exp2(
                    scores[s] * EXPONENT_SCALE - logs[s, j, 0:1]
                )
                if masked:
                    probs = jnp.where(keep, probs, 0.0)
                wide = (probs * (grads[s] - delta[s, 0:1])).astype(BF16)
                both.append((wide, probs.astype(BF16)))
            for s in range(4):
                turned[s] += dot_tn(kvs[s], both[s][0])
                block = dot(
                    jnp.concatenate(both[s], axis=1),
                    jnp.concatenate([queries[s, j], grad_pad[s]], axis=0),
                )
                acc[s, slot0] += block[0:128]
                acc[s, slot1] += block[128:256]

        last = mine // 2
        lax.fori_loop(0, last, lambda i, c: (step(i, False), c)[1], 0)
        step(last, True)
        for s in range(4):
            t = turned[s].T * 0.125
            grad_q[s, j] = jnp.where(low, t[0:128], pltpu.roll(t[128:256], 64, 1))
    scale = jnp.where(low, 0.125, 1.0)

    def finish(n, c):
        for s in range(4):
            grad_kv[s, n] = (acc[s, n] * scale).astype(BF16)
        return c

    lax.fori_loop(0, 32, finish, 0)


class Reduce:
    @staticmethod
    def scratch(A, R):
        return (
            pltpu.VMEM((A, R, 512), BF16),
            pltpu.VMEM((A, R, 512), BF16),
            pltpu.SemaphoreType.DMA((2,)),
            pltpu.SemaphoreType.DMA((2,)),
        ) + Scatter.scratch(1, (A, R // 4, 128))

    def __init__(self, source, got, pair, ssem, rsem, *rest):
        self.source, self.got, self.pair = source, got, pair
        self.ssem, self.rsem = ssem, rsem
        self.rows = source.shape[1] // 4
        self.sum = Scatter("ctx", 1, self.piece, *rest)

    def piece(self, i, k, route):
        row = pl.multiple_of(lax.rem(i // 2, 4) * self.rows, 16)
        column = pl.multiple_of((i // 8) * 256 + route * 128, 128)
        return self.pair.at[:, pl.ds(row, self.rows), pl.ds(column, 128)]

    def columns(self, y, core):
        return pl.ds(pl.multiple_of((2 * y + core) * 256, 256), 256)

    def exchange(self):
        core = lax.rem(lax.axis_index("ctx"), 2)
        self.copies = []
        for y in range(2):
            copy = rcopy(
                self.source.at[:, :, self.columns(y, 1 - core)],
                self.got.at[:, :, y * 256 : y * 256 + 256],
                self.ssem.at[y],
                self.rsem.at[y],
                "ctx",
                sibling(),
            )
            copy.start()
            self.copies.append(copy)

    def start(self):
        core = lax.rem(lax.axis_index("ctx"), 2)
        for y in range(2):
            self.copies[y].wait_recv()
            columns = slice(y * 256, y * 256 + 256)
            mine = self.source[:, :, self.columns(y, core)].astype(F32)
            self.pair[:, :, columns] = (mine + self.got[:, :, columns].astype(F32)).astype(BF16)
        self.sum.start(1, 0)
        self.sum.start(0, 0)

    def result(self, store):
        for route in range(2):
            store(route, self.sum.result(0, route).astype(BF16))

    def drain(self):
        for copy in self.copies:
            copy.wait_send()
        self.sum.drain()


class Spread:
    @staticmethod
    def scratch():
        return Gather.scratch(1) + (pltpu.SemaphoreType.DMA((8,)), pltpu.SemaphoreType.DMA((8,)))

    def __init__(self, target, ssem, rsem, fs, fr):
        self.target, self.fs, self.fr = target, fs, fr
        self.rows = target.shape[1] // 4
        self.gather = Gather("ctx", self.piece, ssem, rsem)
        self.forwards = []

    def view(self, i, shift, width):
        row = pl.multiple_of(lax.rem(i // 2, 4) * self.rows, 16)
        column = pl.multiple_of((2 * (i // 8) + lax.rem(i, 2)) * 256 + shift, 128)
        return self.target.at[:, pl.ds(row, self.rows), pl.ds(column, width)]

    def piece(self, i, k, route):
        return self.view(i, route * 128, 128)

    def own(self):
        return self.view(lax.axis_index("ctx"), 0, 256)

    def forward(self, rel):
        slot = len(self.forwards)
        view = self.view(self.gather.index[rel], 0, 256)
        self.forwards.append(forward_copy(view, self.fs.at[slot], self.fr.at[slot]))

    def start(self):
        self.gather.start(0)
        self.forward("M")

    def finish(self):
        for rel in RELS:
            for route in range(2):
                self.gather.arrive(rel, 0, route)
            self.forward(rel)

    def drain(self):
        self.gather.drain()
        ctx = lax.axis_index("ctx")
        for slot, rel in enumerate(("M",) + RELS):
            self.forwards[slot].wait_send()
            view = self.view(self.gather.index[rel] + sibling() - ctx, 0, 256)
            rcopy(view, view, self.fs.at[slot], self.fr.at[slot], "ctx", sibling()).wait_recv()


def middle_kernel(
    x, attended, w, gain2, cot, cot_full, gate_up, down,
    mixed, d_mixed, part_o, d_att, gain_part, out_part, ffn_own,
    part, full, part_d, branch, turned, grads, *scratch,
):
    mp = lax.axis_index("mp")
    enter(("mp", "ctx"), sib=True)
    sums1, rest = take(scratch, 6)
    sums2, rest = take(rest, 6)
    (s1, r1, s2, r2), sums3 = take(rest, 4)
    rs1 = Scatter("mp", 4, mp_rows(part), *sums1, alt=(3,))
    rs2 = Scatter("mp", 4, mp_rows(part_d), *sums2, alt=(3,))
    ag2 = Gather("mp", mp_rows(full), s1, r1, alt=(0, 2))
    ag3 = Gather("mp", mp_rows(branch), s2, r2, alt=(0,))
    reduce = Reduce(grads, *sums3)

    def mix(k):
        for t in range(2):
            m = x[k, t].astype(F32) + rs1.result(k, t)
            mixed[k, t] = m
            full[k, t, rows_of(mp), :] = (m * rms_scale(m) * gain2[...]).astype(BF16)
        ag2.start(k)

    def feed(k):
        rows = full[k].reshape(256, 1024)
        columns = slice(k * 256, k * 256 + 256)
        gate = dot_nt(rows, gate_up[0])
        up = dot_nt(rows, gate_up[1])
        sig = 1.0 / (1.0 + jnp.exp(-gate))
        d_active = dot_nt(cot_full[k].reshape(256, 1024), down[...])
        d_gate = (d_active * up * sig * (1.0 + gate * (1.0 - sig))).astype(BF16)
        d_up = (d_active * gate * sig).astype(BF16)
        both = dot(d_gate, gate_up[0]) + dot(d_up, gate_up[1])
        part_d[k] = both.astype(BF16).reshape(2, 128, 1024)
        rs2.start(1, k)
        rs2.start(0, k)
        active = (gate * sig * up).astype(BF16)
        part_o[k] = dot(active, down[...]).astype(BF16).reshape(2, 128, 1024)
        turned[0, :, columns] = d_gate.T
        turned[1, :, columns] = d_up.T
        turned[2, :, columns] = active.T

    def weigh():
        def tile(n, c):
            columns = pl.ds(pl.multiple_of(n * 256, 256), 256)
            rows = full[:, :, :, columns].reshape(1024, 256)
            for i in range(2):
                grads[i, :, columns] = dot(turned[i], rows).astype(BF16)
            rows = cot_full[:, :, :, columns].reshape(1024, 256)
            grads[2, :, columns] = dot(turned[2], rows).astype(BF16)
            return c

        lax.fori_loop(0, 4, tile, 0)

    gain_part[...] = jnp.zeros_like(gain_part)

    def back(k):
        for t in range(2):
            g = rs2.result(k, t)
            m = mixed[k, t]
            scale = rms_scale(m)
            normed = m * scale
            gain_part[...] += jnp.sum(g * normed, axis=0, keepdims=True)
            dm = cot[k, t].astype(F32) + norm_back(g, normed, scale, gain2[...])
            d_mixed[k, t] = dm
            branch[k, t, rows_of(mp), :] = dm.astype(BF16)
        ag3.start(k)

    def attend(k):
        rows = branch[k].reshape(256, 1024)
        d_att[k] = dot_nt(rows, w[...]).astype(BF16).reshape(2, 128, 128)

    def at(k, *steps):
        if 0 <= k < 4:
            for step in steps:
                step(k)

    for k in range(4):
        part[k] = dot(attended[k].reshape(256, 128), w[...]).astype(BF16).reshape(2, 128, 1024)
        rs1.start(1, k)
        rs1.start(0, k)
    for step in range(4 + 11):
        at(step, lambda k: rs1.middle(1, k))
        at(step - 1, rs1.cross, lambda k: rs1.middle(0, k))
        at(step - 2, mix)
        at(step - 3, ag2.relay_row, ag2.relay_opposite)
        at(step - 4, ag2.relay_last)
        at(step - 5, ag2.finish, feed)
        at(step - 6, lambda k: rs2.middle(1, k))
        at(step - 7, rs2.cross, lambda k: rs2.middle(0, k))
        if step == 8:
            weigh()
            reduce.exchange()
        if step == 9:
            reduce.start()
        at(step - 8, back)
        if step == 10:
            reduce.sum.middle(1, 0)
        if step == 11:
            reduce.sum.cross(0)
            reduce.sum.middle(0, 0)
        at(step - 9, ag3.relay_row, ag3.relay_opposite)
        at(step - 10, ag3.relay_last)
        at(step - 11, ag3.finish, attend)
    rows = attended[...].reshape(1024, 128).T
    for n in range(4):
        columns = slice(n * 256, n * 256 + 256)
        out_part[:, columns] = dot(rows, branch[:, :, :, columns].reshape(1024, 256)).astype(BF16)

    def store(route, value):
        ffn_own[:, :, route * 128 : route * 128 + 128] = value

    reduce.result(store)
    for item in (rs1, ag2, rs2, ag3, reduce):
        item.drain()


def last_kernel(
    grad_kv, grad_q, raw, cosine, sine, query_gain, key_gain, w, x, gain1, d_mixed,
    mixed, part_o, full, out_part, gain2_part,
    out, in_grad, attn_sum, total,
    pair, got, d_qkv, part, grads, gain_row, small, by_mp, by_ctx, *scratch,
):
    ctx = lax.axis_index("ctx")
    mp = lax.axis_index("mp")
    barrier = pltpu.get_barrier_semaphore()
    for axis, size in (("mp", 8), ("ctx", 16)):
        me = lax.axis_index(axis)
        for n in range(1, size):
            pl.semaphore_signal(
                barrier, inc=1, device_id={axis: lax.rem(me + n, size)}, device_id_type=MESH
            )
    pl.semaphore_wait(barrier, 22)
    sums_k, rest = take(scratch, 6)
    sums_o, rest = take(rest, 6)
    sums_n, rest = take(rest, 6)
    sums_a, rest = take(rest, 10)
    spread_a, rest = take(rest, 4)
    s1, r1, s2, r2, s3, r3 = rest
    core = lax.rem(ctx, 2)
    sib = sibling()
    copies = []
    for s in range(4):
        for chip in range(8):
            src = grad_kv.at[s, pl.ds(chip * 4 + (1 - core) * 2, 2)]
            copy = rcopy(
                src, got.at[s, pl.ds(chip * 2, 2)], s1.at[s, chip], r1.at[s, chip], "ctx", sib
            )
            copy.start()
            copies.append(copy)
    rs_k = Scatter("ctx", 4, lambda i, k, route: pair.at[k, (i // 2) * 2 + route], *sums_k)
    rs_o = Scatter("mp", 4, mp_rows(part_o), *sums_o)
    rs_n = Scatter("mp", 4, mp_rows(part), *sums_n, alt=(3,))
    reduce = Reduce(grads, *sums_a)
    attn = Spread(attn_sum, *spread_a)
    for s in range(4):
        rs_o.start(1, s)
        rs_o.start(0, s)
        for chip in range(8):
            copies[s * 8 + chip].wait_recv()
            mine = grad_kv[s, pl.ds(chip * 4 + core * 2, 2)].astype(F32)
            both = mine + got[s, chip * 2 : chip * 2 + 2].astype(F32)
            pair[s, chip * 2 : chip * 2 + 2] = both.astype(BF16)
        rs_k.start(1, s)
        rs_k.start(0, s)
    grads[0, 256:384, :] = out_part[...]
    lane = lane_iota((256, 128))
    low = lane < 64
    first_half = lax.rem(lane, 64) < 32
    inv = 1 / 64
    small[...] = jnp.zeros_like(small)
    gain_row[...] = jnp.zeros_like(gain_row)
    for n in range(8):
        small[8 + n : 9 + n, :] = gain2_part[:, n * 128 : n * 128 + 128]
    gain_q, gain_k = head_gains(query_gain, key_gain)

    def project_queries(s):
        a = raw[s, :, 0:128]
        cos, sin = cosine[s], sine[s]
        lo, hi = head_sums(a * a, low)
        scale = jnp.where(low, lax.rsqrt(lo * inv + EPSILON), lax.rsqrt(hi * inv + EPSILON))
        n = a * scale
        d = grad_q[s].reshape(256, 128)
        g = d * cos - swap_halves(d, first_half) * sin
        small[16:17, :] += jnp.sum(g * n, axis=0, keepdims=True)
        e = g * gain_q
        lo, hi = head_sums(e * n, low)
        dq = scale * (e - n * jnp.where(low, lo * inv, hi * inv))
        d_qkv[s, :, 0:128] = dq.astype(BF16)

    def project(s):
        b = raw[s, :, 128:256]
        cos, sin = cosine[s], sine[s]
        lo, _ = head_sums(b * b, low)
        scale = lax.rsqrt(lo * inv + EPSILON)
        n = b * scale
        d = jnp.concatenate([rs_k.result(s, 0), rs_k.result(s, 1)], axis=0)
        g = d * cos - swap_halves(d, first_half) * sin
        small[17:18, :] += jnp.sum(g * n, axis=0, keepdims=True)
        e = g * gain_k
        lo, _ = head_sums(e * n, low)
        dk = scale * (e - n * (lo * inv))
        d_qkv[s, :, 128:256] = jnp.where(low, dk, d).astype(BF16)
        part[s] = dot_nt(d_qkv[s], w[...]).astype(BF16).reshape(2, 128, 1024)
        rs_n.start(1, s)
        rs_n.start(0, s)

    def write_out(s):
        for t in range(2):
            out[s, t] = (mixed[s, t] + rs_o.result(s, t)).astype(BF16)

    def weigh():
        rows = d_qkv[...].reshape(1024, 256).T
        for n in range(4):
            columns = slice(n * 256, n * 256 + 256)
            value = dot(rows, full[:, :, :, columns].reshape(1024, 256))
            grads[0, 0:256, columns] = value.astype(BF16)

    def write_grad(s):
        for t in range(2):
            g = rs_n.result(s, t)
            v = x[s, t].astype(F32)
            scale = rms_scale(v)
            normed = v * scale
            gain_row[...] += jnp.sum(g * normed, axis=0, keepdims=True)
            in_grad[s, t] = (d_mixed[s, t] + norm_back(g, normed, scale, gain1[...])).astype(BF16)

    def at(k, *steps):
        if 0 <= k < 4:
            for step in steps:
                step(k)

    def store(route, value):
        attn.piece(ctx, 0, route)[...] = value

    for step in range(4 + 3):
        at(step, lambda k: rs_k.middle(1, k), lambda k: rs_o.middle(1, k))
        at(step, project_queries)
        at(step - 1, rs_k.cross, lambda k: rs_k.middle(0, k))
        at(step - 1, rs_o.cross, lambda k: rs_o.middle(0, k))
        at(step - 2, project)
        if step == 5:
            weigh()
            reduce.exchange()
        at(step - 3, lambda k: rs_n.middle(1, k))
    reduce.start()
    for k in range(4):
        rs_n.cross(k)
        rs_n.middle(0, k)
    for k in range(4):
        write_out(k)
    reduce.sum.middle(1, 0)
    reduce.sum.cross(0)
    reduce.sum.middle(0, 0)
    write_grad(0)
    write_grad(1)
    reduce.result(store)
    attn.start()
    write_grad(2)
    write_grad(3)
    for n in range(8):
        small[n : n + 1, :] = gain_row[:, n * 128 : n * 128 + 128]
    copies2 = []
    for n in range(1, 8):
        copy = rcopy(small, by_mp.at[n], s2.at[n], r2.at[n], "mp", lax.rem(mp + n, 8))
        copy.start()
        copies2.append(copy)
    attn.gather.relay_row(0)
    attn.gather.relay_opposite(0)
    by_mp[0] = small[...]
    for copy in copies2:
        copy.wait()
    by_ctx[0] = jnp.sum(by_mp[...], axis=0)
    copies3 = []
    for n in range(1, 16):
        copy = rcopy(
            by_ctx.at[0], by_ctx.at[n], s3.at[n], r3.at[n], "ctx", lax.rem(ctx + n, 16)
        )
        copy.start()
        copies3.append(copy)
    attn.gather.relay_last(0)
    attn.finish()
    for copy in copies3:
        copy.wait()
    total[...] = jnp.zeros_like(total)

    def add(i, c):
        total[...] += by_ctx[lax.rem(ctx - i + 16, 16)]
        return c

    lax.fori_loop(0, 16, add, 0)
    for copy in copies:
        copy.wait_send()
    for item in (rs_k, rs_o, rs_n, reduce, attn):
        item.drain()


def widen_kernel(ffn_all, attn_sum, gate_up_grad, down_grad, qkv_grad, out_grad):
    step = pl.program_id(0)

    def widen(target):
        for y in range(2):
            for core in range(2):
                start = (2 * y + core) * 256
                target[:, start : start + 256] = ffn_all[y, 0, core, 0].astype(F32)

    @pl.when(step == 0)
    def _():
        qkv_grad[...] = attn_sum[0, 0:256].astype(F32).T.reshape(1024, 1, 256)
        out_grad[...] = attn_sum[0, 256:384].astype(F32)

    @pl.when(step < 8)
    def _():
        widen(gate_up_grad.at[0])

    @pl.when(step >= 8)
    def _():
        widen(down_grad)


def vm(n):
    return [pl.BlockSpec(memory_space=pltpu.VMEM)] * n


def sds(shape, dtype):
    return jax.ShapeDtypeStruct(shape, dtype)


def local(
    residual_in,
    attn_norm,
    query_key_value_weight,
    query_gain,
    key_gain,
    out_weight,
    ffn_norm,
    gate_up,
    down_weight,
    cotangent,
    positions,
    block_map,
):
    rows_shape = (4, 2, 16, 1024)
    full_shape = (4, 2, 128, 1024)
    piece = (16, 1024)
    dma = pltpu.SemaphoreType.DMA

    inverse_freq = 1.0 / ROPE_BASE ** (np.arange(0, 64, 2) / 64)
    frequency = np.tile(inverse_freq, 4).reshape(1, 128).astype(np.float32)
    gain_q, gain_k = query_gain.reshape(1, 64), key_gain.reshape(1, 64)
    smem = [pl.BlockSpec(memory_space=pltpu.SMEM)]
    cot_full = lax.all_gather(cotangent, "mp", axis=2, tiled=True)
    gain1 = attn_norm.reshape(1, 1024)
    gain2 = ffn_norm.reshape(1, 1024)
    w_qkv = query_key_value_weight.reshape(1024, 256)

    full1, cosine, sine, raw, queries, kv_all = pl.pallas_call(
        qkv_kernel,
        out_shape=(
            sds(full_shape, BF16),
            sds((4, 256, 128), F32),
            sds((4, 256, 128), F32),
            sds((4, 256, 256), F32),
            sds((4, 2, 256, 128), BF16),
            sds((4, 32, 128, 128), BF16),
        ),
        in_specs=smem + vm(7),
        out_specs=tuple(vm(6)),
        scratch_shapes=Gather.scratch(4) * 2 + (dma((8, 4)), dma((8, 4))),
        compiler_params=params(1),
    )(block_map, residual_in, gain1, w_qkv, gain_q, gain_k, positions.reshape(4, 32, 128), frequency)

    attended, attended_high, logs = pl.pallas_call(
        attention_kernel,
        out_shape=(
            sds((4, 2, 128, 128), BF16),
            sds((4, 2, 128, 128), F32),
            sds((4, 2, 8, 256), F32),
        ),
        in_specs=smem + vm(2),
        out_specs=tuple(vm(3)),
        scratch_shapes=[pltpu.SMEM((32,), jnp.int32), pltpu.VMEM((4, 256, 128), F32)],
        compiler_params=pltpu.CompilerParams(vmem_limit_bytes=VMEM_LIMIT),
    )(block_map, queries, kv_all)

    gate_up_t = jnp.transpose(gate_up, (1, 2, 0))
    mixed, d_mixed, part_o, d_att, gain2_part, out_part, ffn_own = pl.pallas_call(
        middle_kernel,
        out_shape=(
            sds(rows_shape, F32),
            sds(rows_shape, F32),
            sds(full_shape, BF16),
            sds((4, 2, 128, 128), BF16),
            sds((1, 1024), F32),
            sds((128, 1024), BF16),
            sds((3, 144, 256), BF16),
        ),
        in_specs=vm(8),
        out_specs=tuple(vm(7)),
        scratch_shapes=(pltpu.VMEM(full_shape, BF16),) * 4
        + (pltpu.VMEM((3, 576, 1024), BF16),) * 2
        + Scatter.scratch(4, piece) * 2
        + Gather.scratch(4) * 2
        + Reduce.scratch(3, 576),
        compiler_params=params(2),
    )(
        residual_in, attended, out_weight, gain2, cotangent, cot_full, gate_up_t, down_weight
    )

    ffn_all = lax.all_gather(ffn_own, "ctx", axis=0).reshape(2, 4, 2, 3, 144, 256)

    grad_q, grad_kv = pl.pallas_call(
        attention_back_kernel,
        out_shape=(sds((4, 2, 128, 128), F32), sds((4, 32, 128, 128), BF16)),
        in_specs=smem + vm(5),
        out_specs=tuple(vm(2)),
        scratch_shapes=[
            pltpu.SMEM((32,), jnp.int32),
            pltpu.VMEM((4, 32, 128, 128), F32),
            pltpu.VMEM((4, 256, 128), BF16),
            pltpu.VMEM((4, 128, 256), F32),
            pltpu.VMEM((4, 8, 256), F32),
        ],
        compiler_params=pltpu.CompilerParams(vmem_limit_bytes=VMEM_LIMIT),
    )(block_map, queries, kv_all, d_att, attended_high, logs)

    output, input_grad, attn_sum, sums = pl.pallas_call(
        last_kernel,
        out_shape=(
            sds(rows_shape, BF16),
            sds(rows_shape, BF16),
            sds((1, 384, 1024), BF16),
            sds((24, 128), F32),
        ),
        in_specs=vm(16),
        out_specs=tuple(vm(4)),
        scratch_shapes=(
            pltpu.VMEM((4, 16, 128, 128), BF16),
            pltpu.VMEM((4, 16, 128, 128), BF16),
            pltpu.VMEM((4, 256, 256), BF16),
            pltpu.VMEM(full_shape, BF16),
            pltpu.VMEM((1, 384, 1024), BF16),
            pltpu.VMEM((1, 1024), F32),
            pltpu.VMEM((24, 128), F32),
            pltpu.VMEM((8, 24, 128), F32),
            pltpu.VMEM((16, 24, 128), F32),
        )
        + Scatter.scratch(4, (128, 128))
        + Scatter.scratch(4, piece) * 2
        + Reduce.scratch(1, 384)
        + Spread.scratch()
        + (dma((4, 8)), dma((4, 8)), dma((8,)), dma((8,)), dma((16,)), dma((16,))),
        compiler_params=params(3),
    )(
        grad_kv, grad_q, raw, cosine, sine, gain_q, gain_k, w_qkv, residual_in, gain1,
        d_mixed, mixed, part_o, full1, out_part, gain2_part,
    )

    gate_up_grad, down_grad, qkv_grad, out_grad = pl.pallas_call(
        widen_kernel,
        grid=(12,),
        out_shape=(
            sds((2, 576, 1024), F32),
            sds((576, 1024), F32),
            sds((1024, 1, 256), F32),
            sds((128, 1024), F32),
        ),
        in_specs=[
            pl.BlockSpec((2, 1, 2, 1, 144, 256), lambda i: (0, i % 4, 0, i // 4, 0, 0)),
            pl.BlockSpec((1, 384, 1024), lambda i: (0, 0, 0)),
        ],
        out_specs=(
            pl.BlockSpec((1, 144, 1024), lambda i: (jnp.minimum(i, 7) // 4, jnp.minimum(i, 7) % 4, 0)),
            pl.BlockSpec((144, 1024), lambda i: (jnp.maximum(i - 8, 0), 0)),
            pl.BlockSpec((1024, 1, 256), lambda i: (0, 0, 0)),
            pl.BlockSpec((128, 1024), lambda i: (0, 0)),
        ),
        compiler_params=pltpu.CompilerParams(vmem_limit_bytes=VMEM_LIMIT),
    )(ffn_all, attn_sum)

    return (
        output,
        input_grad,
        sums[0:8].reshape(1024),
        qkv_grad,
        sums[16, :64] + sums[16, 64:128],
        sums[17, :64],
        out_grad,
        sums[8:16].reshape(1024),
        jnp.transpose(gate_up_grad, (2, 0, 1)),
        down_grad,
    )


def solution(mesh):
    return jax.shard_map(
        local,
        mesh=mesh,
        in_specs=(
            P(None, "ctx", "mp", None),
            P(),
            P(None, "mp", None),
            P(),
            P(),
            P("mp", None),
            P(),
            P(None, None, "mp"),
            P("mp", None),
            P(None, "ctx", "mp", None),
            P(),
            P(),
        ),
        out_specs=(
            P(None, "ctx", "mp", None),
            P(None, "ctx", "mp", None),
            P(),
            P(None, "mp", None),
            P(),
            P(),
            P("mp", None),
            P(),
            P(None, None, "mp"),
            P("mp", None),
        ),
        check_vma=False,
    )
```
